256 devices in a mesh: dp: 32 (over y_hi, z, core), ctx: 8 (over y_lo, x).
Axes of the slice: x: 4, y: 4 (y_hi: 2, y_lo: 2; y = y_hi * 2 + y_lo), z: 8, core: 2. Of those that a mesh axis runs over, the one named last changes fastest.
Arguments:
- inputs: bfloat16 [64, 512, 1024], P('dp', 'ctx'), may hold values from -8 to 8
- frames: int32 [64], P('dp'), may hold values from 64 to 512, as said below
- gain_first: float32 [1024], replicated, may hold values from 0.25 to 1.75
- w_first: bfloat16 [1024, 2048], P('dp'), may hold values from -0.1875 to 0.1875
- depth_kernel: float32 [31, 1024], replicated, may hold values from -1 to 1
- gain_second: float32 [1024], replicated, may hold values from 0.25 to 1.75
- w_second: bfloat16 [1024, 1024], P('dp'), may hold values from -0.1875 to 0.1875
- gain_attn: float32 [1024], replicated, may hold values from 0.25 to 1.75
- w_qkv: bfloat16 [1024, 3072], P('dp'), may hold values from -2.25 to 2.25
- w_proj: bfloat16 [1024, 1024], P('dp'), may hold values from -2.5 to 2.5
- grad_out: bfloat16 [64, 512, 1024], P('dp', 'ctx'), may hold values from -6 to 6
Outputs:
- result: bfloat16 [64, 512, 1024], P('dp', 'ctx')
- grad_in: bfloat16 [64, 512, 1024], P('dp', 'ctx')
- grad_first: float32 [1024, 2048], P('dp')
- grad_kernel: float32 [31, 1024], replicated
The draws below stay inside these ranges and needn't reach their ends.
Inputs may be any that keep to these rules, and one draw needn't show every extreme that they name: Recording b has frames[b] real frames at the start and padding after them; some recording is full.
All inputs are finite; a program needn't handle non-finite values.
Results may differ from the reference program's by a relative error of at most 0.025.
Values may be sent and summed in bfloat16 or wider, within the bound.
No kernel may reach another device: no remote copies, remote signals or barrier semaphores. Data moves between devices by JAX's collectives and lax.ppermute only.
A program may use at most 128 MiB of HBM per device.

```python
import jax
import jax.numpy as jnp
from jax import lax

D = 1024
HEADS = 16
KERNEL = 31
BATCH = 64
LENGTH = 512


def draw_frames(key, part):
    key = jax.random.fold_in(key, 11)
    first_key, second_key = jax.random.split(key)
    drawn = jax.random.randint(first_key, (BATCH,), LENGTH // 8, LENGTH + 1)
    chosen = jax.random.randint(second_key, (), 0, BATCH)
    return jnp.where(jnp.arange(BATCH) == chosen, LENGTH, drawn).astype(jnp.int32)


def draw_w_qkv(key, part):
    key = jax.random.fold_in(key, 23)
    first_key = jax.random.fold_in(key, 0)
    return (jax.random.normal(first_key, (D, 3 * D), jnp.float32) * D ** (-0.5)).astype(jnp.bfloat16)


def raised(values, key, source, target, blocks, factor):
    def block_of(position):
        return (jnp.arange(values.shape[position]) // (values.shape[position] // blocks)).reshape((-1,) + (1,) * (values.ndim - 1 - position))

    first = jax.random.permutation(key, blocks)[block_of(target)]
    second = (block_of(target) + blocks // 2) % blocks
    return jnp.where((block_of(source) == first) | (block_of(source) == second), factor * values, values)


def levels(own_key, extent, pieces, smallest, high):
    def one(dim, blocks):
        heights = jax.random.uniform(jax.random.fold_in(jax.random.fold_in(own_key, 6), dim), (blocks,), jnp.float32, smallest / len(pieces), high / len(pieces))
        return jnp.repeat(jnp.exp(heights), extent[dim] // blocks).reshape((-1,) + (1,) * (len(extent) - dim - 1))

    gain = one(*pieces[0])
    for cut in pieces[1:]:
        gain = gain * one(*cut)
    return gain


def centred(key, shape, scale, bound, cuts=(), kind=jnp.bfloat16):
    factor_of = levels(key, shape, cuts, -0.22, 0.18) if cuts else 1.0
    values = jax.random.normal(key, shape, jnp.float32) * scale * factor_of
    return jnp.minimum(jnp.maximum(values, -bound), bound).astype(kind)


def heavy_noise(rng, extent, scale, most, cuts, heavy, kind=jnp.bfloat16):
    entries = scale * jax.random.normal(rng, extent, jnp.float32)
    if cuts:
        entries = entries * levels(rng, extent, cuts, -0.22, 0.18)
    return jnp.clip(raised(entries, jax.random.fold_in(rng, 3), *heavy), -most, most).astype(kind)


def setup_inputs(seed: int = 0) -> dict:
    arg_keys = jax.random.split(jax.random.key(seed), 12)
    inputs = heavy_noise(arg_keys[0], (BATCH, LENGTH, D), 1.0, 8.0, ((0, 32), (1, 8)), (0, 2, 32, 2.75))
    frames = draw_frames(jax.random.fold_in(arg_keys[11], 71), 0)
    gain_first = jnp.clip(1.0 + 0.15 * jax.random.normal(arg_keys[2], (D,), jnp.float32), 0.25, 1.75)
    w_first = centred(arg_keys[3], (D, 2 * D), D ** -0.5, 0.1875, ((0, 32),))
    depth_kernel = centred(arg_keys[4], (KERNEL, D), KERNEL ** -0.5, 1.0, (), jnp.float32)
    gain_second = jnp.clip(1.0 + 0.15 * jax.random.normal(arg_keys[5], (D,), jnp.float32), 0.25, 1.75)
    w_second = centred(arg_keys[6], (D, D), D ** -0.5, 0.1875, ((0, 32),))
    gain_attn = jnp.clip(1.0 + 0.15 * jax.random.normal(arg_keys[7], (D,), jnp.float32), 0.25, 1.75)
    w_qkv = draw_w_qkv(jax.random.fold_in(arg_keys[11], 71), 0)
    w_proj = centred(arg_keys[9], (D, D), (5.0 * D ** -0.5), 2.5, ((0, 32),))
    grad_out = centred(arg_keys[10], (BATCH, LENGTH, D), 1.0, 6.0, ((0, 32), (1, 8)))
    return dict(inputs=inputs, frames=frames, gain_first=gain_first, w_first=w_first, depth_kernel=depth_kernel, gain_second=gain_second, w_second=w_second, gain_attn=gain_attn, w_qkv=w_qkv, w_proj=w_proj, grad_out=grad_out)


EPSILON = 1e-05

def normalize(values, gain_vec):
    centre = values - lax.optimization_barrier(jnp.mean(values, -1, keepdims=True))
    spread = lax.optimization_barrier(jnp.mean(centre * centre, -1, keepdims=True))
    return centre * lax.rsqrt(spread + EPSILON) * gain_vec

def swish_norm(values, gain_vec):
    normal_part = normalize(values, gain_vec)
    return normal_part * jax.nn.sigmoid(normal_part)

def rounded(values):
    return lax.optimization_barrier(values.astype(jnp.bfloat16))

def reference(inputs, frames, gain_first, w_first, depth_kernel, gain_second, w_second, gain_attn, w_qkv, w_proj, grad_out):
    record_count, frame_slots, model_dim = inputs.shape
    reach = (KERNEL - 1) // 2
    head_dim = model_dim // HEADS
    positions = jnp.arange(frame_slots, dtype=jnp.int32)
    present = (positions[None, :] < frames[:, None]).astype(jnp.float32)
    present_rows = present.reshape(-1, 1)
    flat_in = inputs.reshape(-1, model_dim).astype(jnp.float32)
    normed = normalize(flat_in, gain_first).astype(jnp.bfloat16)
    hidden = jnp.dot(normed, w_first, preferred_element_type=jnp.float32)
    linear = hidden[:, :model_dim]
    gating = hidden[:, model_dim:]
    gated = rounded(present_rows * linear * jax.nn.sigmoid(gating))
    gated_wide = jnp.pad(gated.astype(jnp.float32).reshape(record_count, frame_slots, model_dim), ((0, 0), (reach, reach), (0, 0)))
    convolved = jnp.zeros((record_count, frame_slots, model_dim), jnp.float32)
    for tap_index in range(KERNEL):
        convolved = convolved + depth_kernel[tap_index] * gated_wide[:, tap_index:tap_index + frame_slots]
    swished, pull_back = jax.vjp(lambda v: swish_norm(v, gain_second), convolved.reshape(-1, model_dim))
    residual = (flat_in + jnp.dot(swished.astype(jnp.bfloat16), w_second, preferred_element_type=jnp.float32)).astype(jnp.bfloat16)
    attn_in = normalize(residual.astype(jnp.float32), gain_attn).astype(jnp.bfloat16)
    packed = jnp.dot(attn_in, w_qkv, preferred_element_type=jnp.float32).astype(jnp.bfloat16)
    packed = packed.reshape(record_count, frame_slots, 3, HEADS, head_dim)
    scaling = head_dim ** (-0.5)

    def one_record(bundle):
        record, key_ok = bundle
        queries = record[:, 0].astype(jnp.float32)
        keyset = record[:, 1].astype(jnp.float32)
        values = record[:, 2].astype(jnp.float32)
        scores = jnp.einsum('qhe,khe->hqk', queries, keyset) * scaling
        scores = jnp.where(key_ok[None, None, :] > 0, scores, -1e+30)
        row_max = lax.optimization_barrier(jnp.max(scores, -1, keepdims=True))
        numerator = jnp.exp(scores - row_max) * key_ok[None, None, :]
        denominator = lax.optimization_barrier(jnp.sum(numerator, -1, keepdims=True))
        weights = rounded(numerator).astype(jnp.float32)
        summed = jnp.einsum('hqk,khe->hqe', weights, values) / denominator
        return jnp.transpose(summed, (1, 0, 2)).reshape(frame_slots, model_dim).astype(jnp.bfloat16)
    attended = lax.map(one_record, (packed, present))
    projected = jnp.dot(attended.reshape(-1, model_dim), w_proj, preferred_element_type=jnp.float32)
    result = (residual.astype(jnp.float32) + present_rows * projected).astype(jnp.bfloat16)
    result = result.reshape(record_count, frame_slots, model_dim)
    cotangent = grad_out.reshape(-1, model_dim)
    back_two = jnp.dot(cotangent, w_second.T, preferred_element_type=jnp.float32)
    grad_conv = rounded(pull_back(back_two)[0]).astype(jnp.float32).reshape(record_count, frame_slots, model_dim)
    conv_wide = jnp.pad(grad_conv, ((0, 0), (reach, reach), (0, 0)))
    grad_gated = jnp.zeros((record_count, frame_slots, model_dim), jnp.float32)
    for tap_index in range(KERNEL):
        lead_in = 2 * reach - tap_index
        grad_gated = grad_gated + depth_kernel[tap_index] * conv_wide[:, lead_in:lead_in + frame_slots]
    grad_gated = grad_gated.reshape(-1, model_dim) * present_rows
    opening = jax.nn.sigmoid(gating)
    grad_hidden = jnp.concatenate([grad_gated * opening, grad_gated * linear * opening * (1.0 - opening)], 1).astype(jnp.bfloat16)
    grad_first = jnp.dot(normed.T, grad_hidden, preferred_element_type=jnp.float32)
    grad_kernel = jnp.stack([lax.optimization_barrier(jnp.sum(gated_wide[:, tap_index:tap_index + frame_slots] * grad_conv, axis=(0, 1))) for tap_index in range(KERNEL)])
    back_one = jnp.dot(grad_hidden, w_first.T, preferred_element_type=jnp.float32)
    unused_out, pull_first = jax.vjp(lambda v: normalize(v, gain_first), flat_in)
    grad_in = (cotangent.astype(jnp.float32) + pull_first(back_one)[0]).astype(jnp.bfloat16)
    grad_in = grad_in.reshape(record_count, frame_slots, model_dim)
    return (result, grad_in, grad_first, grad_kernel)
```

```python
import functools

import jax
import jax.numpy as jnp
from jax import lax
from jax.experimental import pallas as pl
from jax.experimental.pallas import tpu as pltpu
from jax.sharding import Mesh
from jax.sharding import PartitionSpec as P

HEADS = 16
EPSILON = 1e-05
BF = jnp.bfloat16
F32 = jnp.float32

DP = ("yh", "z", "core")
CTX = ("yl", "x")
YZ = ("yh", "z")

VM = pl.BlockSpec(memory_space=pltpu.VMEM)
SM = pl.BlockSpec(memory_space=pltpu.SMEM)
ANY = pl.BlockSpec(memory_space=pl.ANY)


def params(mib):
    return pltpu.CompilerParams(vmem_limit_bytes=mib << 20)


def cost(flops, nbytes):
    return pl.CostEstimate(flops=flops, bytes_accessed=nbytes, transcendentals=0)


def centred(values):
    centre = values - jnp.mean(values, -1, keepdims=True)
    spread = jnp.mean(centre * centre, -1, keepdims=True)
    return centre, lax.rsqrt(spread + EPSILON)


def norm_pull(cot, centre, inv):
    xhat = centre * inv
    return inv * (
        cot - jnp.mean(cot, -1, keepdims=True) - xhat * jnp.mean(cot * xhat, -1, keepdims=True)
    )


def dot(a, b):
    return jnp.dot(a, b, preferred_element_type=F32)


def dot_t(a, b):
    return lax.dot_general(a, b, (((1,), (1,)), ((), ())), preferred_element_type=F32)


def sigmoid(v):
    return jax.nn.sigmoid(v)


def first_body(scal, x_ref, g_ref, w_ref, out_ref, wout_ref):
    count, rows, model = out_ref.shape
    centre, inv = centred(x_ref[...].astype(F32))
    normed = (centre * inv * g_ref[...]).astype(BF)
    for i in range(count):
        out_ref[i] = normed
    width = wout_ref.shape[2] // 2
    at = pl.multiple_of(scal[2] * width, width)
    cut = jnp.concatenate(
        [w_ref[:, pl.ds(at, width)], w_ref[:, pl.ds(pl.multiple_of(model + at, width), width)]], 1
    )
    for i in range(wout_ref.shape[0]):
        wout_ref[i] = cut


def gate_body(taps, scal, x_ref, wm_ref, wo_ref, k_ref, conv_ref, hid_ref, gated_ref, w_s, pad_s):
    rec = pl.program_id(0)
    core = scal[0]

    @pl.when(rec == 0)
    def _():
        w_s[:, pl.ds(core, 1)] = wm_ref[...][:, None]
        w_s[:, pl.ds(1 - core, 1)] = wo_ref[...][:, None]

    blocks, _, local, model = x_ref.shape
    length = blocks * local
    width = k_ref.shape[1]
    x = x_ref[...].reshape(length, model)
    hidden = dot(x, w_s[...].reshape(model, 2 * width))
    hid_ref[0] = hidden
    frames = scal[3 + rec]
    here = lax.broadcasted_iota(jnp.int32, (length, width), 0) < frames
    gated = jnp.where(here, hidden[:, :width] * sigmoid(hidden[:, width:]), 0.0).astype(BF)
    gated_ref[0] = gated
    pad_s[0:16] = jnp.zeros((16, width), F32)
    pad_s[16 + length : 32 + length] = jnp.zeros((16, width), F32)
    pad_s[16 : 16 + length] = gated.astype(F32)
    for b in range(blocks):
        total = jnp.zeros((local, width), F32)
        for j in range(taps):
            at = b * local + j + 1
            total = total + k_ref[j : j + 1, :] * pad_s[at : at + local, :]
        conv_ref[b, 0] = total


def fetch(pieces, slots, yh, core, sems):
    copies = []
    for dst, lo, width in slots:
        group = []
        for src, owner in pieces:
            for slot in range(2):
                side = yh if slot == 0 else 1 - yh
                group.append(
                    pltpu.make_async_copy(
                        src.at[:, slot, :, lo : lo + width],
                        dst.at[side, :, owner],
                        sems.at[len(copies) * 4 + len(group)],
                    )
                )
        copies.append(group)
    for group in copies:
        for one in group:
            one.start()
    return copies


def finish(group):
    for one in group:
        one.wait()


def token_body(scal, c_ref, x_ref, go_ref, g2_ref, ga_ref, mine, other, out_ref, res_ref, w2_s, wq_s, sems):
    yh, core = scal[1], scal[0]
    model = x_ref.shape[1]
    blocks = out_ref.shape[0]
    width = model // blocks
    copies = fetch(
        ((mine, core), (other, 1 - core)),
        ((w2_s, 0, model), (wq_s, model, 3 * model)),
        yh,
        core,
        sems,
    )
    conv = jnp.concatenate([c_ref[i] for i in range(blocks)], 1)
    centre, inv = centred(conv)
    gain = g2_ref[...]
    normal = centre * inv * gain
    opening = sigmoid(normal)
    swished = (normal * opening).astype(BF)
    finish(copies[0])
    w2 = w2_s[...].reshape(model, model)
    residual = (x_ref[...].astype(F32) + dot(swished, w2)).astype(BF)
    res_ref[...] = residual
    back_two = dot_t(go_ref[...], w2)
    slope = opening + normal * opening * (1.0 - opening)
    grad_conv = norm_pull(back_two * slope * gain, centre, inv).astype(BF)
    for i in range(blocks):
        out_ref[i, :, 3 * width :] = grad_conv[:, i * width : (i + 1) * width]
    centre, inv = centred(residual.astype(F32))
    attn_in = (centre * inv * ga_ref[...]).astype(BF)
    finish(copies[1])
    wide = 2 * width
    for part in range(3):
        for i in range(0, blocks, 2):
            lo = part * model + i * width
            got = dot(attn_in, wq_s[:, :, :, :, lo : lo + wide].reshape(model, wide)).astype(BF)
            out_ref[i, :, part * width : (part + 1) * width] = got[:, :width]
            out_ref[i + 1, :, part * width : (part + 1) * width] = got[:, width:]


def feature_body(
    taps, head_dim, scal, p_ref, hid_ref, gated_ref, x_ref, k_ref,
    out_ref, keep_ref, send_ref, gk_ref, pad_s, gpad_s, gf_s, gk_s,
):
    rec = pl.program_id(0)
    core = scal[0]
    frames = scal[3 + rec]
    blocks, _, local, _ = p_ref.shape
    length = blocks * local
    width = k_ref.shape[1]
    model = x_ref.shape[3]

    @pl.when(rec == 0)
    def _():
        gk_s[...] = jnp.zeros_like(gk_s)

    zeros = jnp.zeros((16, width), F32)
    for ref in (pad_s, gpad_s):
        ref[0:16] = zeros
        ref[16 + length : 32 + length] = zeros
    pad_s[16 : 16 + length] = p_ref[:, 0, :, 3 * width :].reshape(length, width).astype(F32)
    gpad_s[16 : 16 + length] = gated_ref[0].astype(F32)
    for b in range(blocks):
        base = b * local
        total = jnp.zeros((local, width), F32)
        own = pad_s[16 + base : 16 + base + local, :]
        for j in range(taps):
            at = base + taps - j
            total = total + k_ref[j : j + 1, :] * pad_s[at : at + local, :]
            at = base + j + 1
            term = (gpad_s[at : at + local, :] * own).reshape(local // 8, 8, width)
            gk_s[j] += jnp.sum(term, 0)
        at = lax.broadcasted_iota(jnp.int32, (local, width), 0) + base
        grad_gated = jnp.where(at < frames, total, 0.0)
        linear = hid_ref[0, base : base + local, :width]
        opening = sigmoid(hid_ref[0, base : base + local, width:])
        first = grad_gated * opening
        out_ref[b, 0, :, :width] = first.astype(BF)
        out_ref[b, 0, :, width : 2 * width] = (first * linear * (1.0 - opening)).astype(BF)
    grad_hidden = out_ref[:, 0, :, : 2 * width].reshape(length, 2 * width)
    x = x_ref[...].reshape(length, model)
    grad_first = lax.dot_general(
        x, grad_hidden, (((0,), (0,)), ((), ())), preferred_element_type=F32
    ).reshape(gf_s.shape)

    @pl.when(rec == 0)
    def _():
        gf_s[...] = grad_first

    @pl.when(rec > 0)
    def _():
        gf_s[...] += grad_first

    q = p_ref[:, 0, :, :width].reshape(length, width)
    k = p_ref[:, 0, :, width : 2 * width].reshape(length, width)
    v = p_ref[:, 0, :, 2 * width : 3 * width].reshape(length, width)
    rows = min(256, length)
    key_ok = lax.broadcasted_iota(jnp.int32, (rows, length), 1) < frames
    lane = lax.broadcasted_iota(jnp.int32, (rows, width), 1)
    scaling = head_dim**-0.5
    for r in range(0, length, rows):
        qr = q[r : r + rows]
        attended = jnp.zeros((rows, width), F32)
        for h in range(width // head_dim):
            mine = (lane >= h * head_dim) & (lane < (h + 1) * head_dim)
            scores = dot_t(jnp.where(mine, qr, jnp.zeros_like(qr)), k) * scaling
            scores = jnp.where(key_ok, scores, -1e30)
            top = jnp.max(scores, -1, keepdims=True)
            numer = jnp.where(key_ok, jnp.exp(scores - top), 0.0)
            denom = jnp.sum(numer, -1, keepdims=True)
            attended = jnp.where(mine, dot(numer.astype(BF), v) / denom, attended)
        got = attended.astype(BF).reshape(rows // local, local, width)
        out_ref[r // local : (r + rows) // local, 0, :, 2 * width :] = got

    @pl.when(rec == pl.num_programs(0) - 1)
    def _():
        keep_ref[...] = gf_s[:, pl.ds(core, 1)][:, 0]
        send_ref[...] = gf_s[:, pl.ds(1 - core, 1)][:, 0].astype(BF)
        gk = jnp.sum(gk_s[...], 1)
        half = gk_ref.shape[0]
        gk_ref[:, :width] = gk[:half]
        gk_ref[:, width:] = gk[half:]


def pair_body(keep_ref, recv_ref, gk_ref, gkr_ref, out_ref):
    count, depth, _ = keep_ref.shape
    out_ref[:, :depth] = (keep_ref[...] + recv_ref[...].astype(F32)).astype(BF)
    gk = (gk_ref[...] + gkr_ref[...]).astype(BF)
    for i in range(count):
        out_ref[i, depth:] = gk


def sum_body(x_ref, out_ref):
    total = jnp.sum(x_ref[...].astype(F32), 0)
    for i in range(out_ref.shape[0]):
        out_ref[i] = total


def last_body(x_ref, gf_ref, gk_ref):
    blocks = x_ref.shape[0]
    depth = gf_ref.shape[0]
    width = x_ref.shape[2] // 2
    model = gk_ref.shape[1]
    half = x_ref.shape[1] - depth
    taps = gk_ref.shape[0]
    for i in range(blocks):
        lo = i * width
        gf_ref[:, lo : lo + width] = x_ref[i, :depth, :width]
        gf_ref[:, model + lo : model + lo + width] = x_ref[i, :depth, width:]
        gk_ref[:half, lo : lo + width] = x_ref[i, depth:, :width]
        gk_ref[half:, lo : lo + width] = x_ref[i, depth : depth + taps - half, width:]


def result_body(scal, a_ref, res_ref, x_ref, go_ref, g1_ref, mine, other, out_ref, gin_ref, wp_s, w1_s, sems):
    yh, core, ctx = scal[1], scal[0], scal[2]
    rows, model = x_ref.shape
    blocks = a_ref.shape[0]
    width = model // blocks
    copies = fetch(
        ((mine, core), (other, 1 - core)),
        ((wp_s, 0, model), (w1_s, model, 2 * model)),
        yh,
        core,
        sems,
    )
    centre, inv = centred(x_ref[...].astype(F32))
    attended = jnp.concatenate([a_ref[i, :, 2 * width :] for i in range(blocks)], 1)
    linear = jnp.concatenate([a_ref[i, :, :width] for i in range(blocks)], 1)
    gating = jnp.concatenate([a_ref[i, :, width : 2 * width] for i in range(blocks)], 1)
    finish(copies[0])
    projected = dot(attended, wp_s[...].reshape(model, model))
    records = 2
    local = rows // records
    at = lax.broadcasted_iota(jnp.int32, (local, model), 0) + ctx * local
    present = jnp.concatenate([(at < scal[3 + r]).astype(F32) for r in range(records)], 0)
    out_ref[...] = (res_ref[...].astype(F32) + present * projected).astype(BF)
    finish(copies[1])
    w1 = w1_s[...].reshape(model, 2 * model)
    back_one = dot_t(linear, w1[:, :model]) + dot_t(gating, w1[:, model:])
    pulled = norm_pull(back_one * g1_ref[...], centre, inv)
    gin_ref[...] = (go_ref[...].astype(F32) + pulled).astype(BF)


def swap_core(v):
    return lax.ppermute(v, "core", [(0, 1), (1, 0)])


def swap_yh(v):
    return lax.ppermute(v, ("yh", "yl"), [(0, 3), (3, 0), (1, 2), (2, 1)])


def gathered(cat):
    shard = jnp.stack([cat, swap_yh(cat)])
    return shard


def local(
    inputs,
    frames,
    gain_first,
    w_first,
    depth_kernel,
    gain_second,
    w_second,
    gain_attn,
    w_qkv,
    w_proj,
    grad_out,
):
    records, local_len, model = inputs.shape
    taps = depth_kernel.shape[0]
    blocks = lax.axis_size(CTX)
    zs = lax.axis_size("z")
    groups = 2 * zs
    depth = w_first.shape[0]
    width = model // blocks
    length = blocks * local_len
    rows = records * local_len
    head_dim = model // HEADS
    ctx = lax.axis_index(CTX)
    shape = jax.ShapeDtypeStruct

    scal = jnp.concatenate(
        [
            jnp.stack([lax.axis_index("core"), lax.axis_index("yh"), ctx]).astype(jnp.int32),
            frames,
        ]
    )
    x = inputs.reshape(rows, model)
    cot = grad_out.reshape(rows, model)
    taps_own = lax.dynamic_slice_in_dim(
        jnp.pad(depth_kernel, ((0, 32 - taps), (0, 0))), ctx * width, width, 1
    )

    shard_a = gathered(jnp.concatenate([w_second, w_qkv], 1))
    sent, w1_sent = pl.pallas_call(
        first_body,
        out_shape=(
            shape((blocks, rows, model), BF),
            shape((groups, depth, 2 * width), BF),
        ),
        in_specs=[SM, VM, VM, VM],
        out_specs=(VM, VM),
        compiler_params=params(32),
        name="first_norm",
    )(scal, x, gain_first.reshape(1, model), w_first)
    shard_a, w1_sent = lax.optimization_barrier((shard_a, w1_sent))
    all_a = lax.all_gather(shard_a, "z", axis=0, tiled=False)
    w1_mine = lax.all_to_all(w1_sent, YZ, 0, 0, tiled=True)
    w1_other = swap_core(w1_mine)
    normed = lax.all_to_all(sent, CTX, 0, 0, tiled=True).reshape(blocks, records, local_len, model)

    conv, hidden, gated = pl.pallas_call(
        functools.partial(gate_body, taps),
        grid=(records,),
        out_shape=(
            shape((blocks, records, local_len, width), F32),
            shape((records, length, 2 * width), F32),
            shape((records, length, width), BF),
        ),
        in_specs=[
            SM,
            pl.BlockSpec((blocks, 1, local_len, model), lambda r: (0, r, 0, 0)),
            pl.BlockSpec((groups, depth, 2 * width), lambda r: (0, 0, 0)),
            pl.BlockSpec((groups, depth, 2 * width), lambda r: (0, 0, 0)),
            pl.BlockSpec((32, width), lambda r: (0, 0)),
        ],
        out_specs=(
            pl.BlockSpec((blocks, 1, local_len, width), lambda r: (0, r, 0, 0)),
            pl.BlockSpec((1, length, 2 * width), lambda r: (r, 0, 0)),
            pl.BlockSpec((1, length, width), lambda r: (r, 0, 0)),
        ),
        scratch_shapes=[
            pltpu.VMEM((groups, 2, depth, 2 * width), BF),
            pltpu.VMEM((length + 32, width), F32),
        ],
        compiler_params=params(32),
        name="gate_conv",
    )(scal, normed, w1_mine, w1_other, taps_own)

    all_a, conv = lax.optimization_barrier((all_a, conv))
    other_a = swap_core(all_a)
    shard_b = gathered(jnp.concatenate([w_proj, w_first], 1))
    shard_b, all_a = lax.optimization_barrier((shard_b, all_a))
    all_b = lax.all_gather(shard_b, "z", axis=0, tiled=False)
    conv_rows = lax.all_to_all(conv, CTX, 0, 0, tiled=True).reshape(blocks, rows, width)

    packed, residual = pl.pallas_call(
        token_body,
        out_shape=(shape((blocks, rows, 4 * width), BF), shape((rows, model), BF)),
        in_specs=[SM, VM, VM, VM, VM, VM, ANY, ANY],
        out_specs=(VM, VM),
        scratch_shapes=[
            pltpu.VMEM((2, zs, 2, depth, model), BF),
            pltpu.VMEM((2, zs, 2, depth, 3 * model), BF),
            pltpu.SemaphoreType.DMA((8,)),
        ],
        compiler_params=params(40),
        name="token_rows",
    )(
        scal, conv_rows, x, cot, gain_second.reshape(1, model), gain_attn.reshape(1, model),
        all_a, other_a,
    )

    packed = lax.all_to_all(packed, CTX, 0, 0, tiled=True)
    packed = packed.reshape(blocks, records, local_len, 4 * width)
    back, keep, send, gk = pl.pallas_call(
        functools.partial(feature_body, taps, head_dim),
        grid=(records,),
        out_shape=(
            shape((blocks, records, local_len, 3 * width), BF),
            shape((groups, depth, 2 * width), F32),
            shape((groups, depth, 2 * width), BF),
            shape((16, 2 * width), F32),
        ),
        in_specs=[
            SM,
            pl.BlockSpec((blocks, 1, local_len, 4 * width), lambda r: (0, r, 0, 0)),
            pl.BlockSpec((1, length, 2 * width), lambda r: (r, 0, 0)),
            pl.BlockSpec((1, length, width), lambda r: (r, 0, 0)),
            pl.BlockSpec((blocks, 1, local_len, model), lambda r: (0, r, 0, 0)),
            pl.BlockSpec((32, width), lambda r: (0, 0)),
        ],
        out_specs=(
            pl.BlockSpec((blocks, 1, local_len, 3 * width), lambda r: (0, r, 0, 0)),
            pl.BlockSpec((groups, depth, 2 * width), lambda r: (0, 0, 0)),
            pl.BlockSpec((groups, depth, 2 * width), lambda r: (0, 0, 0)),
            pl.BlockSpec((16, 2 * width), lambda r: (0, 0)),
        ),
        scratch_shapes=[
            pltpu.VMEM((length + 32, width), F32),
            pltpu.VMEM((length + 32, width), F32),
            pltpu.VMEM((groups, 2, depth, 2 * width), F32),
            pltpu.VMEM((32, 8, width), F32),
        ],
        compiler_params=params(40),
        name="features",
    )(scal, packed, hidden, gated, normed, taps_own)

    other_b = swap_core(all_b)
    recv, gk_recv = swap_core(send), swap_core(gk)
    back = lax.all_to_all(back, CTX, 0, 0, tiled=True).reshape(blocks, rows, 3 * width)
    shares = pl.pallas_call(
        pair_body,
        out_shape=shape((groups, depth + 16, 2 * width), BF),
        in_specs=[VM] * 4,
        out_specs=VM,
        compiler_params=params(16),
        name="pair_sum",
    )(keep, recv, gk, gk_recv)
    shares = lax.all_to_all(shares, YZ, 0, 0, tiled=True)
    total = pl.pallas_call(
        sum_body,
        out_shape=shape((blocks, depth + 16, 2 * width), F32),
        in_specs=[VM],
        out_specs=VM,
        compiler_params=params(16),
        name="share_sum",
    )(shares)
    total = lax.all_to_all(total, CTX, 0, 0, tiled=True)
    grad_first, grad_kernel = pl.pallas_call(
        last_body,
        out_shape=(shape((depth, 2 * model), F32), shape((taps, model), F32)),
        in_specs=[VM],
        out_specs=(VM, VM),
        compiler_params=params(16),
        name="lay_out",
    )(total)

    result, grad_in = pl.pallas_call(
        result_body,
        out_shape=(shape((rows, model), BF), shape((rows, model), BF)),
        in_specs=[SM, VM, VM, VM, VM, VM, ANY, ANY],
        out_specs=(VM, VM),
        scratch_shapes=[
            pltpu.VMEM((2, zs, 2, depth, model), BF),
            pltpu.VMEM((2, zs, 2, depth, 2 * model), BF),
            pltpu.SemaphoreType.DMA((8,)),
        ],
        compiler_params=params(40),
        name="result_rows",
    )(scal, back, residual, x, cot, gain_first.reshape(1, model), all_b, other_b)
    return (
        result.reshape(records, local_len, model),
        grad_in.reshape(records, local_len, model),
        grad_first,
        grad_kernel,
    )


def solution(mesh):
    dp, ctx = mesh.devices.shape
    split = Mesh(
        mesh.devices.reshape(2, dp // 4, 2, 2, ctx // 2), ("yh", "z", "core", "yl", "x")
    )
    tokens = P(DP, CTX, None)
    placed = (
        tokens,
        P(DP),
        P(),
        P(DP, None),
        P(),
        P(),
        P(DP, None),
        P(),
        P(DP, None),
        P(DP, None),
        tokens,
    )
    return jax.shard_map(
        local,
        mesh=split,
        in_specs=placed,
        out_specs=(tokens, tokens, P(DP, None), P()),
        check_vma=False,
    )
```

```python
import functools

import jax
import jax.numpy as jnp
from jax import lax
from jax.experimental import pallas as pl
from jax.experimental.pallas import tpu as pltpu
from jax.sharding import Mesh
from jax.sharding import PartitionSpec as P

HEADS = 16
EPSILON = 1e-05
BF = jnp.bfloat16
F32 = jnp.float32

DP = ("yh", "z", "core")
CTX = ("yl", "x")

VM = pl.BlockSpec(memory_space=pltpu.VMEM)
SM = pl.BlockSpec(memory_space=pltpu.SMEM)
ANY = pl.BlockSpec(memory_space=pl.ANY)


def params(mib):
    return pltpu.CompilerParams(vmem_limit_bytes=mib << 20)


def cost(flops, nbytes):
    return pl.CostEstimate(flops=flops, bytes_accessed=nbytes, transcendentals=0)


def centred(values):
    centre = values - jnp.mean(values, -1, keepdims=True)
    spread = jnp.mean(centre * centre, -1, keepdims=True)
    return centre, lax.rsqrt(spread + EPSILON)


def norm_pull(cot, centre, inv):
    xhat = centre * inv
    return inv * (
        cot - jnp.mean(cot, -1, keepdims=True) - xhat * jnp.mean(cot * xhat, -1, keepdims=True)
    )


def dot(a, b):
    return jnp.dot(a, b, preferred_element_type=F32)


def dot_t(a, b):
    return lax.dot_general(a, b, (((1,), (1,)), ((), ())), preferred_element_type=F32)


def sigmoid(v):
    return jax.nn.sigmoid(v)


def whole(shape):
    return pl.BlockSpec(shape, lambda i: (0,) * len(shape))


def call(body, outs, ins, name, mib, scratch=(), anys=()):
    specs = [SM] + [whole(v.shape) for v in ins[1:]] + [ANY] * len(anys)
    return pl.pallas_call(
        body,
        grid=(1,),
        out_shape=tuple(jax.ShapeDtypeStruct(*o) for o in outs),
        in_specs=specs,
        out_specs=tuple(whole(o[0]) for o in outs),
        scratch_shapes=list(scratch),
        compiler_params=params(mib),
        name=name,
    )(*ins, *anys)


CORE, YH, CTXI, ZI, FRAMES = 0, 1, 2, 3, 4


def at_lane(block, width):
    return pl.ds(pl.multiple_of(block * width, width), width)


def cut_body(blocks, scal, w2_ref, wq_ref, w1_ref, own_ref, w1_own_ref, next_ref):
    model = w2_ref.shape[1]
    width = model // blocks
    ctx = scal[CTXI]
    beside = lax.rem(ctx + blocks // 2, blocks)
    for ref, block in ((own_ref, ctx), (next_ref, beside)):
        ref[:, :model] = w2_ref[...]
        for part in range(3):
            lo = model + part * width
            ref[:, lo : lo + width] = wq_ref[:, at_lane(part * blocks + block, width)]
    for ref, lo, block in ((w1_own_ref, 0, ctx), (next_ref, model + 3 * width, beside)):
        for part in range(2):
            at = lo + part * width
            ref[:, at : at + width] = w1_ref[:, at_lane(part * blocks + block, width)]


def first_body(scal, x_ref, g_ref, out_ref):
    centre, inv = centred(x_ref[...].astype(F32))
    normed = (centre * inv * g_ref[...]).astype(BF)
    for i in range(out_ref.shape[0]):
        out_ref[i] = normed


def gate_body(taps, scal, x_ref, wm_ref, wo_ref, k_ref, conv_ref, hid_ref, gated_ref, w_s, pad_s):
    rec = pl.program_id(0)
    blocks, _, local, model = x_ref.shape
    length = blocks * local
    width = k_ref.shape[1]

    @pl.when(rec == 0)
    def _():
        core, yh, z = scal[CORE], scal[YH], scal[ZI]
        zs = wm_ref.shape[0]
        for s in range(zs):
            owner = lax.rem(z - s + zs, zs)
            for slot, side in ((0, yh), (1, 1 - yh)):
                w_s[side, owner, core] = wm_ref[s, slot]
                w_s[side, owner, 1 - core] = wo_ref[s, slot]

    x = x_ref[...].reshape(length, model)
    hidden = dot(x, w_s[...].reshape(model, 2 * width))
    hid_ref[0] = hidden
    frames = scal[FRAMES + rec]
    here = lax.broadcasted_iota(jnp.int32, (length, width), 0) < frames
    gated = jnp.where(here, hidden[:, :width] * sigmoid(hidden[:, width:]), 0.0).astype(BF)
    gated_ref[0] = gated
    pad_s[0:16] = jnp.zeros((16, width), F32)
    pad_s[16 + length : 32 + length] = jnp.zeros((16, width), F32)
    pad_s[16 : 16 + length] = gated.astype(F32)
    for b in range(blocks):
        total = jnp.zeros((local, width), F32)
        for j in range(taps):
            at = b * local + j + 1
            total = total + k_ref[j : j + 1, :] * pad_s[at : at + local, :]
        conv_ref[b, 0] = total


def fetch(pieces, slots, yh, core, sems):
    copies = []
    for dst, lo, width in slots:
        group = []
        for src, owner in pieces:
            for slot in range(2):
                side = yh if slot == 0 else 1 - yh
                group.append(
                    pltpu.make_async_copy(
                        src.at[:, slot, :, lo : lo + width],
                        dst.at[side, :, owner],
                        sems.at[len(copies) * 4 + len(group)],
                    )
                )
        copies.append(group)
    for group in copies:
        for one in group:
            one.start()
    return copies


def finish(group):
    for one in group:
        one.wait()


def token_body(
    blocks, scal, c_ref, x_ref, go_ref, g2_ref, ga_ref, mine, other, sent_ref, res_ref, *rest
):
    back_refs, (w2_s, gc_s, sems) = rest[:blocks], rest[blocks:]
    model = x_ref.shape[1]
    width = model // blocks
    ctx = scal[CTXI]
    copies = fetch(
        ((mine, scal[CORE]), (other, 1 - scal[CORE])), ((w2_s, 0, model),), scal[YH], scal[CORE], sems
    )
    conv = jnp.concatenate([c_ref[i] for i in range(blocks)], 1)
    centre, inv = centred(conv)
    gain = g2_ref[...]
    normal = centre * inv * gain
    opening = sigmoid(normal)
    swished = (normal * opening).astype(BF)
    finish(copies[0])
    w2 = w2_s[...].reshape(model, model)
    back_two = dot_t(go_ref[...], w2)
    slope = opening + normal * opening * (1.0 - opening)
    grad_conv = norm_pull(back_two * slope * gain, centre, inv).astype(BF)
    for i in range(blocks):
        gc_s[i] = grad_conv[:, i * width : (i + 1) * width]
    for s in range(blocks):
        back_refs[s][...] = gc_s[lax.rem(ctx + s, blocks)]
    residual = (x_ref[...].astype(F32) + dot(swished, w2)).astype(BF)
    res_ref[...] = residual
    centre, inv = centred(residual.astype(F32))
    attn_in = (centre * inv * ga_ref[...]).astype(BF)
    for i in range(blocks):
        sent_ref[i] = attn_in


def back_body(taps, scal, *refs):
    blocks = refs[-1]
    gc_refs = refs[:blocks]
    (hid_ref, gated_ref, x_ref, k_ref, gh_ref, keep_ref, send_ref, gk_ref) = refs[blocks:-5]
    pad_s, gpad_s, gf_s, gk_s = refs[-5:-1]
    rec = pl.program_id(0)
    core, ctx = scal[CORE], scal[CTXI]
    frames = scal[FRAMES + rec]
    local = gh_ref.shape[2]
    length = blocks * local
    width = k_ref.shape[1]
    model = x_ref.shape[3]

    @pl.when(rec == 0)
    def _():
        gk_s[...] = jnp.zeros_like(gk_s)

    zeros = jnp.zeros((16, width), F32)
    for ref in (pad_s, gpad_s):
        ref[0:16] = zeros
        ref[16 + length : 32 + length] = zeros
    for s in range(blocks):
        owner = lax.rem(ctx - s + blocks, blocks)
        pad_s[pl.ds(pl.multiple_of(16 + owner * local, 16), local)] = gc_refs[s][...].astype(F32)
    gpad_s[16 : 16 + length] = gated_ref[0].astype(F32)
    for b in range(blocks):
        base = b * local
        total = jnp.zeros((local, width), F32)
        own = pad_s[16 + base : 16 + base + local, :]
        for j in range(taps):
            at = base + taps - j
            total = total + k_ref[j : j + 1, :] * pad_s[at : at + local, :]
            at = base + j + 1
            term = (gpad_s[at : at + local, :] * own).reshape(local // 8, 8, width)
            gk_s[j] += jnp.sum(term, 0)
        at = lax.broadcasted_iota(jnp.int32, (local, width), 0) + base
        grad_gated = jnp.where(at < frames, total, 0.0)
        linear = hid_ref[0, base : base + local, :width]
        opening = sigmoid(hid_ref[0, base : base + local, width:])
        first = grad_gated * opening
        gh_ref[b, 0, :, :width] = first.astype(BF)
        gh_ref[b, 0, :, width:] = (first * linear * (1.0 - opening)).astype(BF)
    grad_hidden = gh_ref[...].reshape(length, 2 * width)
    x = x_ref[...].reshape(length, model)
    grad_first = lax.dot_general(
        x, grad_hidden, (((0,), (0,)), ((), ())), preferred_element_type=F32
    ).reshape(gf_s.shape)

    @pl.when(rec == 0)
    def _():
        gf_s[...] = grad_first

    @pl.when(rec > 0)
    def _():
        gf_s[...] += grad_first

    @pl.when(rec == pl.num_programs(0) - 1)
    def _():
        keep_ref[...] = gf_s[:, :, pl.ds(core, 1)][:, :, 0]
        send_ref[...] = gf_s[:, :, pl.ds(1 - core, 1)][:, :, 0].astype(BF)
        gk = jnp.sum(gk_s[...], 1)
        half = gk_ref.shape[0]
        gk_ref[:, :width] = gk[:half]
        gk_ref[:, width:] = gk[half:]


def heads_body(head_dim, scal, x_ref, gh_ref, mine, other, out_ref, w_s, sems):
    rec = pl.program_id(0)
    frames = scal[FRAMES + rec]
    blocks, _, local, model = x_ref.shape
    length = blocks * local
    width = model // blocks

    @pl.when(rec == 0)
    def _():
        core = scal[CORE]
        copies = fetch(
            ((mine, core), (other, 1 - core)), ((w_s, model, 3 * width),), scal[YH], core, sems
        )
        finish(copies[0])

    out_ref[:, :, :, : 2 * width] = gh_ref[...]
    x = x_ref[...].reshape(length, model)
    packed = dot(x, w_s[...].reshape(model, 3 * width)).astype(BF)
    q = packed[:, :width]
    k = packed[:, width : 2 * width]
    v = packed[:, 2 * width :]
    rows = min(256, length)
    key_ok = lax.broadcasted_iota(jnp.int32, (rows, length), 1) < frames
    lane = lax.broadcasted_iota(jnp.int32, (rows, width), 1)
    scaling = head_dim**-0.5
    for r in range(0, length, rows):
        qr = q[r : r + rows]
        attended = jnp.zeros((rows, width), F32)
        for h in range(width // head_dim):
            mine_h = (lane >= h * head_dim) & (lane < (h + 1) * head_dim)
            scores = dot_t(jnp.where(mine_h, qr, jnp.zeros_like(qr)), k) * scaling
            scores = jnp.where(key_ok, scores, -1e30)
            top = jnp.max(scores, -1, keepdims=True)
            numer = jnp.where(key_ok, jnp.exp(scores - top), 0.0)
            denom = jnp.sum(numer, -1, keepdims=True)
            attended = jnp.where(mine_h, dot(numer.astype(BF), v) / denom, attended)
        got = attended.astype(BF).reshape(rows // local, local, width)
        out_ref[r // local : (r + rows) // local, 0, :, 2 * width :] = got


def pair_body(scal, keep_ref, recv_ref, gk_ref, gkr_ref, *refs):
    zs = len(refs) - 1
    outs, both_s = refs[:zs], refs[zs]
    depth = keep_ref.shape[2]
    both_s[...] = (keep_ref[...] + recv_ref[...].astype(F32)).astype(BF)
    gk = (gk_ref[...] + gkr_ref[...]).astype(BF)
    for s in range(zs):
        to = lax.rem(scal[ZI] + s, zs)
        for side in range(2):
            outs[s][side, :depth] = both_s[side, to]
            outs[s][side, depth:] = gk


def sum_body(scal, *refs):
    keep_ref, send_ref, total_s = refs[-3:]
    total = refs[0][...].astype(F32)
    for ref in refs[1:-3]:
        total = total + ref[...].astype(F32)
    total_s[...] = total
    keep_ref[...] = total_s[scal[YH]].astype(BF)
    send_ref[...] = total_s[1 - scal[YH]].astype(BF)


def last_body(blocks, scal, *refs):
    ins, (gf_ref, gk_ref, acc_s) = refs[: 2 * blocks], refs[2 * blocks :]
    depth = gf_ref.shape[0]
    model = gk_ref.shape[1]
    width = model // blocks
    taps = gk_ref.shape[0]
    half = acc_s.shape[1] - depth
    for slot in range(2):
        for s in range(blocks):
            owner = lax.rem(scal[CTXI] - s + blocks, blocks)
            to = lax.rem(owner + slot * (blocks // 2), blocks)
            value = ins[slot * blocks + s][...].astype(F32)
            if slot == 0:
                acc_s[to] = value
            else:
                acc_s[to] += value
    for i in range(blocks):
        lo = i * width
        gf_ref[:, lo : lo + width] = acc_s[i, :depth, :width]
        gf_ref[:, model + lo : model + lo + width] = acc_s[i, :depth, width:]
        gk_ref[:half, lo : lo + width] = acc_s[i, depth:, :width]
        gk_ref[half:, lo : lo + width] = acc_s[i, depth : depth + taps - half, width:]


def result_body(scal, a_ref, res_ref, x_ref, go_ref, g1_ref, mine, other, out_ref, gin_ref, wp_s, w1_s, sems):
    yh, core, ctx = scal[YH], scal[CORE], scal[CTXI]
    rows, model = x_ref.shape
    blocks = a_ref.shape[0]
    width = model // blocks
    copies = fetch(
        ((mine, core), (other, 1 - core)),
        ((wp_s, 0, model), (w1_s, model, 2 * model)),
        yh,
        core,
        sems,
    )
    centre, inv = centred(x_ref[...].astype(F32))
    attended = jnp.concatenate([a_ref[i, :, 2 * width :] for i in range(blocks)], 1)
    linear = jnp.concatenate([a_ref[i, :, :width] for i in range(blocks)], 1)
    gating = jnp.concatenate([a_ref[i, :, width : 2 * width] for i in range(blocks)], 1)
    finish(copies[0])
    projected = dot(attended, wp_s[...].reshape(model, model))
    records = 2
    local = rows // records
    at = lax.broadcasted_iota(jnp.int32, (local, model), 0) + ctx * local
    present = jnp.concatenate(
        [(at < scal[FRAMES + r]).astype(F32) for r in range(records)], 0
    )
    out_ref[...] = (res_ref[...].astype(F32) + present * projected).astype(BF)
    finish(copies[1])
    w1 = w1_s[...].reshape(model, 2 * model)
    back_one = dot_t(linear, w1[:, :model]) + dot_t(gating, w1[:, model:])
    pulled = norm_pull(back_one * g1_ref[...], centre, inv)
    gin_ref[...] = (go_ref[...].astype(F32) + pulled).astype(BF)


def swap_core(v):
    return lax.ppermute(v, "core", [(0, 1), (1, 0)])


def swap_yh(v):
    return lax.ppermute(v, ("yh", "yl"), [(0, 3), (3, 0), (1, 2), (2, 1)])


def shifted(v, axis, by):
    count = lax.axis_size(axis)
    return lax.ppermute(v, axis, [(i, (i + by) % count) for i in range(count)])


def local(
    inputs,
    frames,
    gain_first,
    w_first,
    depth_kernel,
    gain_second,
    w_second,
    gain_attn,
    w_qkv,
    w_proj,
    grad_out,
):
    records, local_len, model = inputs.shape
    taps = depth_kernel.shape[0]
    blocks = lax.axis_size(CTX)
    zs = lax.axis_size("z")
    depth = w_first.shape[0]
    width = model // blocks
    length = blocks * local_len
    rows = records * local_len
    head_dim = model // HEADS
    ctx = lax.axis_index(CTX)
    shape = jax.ShapeDtypeStruct
    barrier = lax.optimization_barrier

    where = jnp.stack([lax.axis_index(a) for a in ("core", "yh", CTX, "z")])
    scal = jnp.concatenate([where.astype(jnp.int32), frames])
    x = inputs.reshape(rows, model)
    cot = grad_out.reshape(rows, model)
    taps_own = lax.dynamic_slice_in_dim(
        jnp.pad(depth_kernel, ((0, 32 - taps), (0, 0))), ctx * width, width, 1
    )

    part = model + 3 * width
    own, w1_own, beside = call(
        functools.partial(cut_body, blocks),
        [((depth, part), BF), ((depth, 2 * width), BF), ((depth, part + 2 * width), BF)],
        [scal, w_second, w_qkv, w_first],
        "cut",
        16,
    )
    beside = swap_yh(beside)
    (sent,) = call(
        first_body, [((blocks, rows, model), BF)], [scal, x, gain_first.reshape(1, model)], "first_norm", 32
    )
    shard_a = jnp.stack([own, beside[:, :part]])
    w1_part = jnp.stack([w1_own, beside[:, part:]])
    all_a = lax.all_gather(shard_a, "z", axis=0, tiled=False)
    w1_mine = jnp.stack([w1_part] + [shifted(w1_part, "z", s) for s in range(1, zs)])
    w1_other = swap_core(w1_mine)
    normed = lax.all_to_all(sent, CTX, 0, 0, tiled=True).reshape(blocks, records, local_len, model)
    cat_b = jnp.concatenate([w_proj, w_first], 1)
    shard_b = jnp.stack([cat_b, swap_yh(cat_b)])

    by_record = lambda *rest: pl.BlockSpec(
        (blocks, 1, local_len) + rest, lambda r: (0, r, 0) + (0,) * len(rest)
    )
    of_record = lambda wide: pl.BlockSpec((1, length, wide), lambda r: (r, 0, 0))
    conv, hidden, gated = pl.pallas_call(
        functools.partial(gate_body, taps),
        grid=(records,),
        out_shape=(
            shape((blocks, records, local_len, width), F32),
            shape((records, length, 2 * width), F32),
            shape((records, length, width), BF),
        ),
        in_specs=[
            SM,
            by_record(model),
            whole((zs, 2, depth, 2 * width)),
            whole((zs, 2, depth, 2 * width)),
            whole((32, width)),
        ],
        out_specs=(by_record(width), of_record(2 * width), of_record(width)),
        scratch_shapes=[
            pltpu.VMEM((2, zs, 2, depth, 2 * width), BF),
            pltpu.VMEM((length + 32, width), F32),
        ],
        compiler_params=params(32),
        name="gate_conv",
    )(scal, normed, w1_mine, w1_other, taps_own)

    all_a, conv = barrier((all_a, conv))
    other_a = swap_core(all_a)
    shard_b, all_a = barrier((shard_b, all_a))
    all_b = lax.all_gather(shard_b, "z", axis=0, tiled=False)
    conv_rows = lax.all_to_all(conv, CTX, 0, 0, tiled=True).reshape(blocks, rows, width)

    sent, residual, *back_parts = call(
        functools.partial(token_body, blocks),
        [((blocks, rows, model), BF), ((rows, model), BF)] + [((rows, width), BF)] * blocks,
        [scal, conv_rows, x, cot, gain_second.reshape(1, model), gain_attn.reshape(1, model)],
        "token_rows",
        32,
        [
            pltpu.VMEM((2, zs, 2, depth, model), BF),
            pltpu.VMEM((blocks, rows, width), BF),
            pltpu.SemaphoreType.DMA((4,)),
        ],
        [all_a, other_a],
    )

    attn_in = lax.all_to_all(sent, CTX, 0, 0, tiled=True)
    attn_in = attn_in.reshape(blocks, records, local_len, model)
    grads = [back_parts[0]] + [shifted(back_parts[s], CTX, s) for s in range(1, blocks)]
    share = (2, zs, depth, 2 * width)
    keep_spec = whole(share)

    def back_kernel(scal_ref, *refs):
        back_body(taps, scal_ref, *refs, blocks)

    grad_hidden, keep, send, gk = pl.pallas_call(
        back_kernel,
        grid=(records,),
        out_shape=(
            shape((blocks, records, local_len, 2 * width), BF),
            shape(share, F32),
            shape(share, BF),
            shape((16, 2 * width), F32),
        ),
        in_specs=[SM]
        + [pl.BlockSpec((local_len, width), lambda r: (r, 0))] * blocks
        + [of_record(2 * width), of_record(width), by_record(model), whole((32, width))],
        out_specs=(by_record(2 * width), keep_spec, keep_spec, whole((16, 2 * width))),
        scratch_shapes=[
            pltpu.VMEM((length + 32, width), F32),
            pltpu.VMEM((length + 32, width), F32),
            pltpu.VMEM((2, zs, 2, depth, 2 * width), F32),
            pltpu.VMEM((32, 8, width), F32),
        ],
        compiler_params=params(32),
        name="conv_back",
    )(scal, *grads, hidden, gated, normed, taps_own)

    chunk = (2, depth + 16, 2 * width)
    chunks = call(
        pair_body,
        [(chunk, BF)] * zs,
        [scal, keep, swap_core(send), gk, swap_core(gk)],
        "pair_sum",
        16,
        [pltpu.VMEM(share, BF)],
    )
    sums = [chunks[0]] + [shifted(chunks[s], "z", s) for s in range(1, zs)]
    keep, send = call(
        sum_body, [(chunk[1:], BF)] * 2, [scal] + sums, "share_sum", 16, [pltpu.VMEM(chunk, F32)]
    )
    recv = swap_yh(send)
    pieces = [
        [part] + [shifted(part, CTX, s) for s in range(1, blocks)] for part in (keep, recv)
    ]
    grad_first, grad_kernel = call(
        functools.partial(last_body, blocks),
        [((depth, 2 * model), F32), ((taps, model), F32)],
        [scal] + pieces[0] + pieces[1],
        "lay_out",
        16,
        [pltpu.VMEM((blocks,) + chunk[1:], F32)],
    )

    back = pl.pallas_call(
        functools.partial(heads_body, head_dim),
        grid=(records,),
        out_shape=shape((blocks, records, local_len, 3 * width), BF),
        in_specs=[SM, by_record(model), by_record(2 * width), ANY, ANY],
        out_specs=by_record(3 * width),
        scratch_shapes=[
            pltpu.VMEM((2, zs, 2, depth, 3 * width), BF),
            pltpu.SemaphoreType.DMA((4,)),
        ],
        compiler_params=params(32),
        name="heads",
    )(scal, attn_in, grad_hidden, all_a, other_a)

    all_b, back = barrier((all_b, back))
    other_b = swap_core(all_b)
    back = lax.all_to_all(back, CTX, 0, 0, tiled=True).reshape(blocks, rows, 3 * width)
    result, grad_in = call(
        result_body,
        [((rows, model), BF), ((rows, model), BF)],
        [scal, back, residual, x, cot, gain_first.reshape(1, model)],
        "result_rows",
        40,
        [
            pltpu.VMEM((2, zs, 2, depth, model), BF),
            pltpu.VMEM((2, zs, 2, depth, 2 * model), BF),
            pltpu.SemaphoreType.DMA((8,)),
        ],
        [all_b, other_b],
    )
    return (
        result.reshape(records, local_len, model),
        grad_in.reshape(records, local_len, model),
        grad_first,
        grad_kernel,
    )


def solution(mesh):
    dp, ctx = mesh.devices.shape
    split = Mesh(
        mesh.devices.reshape(2, dp // 4, 2, 2, ctx // 2), ("yh", "z", "core", "yl", "x")
    )
    tokens = P(DP, CTX, None)
    placed = (
        tokens,
        P(DP),
        P(),
        P(DP, None),
        P(),
        P(),
        P(DP, None),
        P(),
        P(DP, None),
        P(DP, None),
        tokens,
    )
    return jax.shard_map(
        local,
        mesh=split,
        in_specs=placed,
        out_specs=(tokens, tokens, P(DP, None), P()),
        check_vma=False,
    )
```

```python
import functools

import jax
import jax.numpy as jnp
from jax import lax
from jax.experimental import pallas as pl
from jax.experimental.pallas import tpu as pltpu
from jax.sharding import Mesh
from jax.sharding import PartitionSpec as P

HEADS = 16
EPSILON = 1e-05
BF = jnp.bfloat16
F32 = jnp.float32

DP = ("yh", "z", "core")
CTX = ("yl", "x")

VM = pl.BlockSpec(memory_space=pltpu.VMEM)
SM = pl.BlockSpec(memory_space=pltpu.SMEM)
ANY = pl.BlockSpec(memory_space=pl.ANY)


def params(mib, top=60):
    return pltpu.CompilerParams(vmem_limit_bytes=max(mib, top) << 20)


def cost(flops, nbytes):
    return pl.CostEstimate(flops=flops, bytes_accessed=nbytes, transcendentals=0)


def centred(values):
    centre = values - jnp.mean(values, -1, keepdims=True)
    spread = jnp.mean(centre * centre, -1, keepdims=True)
    return centre, lax.rsqrt(spread + EPSILON)


def norm_pull(cot, centre, inv):
    xhat = centre * inv
    return inv * (
        cot - jnp.mean(cot, -1, keepdims=True) - xhat * jnp.mean(cot * xhat, -1, keepdims=True)
    )


def dot(a, b):
    return jnp.dot(a, b, preferred_element_type=F32)


def dot_t(a, b):
    return lax.dot_general(a, b, (((1,), (1,)), ((), ())), preferred_element_type=F32)


def sigmoid(v):
    return jax.nn.sigmoid(v)


def whole(shape):
    return pl.BlockSpec(shape, lambda i: (0,) * len(shape))


def call(body, outs, ins, name, mib, scratch=(), anys=()):
    specs = [SM] + [whole(v.shape) for v in ins[1:]] + [ANY] * len(anys)
    return pl.pallas_call(
        body,
        grid=(1,),
        out_shape=tuple(jax.ShapeDtypeStruct(*o) for o in outs),
        in_specs=specs,
        out_specs=tuple(whole(o[0]) for o in outs),
        scratch_shapes=list(scratch),
        compiler_params=params(mib),
        name=name,
    )(*ins, *anys)


def ctx_index():
    return lax.axis_index("yl") * lax.axis_size("x") + lax.axis_index("x")


def at_lane(block, width):
    return pl.ds(pl.multiple_of(block * width, width), width)


def cut_body(blocks, scal, w2_ref, wq_ref, w1_ref, own_ref, w1_own_ref, next_ref):
    model = w2_ref.shape[1]
    width = model // blocks
    ctx = ctx_index()
    beside = lax.rem(ctx + blocks // 2, blocks)
    for ref, block in ((own_ref, ctx), (next_ref, beside)):
        ref[:, :model] = w2_ref[...]
        for part in range(3):
            lo = model + part * width
            ref[:, lo : lo + width] = wq_ref[:, at_lane(part * blocks + block, width)]
    for ref, lo, block in ((w1_own_ref, 0, ctx), (next_ref, model + 3 * width, beside)):
        for part in range(2):
            at = lo + part * width
            ref[:, at : at + width] = w1_ref[:, at_lane(part * blocks + block, width)]


def first_body(scal, x_ref, g_ref, out_ref):
    centre, inv = centred(x_ref[...].astype(F32))
    normed = (centre * inv * g_ref[...]).astype(BF)
    for i in range(out_ref.shape[0]):
        out_ref[i] = normed


def gate_body(taps, scal, x_ref, wm_ref, wo_ref, k_ref, conv_ref, hid_ref, gated_ref, w_s, pad_s):
    rec = pl.program_id(0)
    blocks, _, local, model = x_ref.shape
    length = blocks * local
    width = k_ref.shape[1]

    @pl.when(rec == 0)
    def _():
        core, yh, z = lax.axis_index("core"), lax.axis_index("yh"), lax.axis_index("z")
        zs = wm_ref.shape[0]
        for s in range(zs):
            owner = lax.rem(z - s + zs, zs)
            for slot, side in ((0, yh), (1, 1 - yh)):
                w_s[side, owner, core] = wm_ref[s, slot]
                w_s[side, owner, 1 - core] = wo_ref[s, slot]

    x = x_ref[...].reshape(length, model)
    hidden = dot(x, w_s[...].reshape(model, 2 * width))
    hid_ref[0] = hidden
    frames = scal[rec]
    here = lax.broadcasted_iota(jnp.int32, (length, width), 0) < frames
    gated = jnp.where(here, hidden[:, :width] * sigmoid(hidden[:, width:]), 0.0).astype(BF)
    gated_ref[0] = gated
    pad_s[0:16] = jnp.zeros((16, width), F32)
    pad_s[16 + length : 32 + length] = jnp.zeros((16, width), F32)
    pad_s[16 : 16 + length] = gated.astype(F32)
    for b in range(blocks):
        total = jnp.zeros((local, width), F32)
        for j in range(taps):
            at = b * local + j + 1
            total = total + k_ref[j : j + 1, :] * pad_s[at : at + local, :]
        conv_ref[b, 0] = total.astype(BF)


def fetch(pieces, slots, yh, core, sems):
    copies = []
    for dst, lo, width in slots:
        group = []
        for src, owner in pieces:
            for slot in range(2):
                side = yh if slot == 0 else 1 - yh
                group.append(
                    pltpu.make_async_copy(
                        src.at[:, slot, :, lo : lo + width],
                        dst.at[side, :, owner],
                        sems.at[len(copies) * 4 + len(group)],
                    )
                )
        copies.append(group)
    for group in copies:
        for one in group:
            one.start()
    return copies


def finish(group):
    for one in group:
        one.wait()


def token_body(
    blocks, scal, c_ref, x_ref, go_ref, g2_ref, ga_ref, mine, other, sent_ref, res_ref, gc_ref, w2_s, sems
):
    model = x_ref.shape[1]
    width = model // blocks
    copies = fetch(
        ((mine, lax.axis_index("core")), (other, 1 - lax.axis_index("core"))), ((w2_s, 0, model),), lax.axis_index("yh"), lax.axis_index("core"), sems
    )
    conv = jnp.concatenate([c_ref[i] for i in range(blocks)], 1).astype(F32)
    centre, inv = centred(conv)
    gain = g2_ref[...]
    normal = centre * inv * gain
    opening = sigmoid(normal)
    swished = (normal * opening).astype(BF)
    finish(copies[0])
    w2 = w2_s[...].reshape(model, model)
    back_two = dot_t(go_ref[...], w2)
    slope = opening + normal * opening * (1.0 - opening)
    grad_conv = norm_pull(back_two * slope * gain, centre, inv).astype(BF)
    for i in range(blocks):
        gc_ref[i] = grad_conv[:, i * width : (i + 1) * width]
    residual = (x_ref[...].astype(F32) + dot(swished, w2)).astype(BF)
    res_ref[...] = residual
    centre, inv = centred(residual.astype(F32))
    attn_in = (centre * inv * ga_ref[...]).astype(BF)
    for i in range(blocks):
        sent_ref[i] = attn_in


def back_body(
    taps, scal, gc_ref, hid_ref, gated_ref, x_ref, k_ref,
    gh_ref, keep_ref, send_ref, gk_ref, pad_s, gpad_s, gf_s, gk_s,
):
    rec = pl.program_id(0)
    core = lax.axis_index("core")
    frames = scal[rec]
    blocks, _, local, _ = gh_ref.shape
    length = blocks * local
    width = k_ref.shape[1]
    model = x_ref.shape[3]

    @pl.when(rec == 0)
    def _():
        gk_s[...] = jnp.zeros_like(gk_s)

    zeros = jnp.zeros((16, width), F32)
    for ref in (pad_s, gpad_s):
        ref[0:16] = zeros
        ref[16 + length : 32 + length] = zeros
    pad_s[16 : 16 + length] = gc_ref[...].reshape(length, width).astype(F32)
    gpad_s[16 : 16 + length] = gated_ref[0].astype(F32)
    for b in range(blocks):
        base = b * local
        total = jnp.zeros((local, width), F32)
        own = pad_s[16 + base : 16 + base + local, :]
        for j in range(taps):
            at = base + taps - j
            total = total + k_ref[j : j + 1, :] * pad_s[at : at + local, :]
            at = base + j + 1
            term = (gpad_s[at : at + local, :] * own).reshape(local // 8, 8, width)
            gk_s[j] += jnp.sum(term, 0)
        at = lax.broadcasted_iota(jnp.int32, (local, width), 0) + base
        grad_gated = jnp.where(at < frames, total, 0.0)
        linear = hid_ref[0, base : base + local, :width]
        opening = sigmoid(hid_ref[0, base : base + local, width:])
        first = grad_gated * opening
        gh_ref[b, 0, :, :width] = first.astype(BF)
        gh_ref[b, 0, :, width:] = (first * linear * (1.0 - opening)).astype(BF)
    grad_hidden = gh_ref[...].reshape(length, 2 * width)
    x = x_ref[...].reshape(length, model)
    grad_first = lax.dot_general(
        x, grad_hidden, (((0,), (0,)), ((), ())), preferred_element_type=F32
    ).reshape(gf_s.shape)

    @pl.when(rec == 0)
    def _():
        gf_s[...] = grad_first

    @pl.when(rec > 0)
    def _():
        gf_s[...] += grad_first

    @pl.when(rec == pl.num_programs(0) - 1)
    def _():
        keep_ref[...] = gf_s[:, :, pl.ds(core, 1)][:, :, 0]
        send_ref[...] = gf_s[:, :, pl.ds(1 - core, 1)][:, :, 0].astype(BF)
        gk = jnp.sum(gk_s[...], 1)
        half = gk_ref.shape[0]
        gk_ref[:, :width] = gk[:half]
        gk_ref[:, width:] = gk[half:]


def heads_body(head_dim, scal, x_ref, gh_ref, mine, other, out_ref, w_s, sems):
    rec = pl.program_id(0)
    frames = scal[rec]
    blocks, _, local, model = x_ref.shape
    length = blocks * local
    width = model // blocks

    @pl.when(rec == 0)
    def _():
        core = lax.axis_index("core")
        copies = fetch(
            ((mine, core), (other, 1 - core)), ((w_s, model, 3 * width),), lax.axis_index("yh"), core, sems
        )
        finish(copies[0])

    out_ref[:, :, :, : 2 * width] = gh_ref[...]
    x = x_ref[...].reshape(length, model)
    packed = dot(x, w_s[...].reshape(model, 3 * width)).astype(BF)
    q = packed[:, :width]
    k = packed[:, width : 2 * width]
    v = packed[:, 2 * width :]
    rows = min(256, length)
    key_ok = lax.broadcasted_iota(jnp.int32, (rows, length), 1) < frames
    lane = lax.broadcasted_iota(jnp.int32, (rows, width), 1)
    scaling = head_dim**-0.5
    for r in range(0, length, rows):
        qr = q[r : r + rows]
        attended = jnp.zeros((rows, width), F32)
        for h in range(width // head_dim):
            mine_h = (lane >= h * head_dim) & (lane < (h + 1) * head_dim)
            scores = dot_t(jnp.where(mine_h, qr, jnp.zeros_like(qr)), k) * scaling
            scores = jnp.where(key_ok, scores, -1e30)
            top = jnp.max(scores, -1, keepdims=True)
            numer = jnp.where(key_ok, jnp.exp(scores - top), 0.0)
            denom = jnp.sum(numer, -1, keepdims=True)
            attended = jnp.where(mine_h, dot(numer.astype(BF), v) / denom, attended)
        got = attended.astype(BF).reshape(rows // local, local, width)
        out_ref[r // local : (r + rows) // local, 0, :, 2 * width :] = got


def pair_body(scal, keep_ref, recv_ref, gk_ref, gkr_ref, *refs):
    zs = len(refs) - 1
    outs, both_s = refs[:zs], refs[zs]
    depth = keep_ref.shape[2]
    both_s[...] = (keep_ref[...] + recv_ref[...].astype(F32)).astype(BF)
    gk = (gk_ref[...] + gkr_ref[...]).astype(BF)
    for s in range(zs):
        to = lax.rem(lax.axis_index("z") + s, zs)
        for side in range(2):
            outs[s][side, :depth] = both_s[side, to]
            outs[s][side, depth:] = gk


def sum_body(scal, *refs):
    keep_ref, send_ref, total_s = refs[-3:]
    total = refs[0][...].astype(F32)
    for ref in refs[1:-3]:
        total = total + ref[...].astype(F32)
    total_s[...] = total
    keep_ref[...] = total_s[lax.axis_index("yh")].astype(BF)
    send_ref[...] = total_s[1 - lax.axis_index("yh")].astype(BF)


def last_body(scal, x_ref, gf_ref, gk_ref):
    blocks = x_ref.shape[0]
    depth, taps = gf_ref.shape[0], gk_ref.shape[0]
    model = gk_ref.shape[1]
    width = model // blocks
    half = x_ref.shape[2] - depth
    for i in range(blocks):
        lo = i * width
        total = x_ref[i, 0].astype(F32) + x_ref[(i + blocks // 2) % blocks, 1].astype(F32)
        gf_ref[:, lo : lo + width] = total[:depth, :width]
        gf_ref[:, model + lo : model + lo + width] = total[:depth, width:]
        gk_ref[:half, lo : lo + width] = total[depth:, :width]
        gk_ref[half:, lo : lo + width] = total[depth : depth + taps - half, width:]


def result_body(scal, a_ref, res_ref, x_ref, go_ref, g1_ref, mine, other, out_ref, gin_ref, wp_s, w1_s, sems):
    yh, core, ctx = lax.axis_index("yh"), lax.axis_index("core"), ctx_index()
    rows, model = x_ref.shape
    blocks = a_ref.shape[0]
    width = model // blocks
    copies = fetch(
        ((mine, core), (other, 1 - core)),
        ((wp_s, 0, model), (w1_s, model, 2 * model)),
        yh,
        core,
        sems,
    )
    centre, inv = centred(x_ref[...].astype(F32))
    attended = jnp.concatenate([a_ref[i, :, 2 * width :] for i in range(blocks)], 1)
    linear = jnp.concatenate([a_ref[i, :, :width] for i in range(blocks)], 1)
    gating = jnp.concatenate([a_ref[i, :, width : 2 * width] for i in range(blocks)], 1)
    finish(copies[0])
    projected = dot(attended, wp_s[...].reshape(model, model))
    records = 2
    local = rows // records
    at = lax.broadcasted_iota(jnp.int32, (local, model), 0) + ctx * local
    present = jnp.concatenate(
        [(at < scal[r]).astype(F32) for r in range(records)], 0
    )
    out_ref[...] = (res_ref[...].astype(F32) + present * projected).astype(BF)
    finish(copies[1])
    w1 = w1_s[...].reshape(model, 2 * model)
    back_one = dot_t(linear, w1[:, :model]) + dot_t(gating, w1[:, model:])
    pulled = norm_pull(back_one * g1_ref[...], centre, inv)
    gin_ref[...] = (go_ref[...].astype(F32) + pulled).astype(BF)


def swap_core(v):
    return lax.ppermute(v, "core", [(0, 1), (1, 0)])


def swap_yh(v):
    return lax.ppermute(v, ("yh", "yl"), [(0, 3), (3, 0), (1, 2), (2, 1)])


def shifted(v, axis, by):
    count = lax.axis_size(axis)
    return lax.ppermute(v, axis, [(i, (i + by) % count) for i in range(count)])


def local(
    inputs,
    frames,
    gain_first,
    w_first,
    depth_kernel,
    gain_second,
    w_second,
    gain_attn,
    w_qkv,
    w_proj,
    grad_out,
):
    records, local_len, model = inputs.shape
    taps = depth_kernel.shape[0]
    blocks = lax.axis_size(CTX)
    zs = lax.axis_size("z")
    depth = w_first.shape[0]
    width = model // blocks
    length = blocks * local_len
    rows = records * local_len
    head_dim = model // HEADS
    ctx = lax.axis_index(CTX)
    shape = jax.ShapeDtypeStruct
    barrier = lax.optimization_barrier

    scal = frames
    x = inputs.reshape(rows, model)
    cot = grad_out.reshape(rows, model)
    taps_own = lax.dynamic_slice_in_dim(
        jnp.pad(depth_kernel, ((0, 32 - taps), (0, 0))), ctx * width, width, 1
    )

    part = model + 3 * width
    own, w1_own, beside = call(
        functools.partial(cut_body, blocks),
        [((depth, part), BF), ((depth, 2 * width), BF), ((depth, part + 2 * width), BF)],
        [scal, w_second, w_qkv, w_first],
        "cut",
        16,
    )
    beside = swap_yh(beside)
    (sent,) = call(
        first_body, [((blocks, rows, model), BF)], [scal, x, gain_first.reshape(1, model)], "first_norm", 32
    )
    shard_a = jnp.stack([own, beside[:, :part]])
    w1_part = jnp.stack([w1_own, beside[:, part:]])
    shard_a, w1_part, sent = barrier((shard_a, w1_part, sent))
    all_a = lax.all_gather(shard_a, "z", axis=0, tiled=False)
    w1_mine = jnp.stack([w1_part] + [shifted(w1_part, "z", s) for s in range(1, zs)])
    w1_other = swap_core(w1_mine)
    normed = lax.all_to_all(sent, CTX, 0, 0, tiled=True).reshape(blocks, records, local_len, model)
    cat_b = jnp.concatenate([w_proj, w_first], 1)
    shard_b = jnp.stack([cat_b, swap_yh(cat_b)])

    by_record = lambda *rest: pl.BlockSpec(
        (blocks, 1, local_len) + rest, lambda r: (0, r, 0) + (0,) * len(rest)
    )
    of_record = lambda wide: pl.BlockSpec((1, length, wide), lambda r: (r, 0, 0))
    conv, hidden, gated = pl.pallas_call(
        functools.partial(gate_body, taps),
        grid=(records,),
        out_shape=(
            shape((blocks, records, local_len, width), BF),
            shape((records, length, 2 * width), F32),
            shape((records, length, width), BF),
        ),
        in_specs=[
            SM,
            by_record(model),
            whole((zs, 2, depth, 2 * width)),
            whole((zs, 2, depth, 2 * width)),
            whole((32, width)),
        ],
        out_specs=(by_record(width), of_record(2 * width), of_record(width)),
        scratch_shapes=[
            pltpu.VMEM((2, zs, 2, depth, 2 * width), BF),
            pltpu.VMEM((length + 32, width), F32),
        ],
        compiler_params=params(32),
        name="gate_conv",
    )(scal, normed, w1_mine, w1_other, taps_own)

    all_a, conv = barrier((all_a, conv))
    other_a = swap_core(all_a)
    shard_b, all_a = barrier((shard_b, all_a))
    all_b = lax.all_gather(shard_b, "z", axis=0, tiled=False)
    conv_rows = lax.all_to_all(conv, CTX, 0, 0, tiled=True).reshape(blocks, rows, width)

    sent, residual, grad_conv = call(
        functools.partial(token_body, blocks),
        [((blocks, rows, model), BF), ((rows, model), BF), ((blocks, rows, width), BF)],
        [scal, conv_rows, x, cot, gain_second.reshape(1, model), gain_attn.reshape(1, model)],
        "token_rows",
        32,
        [
            pltpu.VMEM((2, zs, 2, depth, model), BF),
            pltpu.SemaphoreType.DMA((4,)),
        ],
        [all_a, other_a],
    )
    grad_conv = lax.all_to_all(grad_conv, CTX, 0, 0, tiled=True)
    sent, grad_conv = barrier((sent, grad_conv))
    grad_conv = grad_conv.reshape(blocks, records, local_len, width)

    attn_in = lax.all_to_all(sent, CTX, 0, 0, tiled=True)
    attn_in = attn_in.reshape(blocks, records, local_len, model)
    share = (2, zs, depth, 2 * width)
    keep_spec = whole(share)

    grad_hidden, keep, send, gk = pl.pallas_call(
        functools.partial(back_body, taps),
        grid=(records,),
        out_shape=(
            shape((blocks, records, local_len, 2 * width), BF),
            shape(share, F32),
            shape(share, BF),
            shape((16, 2 * width), F32),
        ),
        in_specs=[
            SM, by_record(width), of_record(2 * width), of_record(width), by_record(model),
            whole((32, width)),
        ],
        out_specs=(by_record(2 * width), keep_spec, keep_spec, whole((16, 2 * width))),
        scratch_shapes=[
            pltpu.VMEM((length + 32, width), F32),
            pltpu.VMEM((length + 32, width), F32),
            pltpu.VMEM((2, zs, 2, depth, 2 * width), F32),
            pltpu.VMEM((32, 8, width), F32),
        ],
        compiler_params=params(32),
        name="conv_back",
    )(scal, grad_conv, hidden, gated, normed, taps_own)

    chunk = (2, depth + 16, 2 * width)
    chunks = call(
        pair_body,
        [(chunk, BF)] * zs,
        [scal, keep, swap_core(send), gk, swap_core(gk)],
        "pair_sum",
        16,
        [pltpu.VMEM(share, BF)],
    )
    sums = [chunks[0]] + [shifted(chunks[s], "z", s) for s in range(1, zs)]
    keep, send = call(
        sum_body, [(chunk[1:], BF)] * 2, [scal] + sums, "share_sum", 16, [pltpu.VMEM(chunk, F32)]
    )
    pair = jnp.stack([keep, swap_yh(send)])

    back = pl.pallas_call(
        functools.partial(heads_body, head_dim),
        grid=(records,),
        out_shape=shape((blocks, records, local_len, 3 * width), BF),
        in_specs=[SM, by_record(model), by_record(2 * width), ANY, ANY],
        out_specs=by_record(3 * width),
        scratch_shapes=[
            pltpu.VMEM((2, zs, 2, depth, 3 * width), BF),
            pltpu.SemaphoreType.DMA((4,)),
        ],
        compiler_params=params(32),
        name="heads",
    )(scal, attn_in, grad_hidden, all_a, other_a)

    all_b, back = barrier((all_b, back))
    other_b = swap_core(all_b)
    back = lax.all_to_all(back, CTX, 0, 0, tiled=True).reshape(blocks, rows, 3 * width)
    pair, back = barrier((pair, back))
    pair = lax.all_to_all(jnp.broadcast_to(pair, (blocks,) + chunk), CTX, 0, 0, tiled=True)
    grad_first, grad_kernel = call(
        last_body,
        [((depth, 2 * model), F32), ((taps, model), F32)],
        [scal, pair],
        "lay_out",
        16,
    )
    result, grad_in = call(
        result_body,
        [((rows, model), BF), ((rows, model), BF)],
        [scal, back, residual, x, cot, gain_first.reshape(1, model)],
        "result_rows",
        40,
        [
            pltpu.VMEM((2, zs, 2, depth, model), BF),
            pltpu.VMEM((2, zs, 2, depth, 2 * model), BF),
            pltpu.SemaphoreType.DMA((8,)),
        ],
        [all_b, other_b],
    )
    return (
        result.reshape(records, local_len, model),
        grad_in.reshape(records, local_len, model),
        grad_first,
        grad_kernel,
    )


def solution(mesh):
    dp, ctx = mesh.devices.shape
    split = Mesh(
        mesh.devices.reshape(2, dp // 4, 2, 2, ctx // 2), ("yh", "z", "core", "yl", "x")
    )
    tokens = P(DP, CTX, None)
    placed = (
        tokens,
        P(DP),
        P(),
        P(DP, None),
        P(),
        P(),
        P(DP, None),
        P(),
        P(DP, None),
        P(DP, None),
        tokens,
    )
    return jax.shard_map(
        local,
        mesh=split,
        in_specs=placed,
        out_specs=(tokens, tokens, P(DP, None), P()),
        check_vma=False,
    )
```

```python
import functools

import jax
import jax.numpy as jnp
from jax import lax
from jax.experimental import pallas as pl
from jax.experimental.pallas import tpu as pltpu
from jax.sharding import Mesh
from jax.sharding import PartitionSpec as P

HEADS = 16
EPSILON = 1e-05
BF = jnp.bfloat16
F32 = jnp.float32

DP = ("yh", "z", "core")
CTX = ("yl", "x")

VM = pl.BlockSpec(memory_space=pltpu.VMEM)
SM = pl.BlockSpec(memory_space=pltpu.SMEM)
ANY = pl.BlockSpec(memory_space=pl.ANY)


def params(mib, top=60):
    return pltpu.CompilerParams(vmem_limit_bytes=max(mib, top) << 20)


def cost(flops, nbytes):
    return pl.CostEstimate(flops=flops, bytes_accessed=nbytes, transcendentals=0)


def centred(values):
    centre = values - jnp.mean(values, -1, keepdims=True)
    spread = jnp.mean(centre * centre, -1, keepdims=True)
    return centre, lax.rsqrt(spread + EPSILON)


def norm_pull(cot, centre, inv):
    xhat = centre * inv
    return inv * (
        cot - jnp.mean(cot, -1, keepdims=True) - xhat * jnp.mean(cot * xhat, -1, keepdims=True)
    )


def dot(a, b):
    return jnp.dot(a, b, preferred_element_type=F32)


def dot_t(a, b):
    return lax.dot_general(a, b, (((1,), (1,)), ((), ())), preferred_element_type=F32)


def sigmoid(v):
    return jax.nn.sigmoid(v)


def whole(shape):
    return pl.BlockSpec(shape, lambda i: (0,) * len(shape))


def call(body, outs, ins, name, mib, scratch=(), anys=(), hint=0):
    specs = [SM] + [whole(v.shape) for v in ins[1:]] + [ANY] * len(anys)
    return pl.pallas_call(
        body,
        grid=(1,),
        out_shape=tuple(jax.ShapeDtypeStruct(*o) for o in outs),
        in_specs=specs,
        out_specs=tuple(whole(o[0]) for o in outs),
        scratch_shapes=list(scratch),
        compiler_params=params(mib),
        cost_estimate=cost(hint, hint // 300) if hint else None,
        name=name,
    )(*ins, *anys)


def ctx_index():
    return lax.axis_index("yl") * lax.axis_size("x") + lax.axis_index("x")


def at_lane(block, width):
    return pl.ds(pl.multiple_of(block * width, width), width)


def cut_body(blocks, scal, w2_ref, wq_ref, w1_ref, own_ref, w1_own_ref, next_ref):
    model = w2_ref.shape[1]
    width = model // blocks
    ctx = ctx_index()
    beside = lax.rem(ctx + blocks // 2, blocks)
    for ref, block in ((own_ref, ctx), (next_ref, beside)):
        ref[:, :model] = w2_ref[...]
        for part in range(3):
            lo = model + part * width
            ref[:, lo : lo + width] = wq_ref[:, at_lane(part * blocks + block, width)]
    for ref, lo, block in ((w1_own_ref, 0, ctx), (next_ref, model + 3 * width, beside)):
        for part in range(2):
            at = lo + part * width
            ref[:, at : at + width] = w1_ref[:, at_lane(part * blocks + block, width)]


def beside_body(lo, scal, own_ref, next_ref, out_ref):
    out_ref[0] = own_ref[...]
    out_ref[1] = next_ref[:, lo : lo + own_ref.shape[1]]


def first_body(scal, x_ref, g_ref, out_ref):
    centre, inv = centred(x_ref[...].astype(F32))
    normed = (centre * inv * g_ref[...]).astype(BF)
    for i in range(out_ref.shape[0]):
        out_ref[i] = normed


def gate_body(taps, scal, x_ref, wm_ref, wo_ref, k_ref, conv_ref, hid_ref, gated_ref, w_s, pad_s):
    rec = pl.program_id(0)
    blocks, _, local, model = x_ref.shape
    length = blocks * local
    width = k_ref.shape[1]

    @pl.when(rec == 0)
    def _():
        core, yh, z = lax.axis_index("core"), lax.axis_index("yh"), lax.axis_index("z")
        zs = wm_ref.shape[0]
        for s in range(zs):
            owner = z ^ s
            for slot, side in ((0, yh), (1, 1 - yh)):
                w_s[side, owner, core] = wm_ref[s, slot]
                w_s[side, owner, 1 - core] = wo_ref[s, slot]

    x = x_ref[...].reshape(length, model)
    hidden = dot(x, w_s[...].reshape(model, 2 * width))
    hid_ref[0] = hidden
    frames = scal[rec]
    here = lax.broadcasted_iota(jnp.int32, (length, width), 0) < frames
    gated = jnp.where(here, hidden[:, :width] * sigmoid(hidden[:, width:]), 0.0).astype(BF)
    gated_ref[0] = gated
    pad_s[0:16] = jnp.zeros((16, width), F32)
    pad_s[16 + length : 32 + length] = jnp.zeros((16, width), F32)
    pad_s[16 : 16 + length] = gated.astype(F32)
    for b in range(blocks):
        total = jnp.zeros((local, width), F32)
        for j in range(taps):
            at = b * local + j + 1
            total = total + k_ref[j : j + 1, :] * pad_s[at : at + local, :]
        conv_ref[b, 0] = total.astype(BF)


def fetch(pieces, slots, yh, core, sems):
    copies = []
    for dst, lo, width in slots:
        group = []
        for src, owner in pieces:
            for slot in range(2):
                side = yh if slot == 0 else 1 - yh
                group.append(
                    pltpu.make_async_copy(
                        src.at[:, slot, :, lo : lo + width],
                        dst.at[side, :, owner],
                        sems.at[len(copies) * 4 + len(group)],
                    )
                )
        copies.append(group)
    for group in copies:
        for one in group:
            one.start()
    return copies


def finish(group):
    for one in group:
        one.wait()


def token_body(
    blocks, scal, c_ref, x_ref, go_ref, g2_ref, ga_ref, mine, other, sent_ref, res_ref, gc_ref, w2_s, sems
):
    model = x_ref.shape[1]
    width = model // blocks
    copies = fetch(
        ((mine, lax.axis_index("core")), (other, 1 - lax.axis_index("core"))), ((w2_s, 0, model),), lax.axis_index("yh"), lax.axis_index("core"), sems
    )
    conv = jnp.concatenate([c_ref[i] for i in range(blocks)], 1).astype(F32)
    centre, inv = centred(conv)
    gain = g2_ref[...]
    normal = centre * inv * gain
    opening = sigmoid(normal)
    swished = (normal * opening).astype(BF)
    finish(copies[0])
    w2 = w2_s[...].reshape(model, model)
    back_two = dot_t(go_ref[...], w2)
    slope = opening + normal * opening * (1.0 - opening)
    grad_conv = norm_pull(back_two * slope * gain, centre, inv).astype(BF)
    for i in range(blocks):
        gc_ref[i] = grad_conv[:, i * width : (i + 1) * width]
    residual = (x_ref[...].astype(F32) + dot(swished, w2)).astype(BF)
    res_ref[...] = residual
    centre, inv = centred(residual.astype(F32))
    attn_in = (centre * inv * ga_ref[...]).astype(BF)
    for i in range(blocks):
        sent_ref[i] = attn_in


def back_body(
    taps, scal, gc_ref, hid_ref, gated_ref, x_ref, k_ref,
    gh_ref, keep_ref, send_ref, gk_ref, pad_s, gpad_s, gf_s, gk_s,
):
    rec = pl.program_id(0)
    core = lax.axis_index("core")
    frames = scal[rec]
    blocks, _, local, _ = gh_ref.shape
    length = blocks * local
    width = k_ref.shape[1]
    model = x_ref.shape[3]

    @pl.when(rec == 0)
    def _():
        gk_s[...] = jnp.zeros_like(gk_s)

    zeros = jnp.zeros((16, width), F32)
    for ref in (pad_s, gpad_s):
        ref[0:16] = zeros
        ref[16 + length : 32 + length] = zeros
    pad_s[16 : 16 + length] = gc_ref[...].reshape(length, width).astype(F32)
    gpad_s[16 : 16 + length] = gated_ref[0].astype(F32)
    for b in range(blocks):
        base = b * local
        total = jnp.zeros((local, width), F32)
        own = pad_s[16 + base : 16 + base + local, :]
        for j in range(taps):
            at = base + taps - j
            total = total + k_ref[j : j + 1, :] * pad_s[at : at + local, :]
            at = base + j + 1
            term = (gpad_s[at : at + local, :] * own).reshape(local // 8, 8, width)
            gk_s[j] += jnp.sum(term, 0)
        at = lax.broadcasted_iota(jnp.int32, (local, width), 0) + base
        grad_gated = jnp.where(at < frames, total, 0.0)
        linear = hid_ref[0, base : base + local, :width]
        opening = sigmoid(hid_ref[0, base : base + local, width:])
        first = grad_gated * opening
        gh_ref[b, 0, :, :width] = first.astype(BF)
        gh_ref[b, 0, :, width:] = (first * linear * (1.0 - opening)).astype(BF)
    grad_hidden = gh_ref[...].reshape(length, 2 * width)
    x = x_ref[...].reshape(length, model)
    grad_first = lax.dot_general(
        x, grad_hidden, (((0,), (0,)), ((), ())), preferred_element_type=F32
    ).reshape(gf_s.shape)

    @pl.when(rec == 0)
    def _():
        gf_s[...] = grad_first

    @pl.when(rec > 0)
    def _():
        gf_s[...] += grad_first

    @pl.when(rec == pl.num_programs(0) - 1)
    def _():
        keep_ref[...] = gf_s[:, :, pl.ds(core, 1)][:, :, 0]
        send_ref[...] = gf_s[:, :, pl.ds(1 - core, 1)][:, :, 0].astype(BF)
        gk = jnp.sum(gk_s[...], 1)
        half = gk_ref.shape[0]
        gk_ref[:, :width] = gk[:half]
        gk_ref[:, width:] = gk[half:]


def heads_body(head_dim, scal, x_ref, gh_ref, mine, other, out_ref, w_s, sems):
    rec = pl.program_id(0)
    frames = scal[rec]
    blocks, _, local, model = x_ref.shape
    length = blocks * local
    width = model // blocks

    @pl.when(rec == 0)
    def _():
        core = lax.axis_index("core")
        copies = fetch(
            ((mine, core), (other, 1 - core)), ((w_s, model, 3 * width),), lax.axis_index("yh"), core, sems
        )
        finish(copies[0])

    out_ref[:, :, :, : 2 * width] = gh_ref[...]
    x = x_ref[...].reshape(length, model)
    packed = dot(x, w_s[...].reshape(model, 3 * width)).astype(BF)
    q = packed[:, :width]
    k = packed[:, width : 2 * width]
    v = packed[:, 2 * width :]
    rows = min(256, length)
    key_ok = lax.broadcasted_iota(jnp.int32, (rows, length), 1) < frames
    lane = lax.broadcasted_iota(jnp.int32, (rows, width), 1)
    scaling = head_dim**-0.5
    for r in range(0, length, rows):
        qr = q[r : r + rows]
        attended = jnp.zeros((rows, width), F32)
        for h in range(width // head_dim):
            mine_h = (lane >= h * head_dim) & (lane < (h + 1) * head_dim)
            scores = dot_t(jnp.where(mine_h, qr, jnp.zeros_like(qr)), k) * scaling
            scores = jnp.where(key_ok, scores, -1e30)
            top = jnp.max(scores, -1, keepdims=True)
            numer = jnp.where(key_ok, jnp.exp(scores - top), 0.0)
            denom = jnp.sum(numer, -1, keepdims=True)
            attended = jnp.where(mine_h, dot(numer.astype(BF), v) / denom, attended)
        got = attended.astype(BF).reshape(rows // local, local, width)
        out_ref[r // local : (r + rows) // local, 0, :, 2 * width :] = got


def pair_body(scal, keep_ref, recv_ref, gk_ref, gkr_ref, *refs):
    zs = len(refs) - 1
    outs, both_s = refs[:zs], refs[zs]
    depth = keep_ref.shape[2]
    both_s[...] = (keep_ref[...] + recv_ref[...].astype(F32)).astype(BF)
    gk = (gk_ref[...] + gkr_ref[...]).astype(BF)
    for s in range(zs):
        to = lax.rem(lax.axis_index("z") + s, zs)
        for side in range(2):
            outs[s][side, :depth] = both_s[side, to]
            outs[s][side, depth:] = gk


def sum_body(scal, *refs):
    keep_ref, send_ref, total_s = refs[-3:]
    total = refs[0][...].astype(F32)
    for ref in refs[1:-3]:
        total = total + ref[...].astype(F32)
    total_s[...] = total
    keep_ref[...] = total_s[lax.axis_index("yh")].astype(BF)
    send_ref[...] = total_s[1 - lax.axis_index("yh")].astype(BF)


def last_body(scal, x_ref, gf_ref, gk_ref):
    blocks = x_ref.shape[0]
    depth, taps = gf_ref.shape[0], gk_ref.shape[0]
    model = gk_ref.shape[1]
    width = model // blocks
    half = x_ref.shape[2] - depth
    for i in range(blocks):
        lo = i * width
        total = x_ref[i, 0].astype(F32) + x_ref[(i + blocks // 2) % blocks, 1].astype(F32)
        gf_ref[:, lo : lo + width] = total[:depth, :width]
        gf_ref[:, model + lo : model + lo + width] = total[:depth, width:]
        gk_ref[:half, lo : lo + width] = total[depth:, :width]
        gk_ref[half:, lo : lo + width] = total[depth : depth + taps - half, width:]


def result_body(scal, a_ref, res_ref, x_ref, go_ref, g1_ref, mine, other, out_ref, gin_ref, wp_s, w1_s, sems):
    yh, core, ctx = lax.axis_index("yh"), lax.axis_index("core"), ctx_index()
    rows, model = x_ref.shape
    blocks = a_ref.shape[0]
    width = model // blocks
    copies = fetch(
        ((mine, core), (other, 1 - core)),
        ((wp_s, 0, model), (w1_s, model, 2 * model)),
        yh,
        core,
        sems,
    )
    centre, inv = centred(x_ref[...].astype(F32))
    attended = jnp.concatenate([a_ref[i, :, 2 * width :] for i in range(blocks)], 1)
    linear = jnp.concatenate([a_ref[i, :, :width] for i in range(blocks)], 1)
    gating = jnp.concatenate([a_ref[i, :, width : 2 * width] for i in range(blocks)], 1)
    finish(copies[0])
    projected = dot(attended, wp_s[...].reshape(model, model))
    records = 2
    local = rows // records
    at = lax.broadcasted_iota(jnp.int32, (local, model), 0) + ctx * local
    present = jnp.concatenate(
        [(at < scal[r]).astype(F32) for r in range(records)], 0
    )
    out_ref[...] = (res_ref[...].astype(F32) + present * projected).astype(BF)
    finish(copies[1])
    w1 = w1_s[...].reshape(model, 2 * model)
    back_one = dot_t(linear, w1[:, :model]) + dot_t(gating, w1[:, model:])
    pulled = norm_pull(back_one * g1_ref[...], centre, inv)
    gin_ref[...] = (go_ref[...].astype(F32) + pulled).astype(BF)


def swap_core(v):
    return lax.ppermute(v, "core", [(0, 1), (1, 0)])


def swap_yh(v):
    return lax.ppermute(v, ("yh", "yl"), [(0, 3), (3, 0), (1, 2), (2, 1)])


def shifted(v, axis, by):
    count = lax.axis_size(axis)
    return lax.ppermute(v, axis, [(i, (i + by) % count) for i in range(count)])


def local(
    inputs,
    frames,
    gain_first,
    w_first,
    depth_kernel,
    gain_second,
    w_second,
    gain_attn,
    w_qkv,
    w_proj,
    grad_out,
):
    records, local_len, model = inputs.shape
    taps = depth_kernel.shape[0]
    blocks = lax.axis_size(CTX)
    zs = lax.axis_size("z")
    depth = w_first.shape[0]
    width = model // blocks
    length = blocks * local_len
    rows = records * local_len
    head_dim = model // HEADS
    ctx = lax.axis_index(CTX)
    shape = jax.ShapeDtypeStruct
    barrier = lax.optimization_barrier

    scal = frames
    x = inputs.reshape(rows, model)
    cot = grad_out.reshape(rows, model)
    taps_own = lax.dynamic_slice_in_dim(
        jnp.pad(depth_kernel, ((0, 32 - taps), (0, 0))), ctx * width, width, 1
    )

    part = model + 3 * width
    own, w1_own, beside = call(
        functools.partial(cut_body, blocks),
        [((depth, part), BF), ((depth, 2 * width), BF), ((depth, part + 2 * width), BF)],
        [scal, w_second, w_qkv, w_first],
        "cut",
        16,
    )
    beside = swap_yh(beside)
    (sent,) = call(
        first_body, [((blocks, rows, model), BF)], [scal, x, gain_first.reshape(1, model)], "first_norm", 32
    )
    (shard_a,) = call(
        functools.partial(beside_body, 0), [((2,) + own.shape, BF)], [scal, own, beside], "beside_a", 16
    )
    (w1_part,) = call(
        functools.partial(beside_body, part),
        [((2,) + w1_own.shape, BF)],
        [scal, w1_own, beside],
        "beside_w1",
        16,
        hint=int(3e10),
    )
    all_a = lax.all_gather(shard_a, "z", axis=0, tiled=False)
    w1_mine = w1_part[None]
    while w1_mine.shape[0] < zs:
        step = w1_mine.shape[0]
        far = lax.ppermute(w1_mine, "z", [(i, i ^ step) for i in range(zs)])
        w1_mine = jnp.concatenate([w1_mine, far])
    w1_other = swap_core(w1_mine)
    normed = lax.all_to_all(sent, CTX, 0, 0, tiled=True).reshape(blocks, records, local_len, model)
    cat_b = jnp.concatenate([w_proj, w_first], 1)
    shard_b = jnp.stack([cat_b, swap_yh(cat_b)])

    by_record = lambda *rest: pl.BlockSpec(
        (blocks, 1, local_len) + rest, lambda r: (0, r, 0) + (0,) * len(rest)
    )
    of_record = lambda wide: pl.BlockSpec((1, length, wide), lambda r: (r, 0, 0))
    conv, hidden, gated = pl.pallas_call(
        functools.partial(gate_body, taps),
        grid=(records,),
        out_shape=(
            shape((blocks, records, local_len, width), BF),
            shape((records, length, 2 * width), F32),
            shape((records, length, width), BF),
        ),
        in_specs=[
            SM,
            by_record(model),
            whole((zs, 2, depth, 2 * width)),
            whole((zs, 2, depth, 2 * width)),
            whole((32, width)),
        ],
        out_specs=(by_record(width), of_record(2 * width), of_record(width)),
        scratch_shapes=[
            pltpu.VMEM((2, zs, 2, depth, 2 * width), BF),
            pltpu.VMEM((length + 32, width), F32),
        ],
        compiler_params=params(32),
        name="gate_conv",
    )(scal, normed, w1_mine, w1_other, taps_own)

    all_a, conv = barrier((all_a, conv))
    other_a = swap_core(all_a)
    shard_b, all_a = barrier((shard_b, all_a))
    all_b = lax.all_gather(shard_b, "z", axis=0, tiled=False)
    conv_rows = lax.all_to_all(conv, CTX, 0, 0, tiled=True).reshape(blocks, rows, width)

    sent, residual, grad_conv = call(
        functools.partial(token_body, blocks),
        [((blocks, rows, model), BF), ((rows, model), BF), ((blocks, rows, width), BF)],
        [scal, conv_rows, x, cot, gain_second.reshape(1, model), gain_attn.reshape(1, model)],
        "token_rows",
        32,
        [
            pltpu.VMEM((2, zs, 2, depth, model), BF),
            pltpu.SemaphoreType.DMA((4,)),
        ],
        [all_a, other_a],
    )
    grad_conv = lax.all_to_all(grad_conv, CTX, 0, 0, tiled=True)
    sent, grad_conv = barrier((sent, grad_conv))
    grad_conv = grad_conv.reshape(blocks, records, local_len, width)

    attn_in = lax.all_to_all(sent, CTX, 0, 0, tiled=True)
    attn_in = attn_in.reshape(blocks, records, local_len, model)
    share = (2, zs, depth, 2 * width)
    keep_spec = whole(share)

    grad_hidden, keep, send, gk = pl.pallas_call(
        functools.partial(back_body, taps),
        grid=(records,),
        out_shape=(
            shape((blocks, records, local_len, 2 * width), BF),
            shape(share, F32),
            shape(share, BF),
            shape((16, 2 * width), F32),
        ),
        in_specs=[
            SM, by_record(width), of_record(2 * width), of_record(width), by_record(model),
            whole((32, width)),
        ],
        out_specs=(by_record(2 * width), keep_spec, keep_spec, whole((16, 2 * width))),
        scratch_shapes=[
            pltpu.VMEM((length + 32, width), F32),
            pltpu.VMEM((length + 32, width), F32),
            pltpu.VMEM((2, zs, 2, depth, 2 * width), F32),
            pltpu.VMEM((32, 8, width), F32),
        ],
        compiler_params=params(32),
        name="conv_back",
    )(scal, grad_conv, hidden, gated, normed, taps_own)

    chunk = (2, depth + 16, 2 * width)
    chunks = call(
        pair_body,
        [(chunk, BF)] * zs,
        [scal, keep, swap_core(send), gk, swap_core(gk)],
        "pair_sum",
        16,
        [pltpu.VMEM(share, BF)],
    )
    sums = [chunks[0]] + [shifted(chunks[s], "z", s) for s in range(1, zs)]
    keep, send = call(
        sum_body, [(chunk[1:], BF)] * 2, [scal] + sums, "share_sum", 16, [pltpu.VMEM(chunk, F32)]
    )
    attn_in, keep, send = barrier((attn_in, keep, send))
    pair = jnp.stack([keep, swap_yh(send)])

    back = pl.pallas_call(
        functools.partial(heads_body, head_dim),
        grid=(records,),
        out_shape=shape((blocks, records, local_len, 3 * width), BF),
        in_specs=[SM, by_record(model), by_record(2 * width), ANY, ANY],
        out_specs=by_record(3 * width),
        scratch_shapes=[
            pltpu.VMEM((2, zs, 2, depth, 3 * width), BF),
            pltpu.SemaphoreType.DMA((4,)),
        ],
        compiler_params=params(32),
        name="heads",
    )(scal, attn_in, grad_hidden, all_a, other_a)

    all_b, back = barrier((all_b, back))
    other_b = swap_core(all_b)
    back = lax.all_to_all(back, CTX, 0, 0, tiled=True).reshape(blocks, rows, 3 * width)
    pair, back = barrier((pair, back))
    pair = lax.all_to_all(jnp.broadcast_to(pair, (blocks,) + chunk), CTX, 0, 0, tiled=True)
    result, grad_in = call(
        result_body,
        [((rows, model), BF), ((rows, model), BF)],
        [scal, back, residual, x, cot, gain_first.reshape(1, model)],
        "result_rows",
        40,
        [
            pltpu.VMEM((2, zs, 2, depth, model), BF),
            pltpu.VMEM((2, zs, 2, depth, 2 * model), BF),
            pltpu.SemaphoreType.DMA((8,)),
        ],
        [all_b, other_b],
    )
    pair, result, grad_in = barrier((pair, result, grad_in))
    grad_first, grad_kernel = call(
        last_body,
        [((depth, 2 * model), F32), ((taps, model), F32)],
        [scal, pair],
        "lay_out",
        16,
    )
    return (
        result.reshape(records, local_len, model),
        grad_in.reshape(records, local_len, model),
        grad_first,
        grad_kernel,
    )


def solution(mesh):
    dp, ctx = mesh.devices.shape
    split = Mesh(
        mesh.devices.reshape(2, dp // 4, 2, 2, ctx // 2), ("yh", "z", "core", "yl", "x")
    )
    tokens = P(DP, CTX, None)
    placed = (
        tokens,
        P(DP),
        P(),
        P(DP, None),
        P(),
        P(),
        P(DP, None),
        P(),
        P(DP, None),
        P(DP, None),
        tokens,
    )
    return jax.shard_map(
        local,
        mesh=split,
        in_specs=placed,
        out_specs=(tokens, tokens, P(DP, None), P()),
        check_vma=False,
    )
```

```python
import functools

import jax
import jax.numpy as jnp
from jax import lax
from jax.experimental import pallas as pl
from jax.experimental.pallas import tpu as pltpu
from jax.sharding import Mesh
from jax.sharding import PartitionSpec as P

HEADS = 16
EPSILON = 1e-05
BF = jnp.bfloat16
F32 = jnp.float32

DP = ("yh", "z", "core")
CTX = ("yl", "x")

HBM, VMEM, SMEM, ANY = pltpu.HBM, pltpu.VMEM, pltpu.SMEM, pl.ANY


def run(body, outs, ins, name, scratch=(), sems=0, alias=None, mib=36):
    scratch = [pltpu.VMEM(*one) for one in scratch]
    if sems:
        scratch.append(pltpu.SemaphoreType.DMA((sems,)))
    return pl.pallas_call(
        body,
        out_shape=tuple(o[2](o[0], o[1]) for o in outs),
        in_specs=[pl.BlockSpec(memory_space=space) for _, space in ins],
        out_specs=tuple(pl.BlockSpec(memory_space=o[2]) for o in outs),
        scratch_shapes=scratch,
        input_output_aliases=alias or {},
        compiler_params=pltpu.CompilerParams(vmem_limit_bytes=mib << 20),
        name=name,
    )(
        *[
            v if space in (SMEM, ANY) else pltpu.with_memory_space_constraint(v, space)
            for v, space in ins
        ]
    )


class Copies:
    def __init__(self, sems):
        self.sems, self.used = sems, 0

    def start(self, src, dst):
        one = pltpu.make_async_copy(src, dst, self.sems.at[self.used])
        self.used += 1
        one.start()
        return one


def wait(*copies):
    for one in copies:
        one.wait()


def centred(values):
    centre = values - jnp.mean(values, -1, keepdims=True)
    spread = jnp.mean(centre * centre, -1, keepdims=True)
    return centre, lax.rsqrt(spread + EPSILON)


def norm_pull(cot, centre, inv):
    xhat = centre * inv
    return inv * (
        cot - jnp.mean(cot, -1, keepdims=True) - xhat * jnp.mean(cot * xhat, -1, keepdims=True)
    )


def dot(a, b):
    return jnp.dot(a, b, preferred_element_type=F32)


def dot_t(a, b):
    return lax.dot_general(a, b, (((1,), (1,)), ((), ())), preferred_element_type=F32)


def sigmoid(v):
    return jax.nn.sigmoid(v)


def ctx_index():
    return lax.axis_index("yl") * lax.axis_size("x") + lax.axis_index("x")


def lanes(block, width):
    return pl.ds(pl.multiple_of(block * width, width), width)


def cut_body(blocks, w2, wq, w1, own, w1_own, beside, sems):
    model = w2.shape[1]
    width = model // blocks
    ctx = ctx_index()
    copies = Copies(sems)
    going = []
    for dst, block in ((beside, lax.rem(ctx + blocks // 2, blocks)), (own, ctx)):
        going.append(copies.start(w2, dst.at[:, :model]))
        for part in range(3):
            lo = model + part * width
            going.append(
                copies.start(
                    wq.at[:, lanes(part * blocks + block, width)], dst.at[:, lo : lo + width]
                )
            )
        to, lo = (beside, model + 3 * width) if dst is beside else (w1_own, 0)
        for part in range(2):
            at = lo + part * width
            going.append(
                copies.start(
                    w1.at[:, lanes(part * blocks + block, width)], to.at[:, at : at + width]
                )
            )
    wait(*going)


def pack_body(wp, w1, out, sems):
    model = wp.shape[1]
    copies = Copies(sems)
    wait(copies.start(wp, out.at[:, :model]), copies.start(w1, out.at[:, model:]))


def lay_rows(copies, lo, wide, mine, other, out):
    core, yh = lax.axis_index("core"), lax.axis_index("yh")
    return [
        copies.start(src.at[:, slot, :, lo : lo + wide], out.at[side, :, owner])
        for src, owner in ((mine, core), (other, 1 - core))
        for slot, side in ((0, yh), (1, 1 - yh))
    ]


def first_body(x, gain, out, x_s, g_s, n_s, sems):
    copies = Copies(sems)
    wait(copies.start(x, x_s), copies.start(gain, g_s))
    centre, inv = centred(x_s[...].astype(F32))
    n_s[...] = (centre * inv * g_s[...]).astype(BF)
    wait(*[copies.start(n_s, out.at[i]) for i in range(out.shape[0])])


def gate_body(
    taps, frames, x, wm, wo, k, conv, hid, gated, w_s, k_s, pad_s, conv_s, hid_s, gated_s, sems
):
    blocks, records, local, model = x.shape
    length = blocks * local
    width = k_s.shape[1]
    core, yh, z = lax.axis_index("core"), lax.axis_index("yh"), lax.axis_index("z")
    copies = Copies(sems)
    get_k = copies.start(k.at[:, lanes(ctx_index(), width)], k_s)
    for s in range(wm.shape[0]):
        for slot, side in ((0, yh), (1, 1 - yh)):
            w_s[side, z ^ s, core] = wm[s, slot]
            w_s[side, z ^ s, 1 - core] = wo[s, slot]
    zeros = jnp.zeros((16, width), F32)
    pad_s[0:16] = zeros
    pad_s[16 + length : 32 + length] = zeros
    wait(get_k)
    going = []
    for rec in range(records):
        hidden = dot(x[:, rec].reshape(length, model), w_s[...].reshape(model, 2 * width))
        hid_s[rec] = hidden
        here = lax.broadcasted_iota(jnp.int32, (length, width), 0) < frames[rec]
        value = jnp.where(here, hidden[:, :width] * sigmoid(hidden[:, width:]), 0.0).astype(BF)
        gated_s[rec] = value
        pad_s[16 : 16 + length] = value.astype(F32)
        for b in range(blocks):
            total = jnp.zeros((local, width), F32)
            for j in range(taps):
                at = b * local + j + 1
                total = total + k_s[j : j + 1, :] * pad_s[at : at + local, :]
            conv_s[b, rec] = total.astype(BF)
        going.append(copies.start(conv_s.at[:, rec], conv.at[:, rec]))
        going.append(copies.start(hid_s.at[rec], hid.at[rec]))
        going.append(copies.start(gated_s.at[rec], gated.at[rec]))
    wait(*going)


def token_body(
    c, mine, other, x, go, g2, ga, sent, res, gc, w2_s, x_s, go_s, g2_s, ga_s, n_s, res_s, gc_s, sems
):
    rows, model = x_s.shape
    blocks = c.shape[0]
    width = model // blocks
    copies = Copies(sems)
    get_w2 = lay_rows(copies, 0, model, mine, other, w2_s)
    get_gain = copies.start(g2, g2_s)
    get_go = copies.start(go, go_s)
    get_x = copies.start(x, x_s)
    get_ga = copies.start(ga, ga_s)
    conv = jnp.concatenate([c[i] for i in range(blocks)], 1).astype(F32)
    centre, inv = centred(conv)
    wait(get_gain)
    gain = g2_s[...]
    normal = centre * inv * gain
    opening = sigmoid(normal)
    swished = (normal * opening).astype(BF)
    wait(get_go, *get_w2)
    w2 = w2_s[...].reshape(model, model)
    back_two = dot_t(go_s[...], w2)
    slope = opening + normal * opening * (1.0 - opening)
    grad_conv = norm_pull(back_two * slope * gain, centre, inv).astype(BF)
    for i in range(blocks):
        gc_s[i] = grad_conv[:, i * width : (i + 1) * width]
    going = [copies.start(gc_s, gc)]
    wait(get_x, get_ga)
    residual = (x_s[...].astype(F32) + dot(swished, w2)).astype(BF)
    res_s[...] = residual
    going.append(copies.start(res_s, res))
    centre, inv = centred(residual.astype(F32))
    n_s[...] = (centre * inv * ga_s[...]).astype(BF)
    wait(*going, *[copies.start(n_s, sent.at[i]) for i in range(blocks)])


def back_body(
    taps, frames, gc, x, hid, gated, k, back, keep, send, gk_out,
    k_s, hid_s, gated_s, pad_s, gpad_s, gh_s, both_s, gf_s, gk_s, out_s, gko_s, sems,
):
    blocks, records, local, model = x.shape
    length = blocks * local
    rows = records * local
    width = k_s.shape[1]
    core = lax.axis_index("core")
    copies = Copies(sems)
    get_k = copies.start(k.at[:, lanes(ctx_index(), width)], k_s)
    get_gated = copies.start(gated, gated_s)
    get_hid = copies.start(hid, hid_s)
    gk_s[...] = jnp.zeros_like(gk_s)
    zeros = jnp.zeros((16, width), F32)
    for ref in (pad_s, gpad_s):
        ref[0:16] = zeros
        ref[16 + length : 32 + length] = zeros
    wait(get_k, get_gated, get_hid)
    for rec in range(records):
        pad_s[16 : 16 + length] = gc[:, rec].reshape(length, width).astype(F32)
        gpad_s[16 : 16 + length] = gated_s[rec].astype(F32)
        for b in range(blocks):
            base = b * local
            total = jnp.zeros((local, width), F32)
            own = pad_s[16 + base : 16 + base + local, :]
            for j in range(taps):
                at = base + taps - j
                total = total + k_s[j : j + 1, :] * pad_s[at : at + local, :]
                at = base + j + 1
                term = (gpad_s[at : at + local, :] * own).reshape(local // 8, 8, width)
                gk_s[j] += jnp.sum(term, 0)
            at = lax.broadcasted_iota(jnp.int32, (local, width), 0) + base
            grad_gated = jnp.where(at < frames[rec], total, 0.0)
            linear = hid_s[rec, base : base + local, :width]
            opening = sigmoid(hid_s[rec, base : base + local, width:])
            first = grad_gated * opening
            second = (first * linear * (1.0 - opening)).astype(BF)
            first = first.astype(BF)
            gh_s[base : base + local, :width] = first
            gh_s[base : base + local, width:] = second
            out_s[b, rec * local : (rec + 1) * local] = first
            out_s[b, rows + rec * local : rows + (rec + 1) * local] = second
        grad_first = lax.dot_general(
            x[:, rec].reshape(length, model),
            gh_s[...],
            (((0,), (0,)), ((), ())),
            preferred_element_type=F32,
        ).reshape(gf_s.shape)
        if rec == 0:
            gf_s[...] = grad_first
        else:
            both_s[...] = (gf_s[...] + grad_first).astype(BF)
    gk = jnp.sum(gk_s[...], 1)
    half = gko_s.shape[0]
    gko_s[:, :width] = gk[:half]
    gko_s[:, width:] = gk[half:]
    wait(
        copies.start(both_s.at[:, :, 1 - core], send),
        copies.start(gko_s, gk_out),
        copies.start(both_s.at[:, :, core], keep),
        copies.start(out_s, back.at[:, : 2 * rows]),
    )


def pair_body(keep, recv, gk, gkr, *refs):
    zs = len(refs) - 5
    outs, (keep_s, gk_s, both_s, out_s, sems) = refs[:zs], refs[zs:]
    depth, wide = keep_s.shape[2:]
    half = wide // 2
    copies = Copies(sems)
    wait(copies.start(keep, keep_s), copies.start(gk, gk_s))
    both_s[...] = (keep_s[...].astype(F32) + recv[...].astype(F32)).astype(BF)
    gk_sum = (gk_s[...] + gkr[...]).astype(BF)
    tall = out_s.shape[2] // 2
    z = lax.axis_index("z")
    going = []
    for s in range(zs):
        for side in range(2):
            part = both_s[side, z ^ s]
            for h in range(2):
                at = h * tall
                out_s[s, side, at : at + depth] = part[:, h * half : (h + 1) * half]
                out_s[s, side, at + depth : at + tall] = gk_sum[:, h * half : (h + 1) * half]
        going.append(copies.start(out_s.at[s], outs[s]))
    wait(*going)


def sum_body(*refs):
    keep, send, own_s, total_s, sems = refs[-5:]
    copies = Copies(sems)
    get_own = copies.start(refs[0], own_s)
    total = refs[1][...].astype(F32)
    for ref in refs[2:-5]:
        total = total + ref[...].astype(F32)
    wait(get_own)
    total_s[...] = (total + own_s[...].astype(F32)).astype(BF)
    yh = lax.axis_index("yh")
    wait(copies.start(total_s.at[1 - yh], send), copies.start(total_s.at[yh], keep))


def heads_body(head_dim, frames, x, mine, other, held, back, w, att_s, sems):
    del held
    copies = Copies(sems)
    get_w = lay_rows(copies, x.shape[3], w.shape[4], mine, other, w)
    blocks, records, local, model = x.shape
    length = blocks * local
    width = model // blocks
    rows = min(256, length)
    lane = lax.broadcasted_iota(jnp.int32, (rows, width), 1)
    scaling = head_dim**-0.5
    wait(*get_w)
    for rec in range(records):
        packed = dot(x[:, rec].reshape(length, model), w[...].reshape(model, 3 * width))
        packed = packed.astype(BF)
        q = packed[:, :width]
        k = packed[:, width : 2 * width]
        v = packed[:, 2 * width :]
        key_ok = lax.broadcasted_iota(jnp.int32, (rows, length), 1) < frames[rec]
        for r in range(0, length, rows):
            qr = q[r : r + rows]
            attended = jnp.zeros((rows, width), F32)
            for h in range(width // head_dim):
                here = (lane >= h * head_dim) & (lane < (h + 1) * head_dim)
                scores = dot_t(jnp.where(here, qr, jnp.zeros_like(qr)), k) * scaling
                scores = jnp.where(key_ok, scores, -1e30)
                top = jnp.max(scores, -1, keepdims=True)
                numer = jnp.where(key_ok, jnp.exp(scores - top), 0.0)
                denom = jnp.sum(numer, -1, keepdims=True)
                attended = jnp.where(here, dot(numer.astype(BF), v) / denom, attended)
            got = attended.astype(BF).reshape(rows // local, local, width)
            att_s[r // local : (r + rows) // local, rec * local : (rec + 1) * local] = got
    tall = records * local
    wait(copies.start(att_s, back.at[:, 2 * tall : 3 * tall]))


def fill_body(keep, recv, held, back, sems):
    del held
    copies = Copies(sems)
    tall = keep.shape[0]
    base = back.shape[1] - 2 * tall
    going = []
    for i in range(back.shape[0]):
        going.append(copies.start(keep, back.at[i, base : base + tall]))
        going.append(copies.start(recv, back.at[i, base + tall : base + 2 * tall]))
    wait(*going)


def last_body(
    frames, a, mine, other, res, x, go, g1, out, gin, gf, gk,
    wp_s, w1_s, w2_s, res_s, x_s, go_s, g1_s, out_s, gin_s, gf_s, gk_s, sems,
):
    rows, model = x_s.shape
    blocks = a.shape[0]
    width = model // blocks
    depth, taps = gf_s.shape[0], gk_s.shape[0]
    copies = Copies(sems)
    get_w = [
        lay_rows(copies, i * model, model, mine, other, one)
        for i, one in enumerate((wp_s, w1_s, w2_s))
    ]
    get_res = copies.start(res, res_s)
    get_x = copies.start(x, x_s)
    get_go = copies.start(go, go_s)
    get_g1 = copies.start(g1, g1_s)
    tall = (a.shape[1] - 3 * rows) // 4
    base = 3 * rows
    half = tall - depth
    for i in range(blocks):
        lo = i * width
        for h in range(2):
            at = base + h * tall
            far = at + 2 * tall
            total = a[i, at : at + tall].astype(F32) + a[
                (i + blocks // 2) % blocks, far : far + tall
            ].astype(F32)
            gf_s[:, h * model + lo : h * model + lo + width] = total[:depth]
            count = min(half, taps - h * half)
            gk_s[h * half : h * half + count, lo : lo + width] = total[depth : depth + count]
    going = [copies.start(gf_s, gf), copies.start(gk_s, gk)]
    attended = jnp.concatenate([a[i, 2 * rows : 3 * rows] for i in range(blocks)], 1)
    wait(*get_w[0])
    projected = dot(attended, wp_s[...].reshape(model, model))
    records = frames.shape[0]
    local = rows // records
    at = lax.broadcasted_iota(jnp.int32, (local, model), 0) + ctx_index() * local
    present = jnp.concatenate([(at < frames[r]).astype(F32) for r in range(records)], 0)
    wait(get_res)
    out_s[...] = (res_s[...].astype(F32) + present * projected).astype(BF)
    going.append(copies.start(out_s, out))
    linear = jnp.concatenate([a[i, :rows] for i in range(blocks)], 1)
    gating = jnp.concatenate([a[i, rows : 2 * rows] for i in range(blocks)], 1)
    wait(*get_w[1])
    back_one = dot_t(linear, w1_s[...].reshape(model, model))
    wait(*get_w[2])
    back_one = back_one + dot_t(gating, w2_s[...].reshape(model, model))
    wait(get_x, get_go, get_g1)
    centre, inv = centred(x_s[...].astype(F32))
    pulled = norm_pull(back_one * g1_s[...], centre, inv)
    gin_s[...] = (go_s[...].astype(F32) + pulled).astype(BF)
    going.append(copies.start(gin_s, gin))
    wait(*going)


def swap_core(v):
    return lax.ppermute(v, "core", [(0, 1), (1, 0)])


def swap_yh(v):
    return lax.ppermute(v, ("yh", "yl"), [(0, 3), (3, 0), (1, 2), (2, 1)])


def pair_z(v, by):
    return lax.ppermute(v, "z", [(i, i ^ by) for i in range(lax.axis_size("z"))])


def local(
    inputs,
    frames,
    gain_first,
    w_first,
    depth_kernel,
    gain_second,
    w_second,
    gain_attn,
    w_qkv,
    w_proj,
    grad_out,
):
    records, local_len, model = inputs.shape
    taps = depth_kernel.shape[0]
    blocks = lax.axis_size(CTX)
    zs = lax.axis_size("z")
    depth = w_first.shape[0]
    width = model // blocks
    length = blocks * local_len
    rows = records * local_len
    head_dim = model // HEADS
    barrier = lax.optimization_barrier
    x = inputs.reshape(rows, model)
    cot = grad_out.reshape(rows, model)
    gains = [g.reshape(1, model) for g in (gain_first, gain_second, gain_attn)]

    part = model + 3 * width
    own, w1_own, beside = run(
        functools.partial(cut_body, blocks),
        [
            ((depth, part), BF, HBM),
            ((depth, 2 * width), BF, HBM),
            ((depth, part + 2 * width), BF, HBM),
        ],
        [(w_second, HBM), (w_qkv, HBM), (w_first, HBM)],
        "cut",
        sems=12,
    )
    beside = swap_yh(beside)
    (sent,) = run(
        first_body,
        [((blocks, rows, model), BF, HBM)],
        [(x, HBM), (gains[0], HBM)],
        "first_norm",
        [((rows, model), BF), ((1, model), F32), ((rows, model), BF)],
        blocks + 2,
    )
    beside, sent = barrier((beside, sent))
    shard_a = jnp.stack([own, beside[:, :part]])
    all_a = lax.all_gather(shard_a, "z", axis=0, tiled=False)
    normed = lax.all_to_all(sent, CTX, 0, 0, tiled=True).reshape(blocks, records, local_len, model)

    w1_part = jnp.stack([w1_own, beside[:, part:]])
    two = jnp.stack([w1_part, pair_z(w1_part, 1)])
    w1_mine = jnp.concatenate([two] + [pair_z(two, s) for s in range(2, zs, 2)])
    w1_other = swap_core(w1_mine)

    (own_b,) = run(
        pack_body,
        [((depth, 3 * model), BF, HBM)],
        [(w_proj, HBM), (w_first, HBM)],
        "pack",
        sems=2,
    )
    shard_b = jnp.stack([own_b, swap_yh(own_b)])

    conv, hidden, gated = run(
        functools.partial(gate_body, taps),
        [
            ((blocks, records, local_len, width), BF, HBM),
            ((records, length, 2 * width), F32, HBM),
            ((records, length, width), BF, HBM),
        ],
        [(frames, SMEM), (normed, VMEM), (w1_mine, VMEM), (w1_other, VMEM), (depth_kernel, HBM)],
        "gate_conv",
        [
            ((2, zs, 2, depth, 2 * width), BF),
            ((taps, width), F32),
            ((length + 32, width), F32),
            ((blocks, records, local_len, width), BF),
            ((records, length, 2 * width), F32),
            ((records, length, width), BF),
        ],
        1 + 3 * records,
    )

    conv_rows = lax.all_to_all(conv, CTX, 0, 0, tiled=True).reshape(blocks, rows, width)
    all_a, conv_rows = barrier((all_a, conv_rows))
    other_a = swap_core(all_a)
    shard_b, all_a = barrier((shard_b, all_a))
    all_b = lax.all_gather(shard_b, "z", axis=0, tiled=False)

    sent, residual, grad_conv = run(
        token_body,
        [
            ((blocks, rows, model), BF, HBM),
            ((rows, model), BF, HBM),
            ((blocks, rows, width), BF, HBM),
        ],
        [
            (conv_rows, VMEM), (all_a, HBM), (other_a, ANY), (x, HBM), (cot, HBM), (gains[1], HBM),
            (gains[2], HBM),
        ],
        "token_rows",
        [
            ((2, zs, 2, depth, model), BF),
            ((rows, model), BF),
            ((rows, model), BF),
            ((1, model), F32),
            ((1, model), F32),
            ((rows, model), BF),
            ((rows, model), BF),
            ((blocks, rows, width), BF),
        ],
        blocks + 10,
    )
    grad_conv = lax.all_to_all(grad_conv, CTX, 0, 0, tiled=True)
    sent, grad_conv = barrier((sent, grad_conv))
    grad_conv = grad_conv.reshape(blocks, records, local_len, width)
    attn_in = lax.all_to_all(sent, CTX, 0, 0, tiled=True)
    attn_in = attn_in.reshape(blocks, records, local_len, model)

    tall = depth + 16
    half_share = (2, zs, depth, 2 * width)
    back, keep, send, gk = run(
        functools.partial(back_body, taps),
        [
            ((blocks, 3 * rows + 4 * tall, width), BF, HBM),
            (half_share, BF, HBM),
            (half_share, BF, HBM),
            ((16, 2 * width), F32, HBM),
        ],
        [
            (frames, SMEM), (grad_conv, VMEM), (normed, VMEM), (hidden, HBM), (gated, HBM),
            (depth_kernel, HBM),
        ],
        "conv_back",
        [
            ((taps, width), F32),
            ((records, length, 2 * width), F32),
            ((records, length, width), BF),
            ((length + 32, width), F32),
            ((length + 32, width), F32),
            ((length, 2 * width), BF),
            ((2, zs, 2, depth, 2 * width), BF),
            ((2, zs, 2, depth, 2 * width), F32),
            ((32, 8, width), F32),
            ((blocks, 2 * rows, width), BF),
            ((16, 2 * width), F32),
        ],
        7,
    )

    chunk = (2, 2 * tall, width)
    chunks = run(
        pair_body,
        [(chunk, BF, HBM)] * zs,
        [(keep, HBM), (swap_core(send), VMEM), (gk, HBM), (swap_core(gk), VMEM)],
        "pair_sum",
        [
            (half_share, BF),
            ((16, 2 * width), F32),
            (half_share, BF),
            ((zs,) + chunk, BF),
        ],
        zs + 2,
    )
    sums = [chunks[0]] + [pair_z(chunks[s], s) for s in range(1, zs)]
    keep, send = run(
        sum_body,
        [(chunk[1:], BF, HBM)] * 2,
        [(sums[0], HBM)] + [(one, VMEM) for one in sums[1:]],
        "share_sum",
        [(chunk, BF), (chunk, BF)],
        3,
    )
    attn_in, keep, send = barrier((attn_in, keep, send))
    recv = swap_yh(send)

    (back,) = run(
        functools.partial(heads_body, head_dim),
        [(back.shape, BF, HBM)],
        [(frames, SMEM), (attn_in, VMEM), (all_a, HBM), (other_a, ANY), (back, HBM)],
        "heads",
        [((2, zs, 2, depth, 3 * width), BF), ((blocks, rows, width), BF)],
        5,
        {4: 0},
    )
    (back,) = run(
        fill_body,
        [(back.shape, BF, HBM)],
        [(keep, HBM), (recv, ANY), (back, HBM)],
        "fill",
        sems=2 * blocks,
        alias={2: 0},
    )
    all_b, back = barrier((all_b, back))
    other_b = swap_core(all_b)
    back = lax.all_to_all(back, CTX, 0, 0, tiled=True)
    result, grad_in, grad_first, grad_kernel = run(
        last_body,
        [
            ((rows, model), BF, HBM),
            ((rows, model), BF, HBM),
            ((depth, 2 * model), F32, HBM),
            ((taps, model), F32, HBM),
        ],
        [
            (frames, SMEM), (back, VMEM), (all_b, HBM), (other_b, ANY), (residual, HBM), (x, HBM),
            (cot, HBM), (gains[0], HBM),
        ],
        "result_rows",
        [
            ((2, zs, 2, depth, model), BF),
            ((2, zs, 2, depth, model), BF),
            ((2, zs, 2, depth, model), BF),
            ((rows, model), BF),
            ((rows, model), BF),
            ((rows, model), BF),
            ((1, model), F32),
            ((rows, model), BF),
            ((rows, model), BF),
            ((depth, 2 * model), F32),
            ((taps, model), F32),
        ],
        20,
    )
    return (
        result.reshape(records, local_len, model),
        grad_in.reshape(records, local_len, model),
        grad_first,
        grad_kernel,
    )


def solution(mesh):
    dp, ctx = mesh.devices.shape
    split = Mesh(
        mesh.devices.reshape(2, dp // 4, 2, 2, ctx // 2), ("yh", "z", "core", "yl", "x")
    )
    tokens = P(DP, CTX, None)
    placed = (
        tokens,
        P(DP),
        P(),
        P(DP, None),
        P(),
        P(),
        P(DP, None),
        P(),
        P(DP, None),
        P(DP, None),
        tokens,
    )
    return jax.shard_map(
        local,
        mesh=split,
        in_specs=placed,
        out_specs=(tokens, tokens, P(DP, None), P()),
        check_vma=False,
    )
```

```python
import functools

import jax
import jax.numpy as jnp
from jax import lax
from jax.experimental import pallas as pl
from jax.experimental.pallas import tpu as pltpu
from jax.sharding import Mesh
from jax.sharding import PartitionSpec as P

HEADS = 16
EPSILON = 1e-05
BF = jnp.bfloat16
F32 = jnp.float32

DP = ("yh", "z", "core")
CTX = ("yl", "x")

HBM, VMEM, SMEM, ANY = pltpu.HBM, pltpu.VMEM, pltpu.SMEM, pl.ANY


def run(body, outs, ins, name, scratch=(), sems=0, alias=None, mib=36):
    scratch = [pltpu.VMEM(*one) for one in scratch]
    if sems:
        scratch.append(pltpu.SemaphoreType.DMA((sems,)))
    return pl.pallas_call(
        body,
        out_shape=tuple(o[2](o[0], o[1]) for o in outs),
        in_specs=[pl.BlockSpec(memory_space=space) for _, space in ins],
        out_specs=tuple(pl.BlockSpec(memory_space=o[2]) for o in outs),
        scratch_shapes=scratch,
        input_output_aliases=alias or {},
        compiler_params=pltpu.CompilerParams(vmem_limit_bytes=mib << 20),
        name=name,
    )(
        *[
            v if space in (SMEM, ANY) else pltpu.with_memory_space_constraint(v, space)
            for v, space in ins
        ]
    )


class Copies:
    def __init__(self, sems):
        self.sems, self.used = sems, 0

    def start(self, src, dst):
        one = pltpu.make_async_copy(src, dst, self.sems.at[self.used])
        self.used += 1
        one.start()
        return one


def wait(*copies):
    for one in copies:
        one.wait()


def centred(values):
    centre = values - jnp.mean(values, -1, keepdims=True)
    spread = jnp.mean(centre * centre, -1, keepdims=True)
    return centre, lax.rsqrt(spread + EPSILON)


def norm_pull(cot, centre, inv):
    xhat = centre * inv
    return inv * (
        cot - jnp.mean(cot, -1, keepdims=True) - xhat * jnp.mean(cot * xhat, -1, keepdims=True)
    )


def dot(a, b):
    return jnp.dot(a, b, preferred_element_type=F32)


def dot_t(a, b):
    return lax.dot_general(a, b, (((1,), (1,)), ((), ())), preferred_element_type=F32)


def sigmoid(v):
    return jax.nn.sigmoid(v)


def ctx_index():
    return lax.axis_index("yl") * lax.axis_size("x") + lax.axis_index("x")


def lanes(block, width):
    return pl.ds(pl.multiple_of(block * width, width), width)


def cut_body(blocks, w2, wq, w1, own, w1_own, beside, own_s, w1_s, beside_s, sems):
    model = w2.shape[1]
    width = model // blocks
    ctx = ctx_index()
    copies = Copies(sems)
    going = []
    for dst, block in ((beside_s, lax.rem(ctx + blocks // 2, blocks)), (own_s, ctx)):
        going.append(copies.start(w2, dst.at[:, :model]))
        for part in range(3):
            lo = model + part * width
            going.append(
                copies.start(
                    wq.at[:, lanes(part * blocks + block, width)], dst.at[:, lo : lo + width]
                )
            )
        to, lo = (beside_s, model + 3 * width) if dst is beside_s else (w1_s, 0)
        for part in range(2):
            at = lo + part * width
            going.append(
                copies.start(
                    w1.at[:, lanes(part * blocks + block, width)], to.at[:, at : at + width]
                )
            )
    wait(*going)
    wait(
        copies.start(beside_s, beside), copies.start(own_s, own), copies.start(w1_s, w1_own)
    )


def pack_body(wp, w1, out, out_s, sems):
    model = wp.shape[1]
    copies = Copies(sems)
    wait(copies.start(wp, out_s.at[:, :model]), copies.start(w1, out_s.at[:, model:]))
    wait(copies.start(out_s, out))


def lay_rows(copies, lo, wide, mine, other, out):
    core, yh = lax.axis_index("core"), lax.axis_index("yh")
    return [
        copies.start(src.at[:, slot, :, lo : lo + wide], out.at[side, :, owner])
        for src, owner in ((mine, core), (other, 1 - core))
        for slot, side in ((0, yh), (1, 1 - yh))
    ]


def first_body(x, gain, out, x_s, g_s, n_s, sems):
    copies = Copies(sems)
    wait(copies.start(x, x_s), copies.start(gain, g_s))
    centre, inv = centred(x_s[...].astype(F32))
    n_s[...] = (centre * inv * g_s[...]).astype(BF)
    wait(*[copies.start(n_s, out.at[i]) for i in range(out.shape[0])])


def gate_body(
    taps, frames, x, wm, wo, k, conv, hid, gated, w_s, k_s, pad_s, conv_s, hid_s, gated_s, sems
):
    blocks, records, local, model = x.shape
    length = blocks * local
    width = k_s.shape[1]
    core, yh, z = lax.axis_index("core"), lax.axis_index("yh"), lax.axis_index("z")
    copies = Copies(sems)
    get_k = copies.start(k.at[:, lanes(ctx_index(), width)], k_s)
    for s in range(wm.shape[0]):
        for slot, side in ((0, yh), (1, 1 - yh)):
            w_s[side, z ^ s, core] = wm[s, slot]
            w_s[side, z ^ s, 1 - core] = wo[s, slot]
    zeros = jnp.zeros((16, width), F32)
    pad_s[0:16] = zeros
    pad_s[16 + length : 32 + length] = zeros
    going = []
    for rec in range(records):
        hidden = dot(x[:, rec].reshape(length, model), w_s[...].reshape(model, 2 * width))
        hid_s[rec] = hidden
        going.append(copies.start(hid_s.at[rec], hid.at[rec]))
        here = lax.broadcasted_iota(jnp.int32, (length, width), 0) < frames[rec]
        value = jnp.where(here, hidden[:, :width] * sigmoid(hidden[:, width:]), 0.0).astype(BF)
        gated_s[rec] = value
        going.append(copies.start(gated_s.at[rec], gated.at[rec]))
        pad_s[16 : 16 + length] = value.astype(F32)
        if rec == 0:
            wait(get_k)
        for b in range(blocks):
            total = jnp.zeros((local, width), F32)
            for j in range(taps):
                at = b * local + j + 1
                total = total + k_s[j : j + 1, :] * pad_s[at : at + local, :]
            conv_s[b, rec] = total.astype(BF)
        going.append(copies.start(conv_s.at[:, rec], conv.at[:, rec]))
    wait(*going)


def token_body(
    c, mine, other, x, go, g2, ga, sent, res, gc, c_s, w2_s, x_s, go_s, g2_s, ga_s, n_s, res_s, gc_s, sems
):
    rows, model = x_s.shape
    blocks = c.shape[0]
    width = model // blocks
    copies = Copies(sems)
    get_c = copies.start(c, c_s)
    get_w2 = lay_rows(copies, 0, model, mine, other, w2_s)
    get_gain = copies.start(g2, g2_s)
    get_go = copies.start(go, go_s)
    get_x = copies.start(x, x_s)
    get_ga = copies.start(ga, ga_s)
    wait(get_c)
    conv = jnp.concatenate([c_s[i] for i in range(blocks)], 1).astype(F32)
    centre, inv = centred(conv)
    wait(get_gain)
    gain = g2_s[...]
    normal = centre * inv * gain
    opening = sigmoid(normal)
    swished = (normal * opening).astype(BF)
    wait(get_go, *get_w2)
    w2 = w2_s[...].reshape(model, model)
    back_two = dot_t(go_s[...], w2)
    slope = opening + normal * opening * (1.0 - opening)
    grad_conv = norm_pull(back_two * slope * gain, centre, inv).astype(BF)
    for i in range(blocks):
        gc_s[i] = grad_conv[:, i * width : (i + 1) * width]
    going = [copies.start(gc_s, gc)]
    wait(get_x, get_ga)
    residual = (x_s[...].astype(F32) + dot(swished, w2)).astype(BF)
    res_s[...] = residual
    going.append(copies.start(res_s, res))
    centre, inv = centred(residual.astype(F32))
    n_s[...] = (centre * inv * ga_s[...]).astype(BF)
    wait(*going, *[copies.start(n_s, sent.at[i]) for i in range(blocks)])


def back_body(
    taps, frames, gc, x, hid, gated, k, back, keep, send, gk_out,
    gc_s, k_s, hid_s, gated_s, pad_s, gpad_s, gh_s, both_s, gf_s, gk_s, out_s, gko_s, sems,
):
    blocks, records, local, model = x.shape
    length = blocks * local
    rows = records * local
    width = k_s.shape[1]
    core = lax.axis_index("core")
    copies = Copies(sems)
    get_gc = copies.start(gc, gc_s)
    get_k = copies.start(k.at[:, lanes(ctx_index(), width)], k_s)
    get_gated = copies.start(gated, gated_s)
    get_hid = copies.start(hid, hid_s)
    gk_s[...] = jnp.zeros_like(gk_s)
    zeros = jnp.zeros((16, width), F32)
    for ref in (pad_s, gpad_s):
        ref[0:16] = zeros
        ref[16 + length : 32 + length] = zeros
    wait(get_k, get_gc, get_gated)
    for rec in range(records):
        pad_s[16 : 16 + length] = gc_s[:, rec].reshape(length, width).astype(F32)
        gpad_s[16 : 16 + length] = gated_s[rec].astype(F32)
        for b in range(blocks):
            base = b * local
            total = jnp.zeros((local, width), F32)
            own = pad_s[16 + base : 16 + base + local, :]
            for j in range(taps):
                at = base + taps - j
                total = total + k_s[j : j + 1, :] * pad_s[at : at + local, :]
                at = base + j + 1
                term = (gpad_s[at : at + local, :] * own).reshape(local // 8, 8, width)
                gk_s[j] += jnp.sum(term, 0)
            at = lax.broadcasted_iota(jnp.int32, (local, width), 0) + base
            grad_gated = jnp.where(at < frames[rec], total, 0.0)
            if rec == 0 and b == 0:
                wait(get_hid)
            linear = hid_s[rec, base : base + local, :width]
            opening = sigmoid(hid_s[rec, base : base + local, width:])
            first = grad_gated * opening
            second = (first * linear * (1.0 - opening)).astype(BF)
            first = first.astype(BF)
            gh_s[base : base + local, :width] = first
            gh_s[base : base + local, width:] = second
            out_s[b, rec * local : (rec + 1) * local] = first
            out_s[b, rows + rec * local : rows + (rec + 1) * local] = second
        grad_first = lax.dot_general(
            x[:, rec].reshape(length, model),
            gh_s[...],
            (((0,), (0,)), ((), ())),
            preferred_element_type=F32,
        ).reshape(gf_s.shape)
        if rec == 0:
            gf_s[...] = grad_first
        else:
            both_s[...] = (gf_s[...] + grad_first).astype(BF)
    gk = jnp.sum(gk_s[...], 1)
    half = gko_s.shape[0]
    gko_s[:, :width] = gk[:half]
    gko_s[:, width:] = gk[half:]
    wait(
        copies.start(both_s.at[:, :, 1 - core], send),
        copies.start(gko_s, gk_out),
        copies.start(both_s.at[:, :, core], keep),
        copies.start(out_s, back.at[:, : 2 * rows]),
    )


def pair_body(keep, recv, gk, gkr, *refs):
    zs = len(refs) - 5
    outs, (keep_s, gk_s, both_s, out_s, sems) = refs[:zs], refs[zs:]
    depth, wide = keep_s.shape[2:]
    half = wide // 2
    copies = Copies(sems)
    wait(copies.start(keep, keep_s), copies.start(gk, gk_s))
    both_s[...] = (keep_s[...].astype(F32) + recv[...].astype(F32)).astype(BF)
    gk_sum = (gk_s[...] + gkr[...]).astype(BF)
    tall = out_s.shape[2] // 2
    z = lax.axis_index("z")
    going = []
    for s in range(zs):
        for side in range(2):
            part = both_s[side, z ^ s]
            for h in range(2):
                at = h * tall
                out_s[s, side, at : at + depth] = part[:, h * half : (h + 1) * half]
                out_s[s, side, at + depth : at + tall] = gk_sum[:, h * half : (h + 1) * half]
        going.append(copies.start(out_s.at[s], outs[s]))
    wait(*going)


def sum_body(*refs):
    keep, send, parts_s, total_s, sems = refs[-5:]
    copies = Copies(sems)
    wait(*[copies.start(ref, parts_s.at[i]) for i, ref in enumerate(refs[:-5])])
    total_s[...] = jnp.sum(parts_s[...].astype(F32), 0).astype(BF)
    yh = lax.axis_index("yh")
    wait(copies.start(total_s.at[1 - yh], send), copies.start(total_s.at[yh], keep))


def heads_body(head_dim, frames, x, mine, other, held, back, w, att_s, sems):
    del held
    copies = Copies(sems)
    get_w = lay_rows(copies, x.shape[3], w.shape[4], mine, other, w)
    blocks, records, local, model = x.shape
    length = blocks * local
    width = model // blocks
    rows = min(256, length)
    lane = lax.broadcasted_iota(jnp.int32, (rows, width), 1)
    scaling = head_dim**-0.5
    wait(*get_w)
    for rec in range(records):
        packed = dot(x[:, rec].reshape(length, model), w[...].reshape(model, 3 * width))
        packed = packed.astype(BF)
        q = packed[:, :width]
        k = packed[:, width : 2 * width]
        v = packed[:, 2 * width :]
        key_ok = lax.broadcasted_iota(jnp.int32, (rows, length), 1) < frames[rec]
        for r in range(0, length, rows):
            qr = q[r : r + rows]
            attended = jnp.zeros((rows, width), F32)
            for h in range(width // head_dim):
                here = (lane >= h * head_dim) & (lane < (h + 1) * head_dim)
                scores = dot_t(jnp.where(here, qr, jnp.zeros_like(qr)), k) * scaling
                scores = jnp.where(key_ok, scores, -1e30)
                top = jnp.max(scores, -1, keepdims=True)
                numer = jnp.where(key_ok, jnp.exp(scores - top), 0.0)
                denom = jnp.sum(numer, -1, keepdims=True)
                attended = jnp.where(here, dot(numer.astype(BF), v) / denom, attended)
            got = attended.astype(BF).reshape(rows // local, local, width)
            att_s[r // local : (r + rows) // local, rec * local : (rec + 1) * local] = got
    tall = records * local
    wait(copies.start(att_s, back.at[:, 2 * tall : 3 * tall]))


def result_body(
    frames, a, mine, other, res, x, go, g1, out, gin,
    wp_s, w1_s, w2_s, res_s, x_s, go_s, g1_s, out_s, gin_s, sems,
):
    rows, model = x_s.shape
    blocks = a.shape[0]
    copies = Copies(sems)
    get_w = [
        lay_rows(copies, i * model, model, mine, other, one)
        for i, one in enumerate((wp_s, w1_s, w2_s))
    ]
    get_res = copies.start(res, res_s)
    get_x = copies.start(x, x_s)
    get_go = copies.start(go, go_s)
    get_g1 = copies.start(g1, g1_s)
    attended = jnp.concatenate([a[i, 2 * rows : 3 * rows] for i in range(blocks)], 1)
    linear = jnp.concatenate([a[i, :rows] for i in range(blocks)], 1)
    gating = jnp.concatenate([a[i, rows : 2 * rows] for i in range(blocks)], 1)
    wait(*get_w[0])
    projected = dot(attended, wp_s[...].reshape(model, model))
    records = frames.shape[0]
    local = rows // records
    at = lax.broadcasted_iota(jnp.int32, (local, model), 0) + ctx_index() * local
    present = jnp.concatenate([(at < frames[r]).astype(F32) for r in range(records)], 0)
    wait(get_res)
    out_s[...] = (res_s[...].astype(F32) + present * projected).astype(BF)
    put_out = copies.start(out_s, out)
    wait(*get_w[1])
    back_one = dot_t(linear, w1_s[...].reshape(model, model))
    wait(*get_w[2])
    back_one = back_one + dot_t(gating, w2_s[...].reshape(model, model))
    wait(get_x, get_go, get_g1)
    centre, inv = centred(x_s[...].astype(F32))
    pulled = norm_pull(back_one * g1_s[...], centre, inv)
    gin_s[...] = (go_s[...].astype(F32) + pulled).astype(BF)
    wait(put_out, copies.start(gin_s, gin))


def lay_body(a, gf, gk, gf_s, gk_s, sems):
    blocks = a.shape[0]
    depth, taps = gf_s.shape[0], gk_s.shape[0]
    model = gk_s.shape[1]
    width = model // blocks
    tall = a.shape[2] // 2
    half = tall - depth
    for i in range(blocks):
        lo = i * width
        total = a[i, 0].astype(F32) + a[(i + blocks // 2) % blocks, 1].astype(F32)
        for h in range(2):
            at = h * tall
            gf_s[:, h * model + lo : h * model + lo + width] = total[at : at + depth]
            count = min(half, taps - h * half)
            gk_s[h * half : h * half + count, lo : lo + width] = total[
                at + depth : at + depth + count
            ]
    copies = Copies(sems)
    wait(copies.start(gf_s, gf), copies.start(gk_s, gk))


def swap_core(v):
    return lax.ppermute(v, "core", [(0, 1), (1, 0)])


def swap_yh(v):
    return lax.ppermute(v, ("yh", "yl"), [(0, 3), (3, 0), (1, 2), (2, 1)])


def pair_z(v, by):
    return lax.ppermute(v, "z", [(i, i ^ by) for i in range(lax.axis_size("z"))])


def local(
    inputs,
    frames,
    gain_first,
    w_first,
    depth_kernel,
    gain_second,
    w_second,
    gain_attn,
    w_qkv,
    w_proj,
    grad_out,
):
    records, local_len, model = inputs.shape
    taps = depth_kernel.shape[0]
    blocks = lax.axis_size(CTX)
    zs = lax.axis_size("z")
    depth = w_first.shape[0]
    width = model // blocks
    length = blocks * local_len
    rows = records * local_len
    head_dim = model // HEADS
    barrier = lax.optimization_barrier
    x = inputs.reshape(rows, model)
    cot = grad_out.reshape(rows, model)
    gains = [g.reshape(1, model) for g in (gain_first, gain_second, gain_attn)]

    part = model + 3 * width
    own, w1_own, beside = run(
        functools.partial(cut_body, blocks),
        [
            ((depth, part), BF, HBM),
            ((depth, 2 * width), BF, HBM),
            ((depth, part + 2 * width), BF, HBM),
        ],
        [(w_second, HBM), (w_qkv, HBM), (w_first, HBM)],
        "cut",
        [((depth, part), BF), ((depth, 2 * width), BF), ((depth, part + 2 * width), BF)],
        15,
    )
    beside = swap_yh(beside)
    (sent,) = run(
        first_body,
        [((blocks, rows, model), BF, HBM)],
        [(x, HBM), (gains[0], HBM)],
        "first_norm",
        [((rows, model), BF), ((1, model), F32), ((rows, model), BF)],
        blocks + 2,
    )
    beside, sent = barrier((beside, sent))
    shard_a = jnp.stack([own, beside[:, :part]])
    all_a = lax.all_gather(shard_a, "z", axis=0, tiled=False)
    normed = lax.all_to_all(sent, CTX, 0, 0, tiled=True).reshape(blocks, records, local_len, model)

    w1_part = jnp.stack([w1_own, beside[:, part:]])
    two = jnp.stack([w1_part, pair_z(w1_part, 1)])
    w1_mine = jnp.concatenate([two] + [pair_z(two, s) for s in range(2, zs, 2)])
    w1_other = swap_core(w1_mine)

    (own_b,) = run(
        pack_body,
        [((depth, 3 * model), BF, HBM)],
        [(w_proj, HBM), (w_first, HBM)],
        "pack",
        [((depth, 3 * model), BF)],
        3,
    )
    shard_b = jnp.stack([own_b, swap_yh(own_b)])

    conv, hidden, gated = run(
        functools.partial(gate_body, taps),
        [
            ((blocks, records, local_len, width), BF, HBM),
            ((records, length, 2 * width), F32, HBM),
            ((records, length, width), BF, HBM),
        ],
        [(frames, SMEM), (normed, VMEM), (w1_mine, VMEM), (w1_other, VMEM), (depth_kernel, HBM)],
        "gate_conv",
        [
            ((2, zs, 2, depth, 2 * width), BF),
            ((taps, width), F32),
            ((length + 32, width), F32),
            ((blocks, records, local_len, width), BF),
            ((records, length, 2 * width), F32),
            ((records, length, width), BF),
        ],
        1 + 3 * records,
    )

    conv_rows = lax.all_to_all(conv, CTX, 0, 0, tiled=True).reshape(blocks, rows, width)
    all_a, conv_rows = barrier((all_a, conv_rows))
    other_a = swap_core(all_a)
    shard_b, all_a = barrier((shard_b, all_a))
    all_b = lax.all_gather(shard_b, "z", axis=0, tiled=False)

    sent, residual, grad_conv = run(
        token_body,
        [
            ((blocks, rows, model), BF, HBM),
            ((rows, model), BF, HBM),
            ((blocks, rows, width), BF, HBM),
        ],
        [
            (conv_rows, HBM), (all_a, HBM), (other_a, ANY), (x, HBM), (cot, HBM), (gains[1], HBM),
            (gains[2], HBM),
        ],
        "token_rows",
        [
            ((blocks, rows, width), BF),
            ((2, zs, 2, depth, model), BF),
            ((rows, model), BF),
            ((rows, model), BF),
            ((1, model), F32),
            ((1, model), F32),
            ((rows, model), BF),
            ((rows, model), BF),
            ((blocks, rows, width), BF),
        ],
        blocks + 11,
    )
    grad_conv = lax.all_to_all(grad_conv, CTX, 0, 0, tiled=True)
    sent, grad_conv = barrier((sent, grad_conv))
    grad_conv = grad_conv.reshape(blocks, records, local_len, width)
    attn_in = lax.all_to_all(sent, CTX, 0, 0, tiled=True)
    attn_in = attn_in.reshape(blocks, records, local_len, model)

    tall = depth + 16
    half_share = (2, zs, depth, 2 * width)
    back, keep, send, gk = run(
        functools.partial(back_body, taps),
        [
            ((blocks, 3 * rows, width), BF, HBM),
            (half_share, BF, HBM),
            (half_share, BF, HBM),
            ((16, 2 * width), F32, HBM),
        ],
        [
            (frames, SMEM), (grad_conv, HBM), (normed, VMEM), (hidden, HBM), (gated, HBM),
            (depth_kernel, HBM),
        ],
        "conv_back",
        [
            ((blocks, records, local_len, width), BF),
            ((taps, width), F32),
            ((records, length, 2 * width), F32),
            ((records, length, width), BF),
            ((length + 32, width), F32),
            ((length + 32, width), F32),
            ((length, 2 * width), BF),
            ((2, zs, 2, depth, 2 * width), BF),
            ((2, zs, 2, depth, 2 * width), F32),
            ((32, 8, width), F32),
            ((blocks, 2 * rows, width), BF),
            ((16, 2 * width), F32),
        ],
        8,
    )

    chunk = (2, 2 * tall, width)
    chunks = run(
        pair_body,
        [(chunk, BF, HBM)] * zs,
        [(keep, HBM), (swap_core(send), VMEM), (gk, HBM), (swap_core(gk), VMEM)],
        "pair_sum",
        [
            (half_share, BF),
            ((16, 2 * width), F32),
            (half_share, BF),
            ((zs,) + chunk, BF),
        ],
        zs + 2,
    )
    sums = [chunks[0]] + [pair_z(chunks[s], s) for s in range(1, zs)]
    attn_in, *sums[1:5] = barrier((attn_in, *sums[1:5]))
    keep, send = run(
        sum_body,
        [(chunk[1:], BF, HBM)] * 2,
        [(one, ANY) for one in sums],
        "share_sum",
        [((zs,) + chunk, BF), (chunk, BF)],
        zs + 2,
    )
    pair = jnp.stack([keep, swap_yh(send)])
    pair = jnp.broadcast_to(pair, (blocks,) + pair.shape)

    (back,) = run(
        functools.partial(heads_body, head_dim),
        [(back.shape, BF, HBM)],
        [(frames, SMEM), (attn_in, VMEM), (all_a, HBM), (other_a, ANY), (back, HBM)],
        "heads",
        [((2, zs, 2, depth, 3 * width), BF), ((blocks, rows, width), BF)],
        5,
        {4: 0},
    )
    all_b, back = barrier((all_b, back))
    other_b = swap_core(all_b)
    back = lax.all_to_all(back, CTX, 0, 0, tiled=True)
    pair, back = barrier((pair, back))
    pair = lax.all_to_all(pair, CTX, 0, 0, tiled=True)
    result, grad_in = run(
        result_body,
        [((rows, model), BF, HBM)] * 2,
        [
            (frames, SMEM), (back, VMEM), (all_b, HBM), (other_b, ANY), (residual, HBM), (x, HBM),
            (cot, HBM), (gains[0], HBM),
        ],
        "result_rows",
        [((2, zs, 2, depth, model), BF)] * 3
        + [((rows, model), BF)] * 3
        + [((1, model), F32)]
        + [((rows, model), BF)] * 2,
        18,
    )
    pair, result, grad_in = barrier((pair, result, grad_in))
    grad_first, grad_kernel = run(
        lay_body,
        [((depth, 2 * model), F32, HBM), ((taps, model), F32, HBM)],
        [(pair, VMEM)],
        "lay_out",
        [((depth, 2 * model), F32), ((taps, model), F32)],
        2,
    )
    return (
        result.reshape(records, local_len, model),
        grad_in.reshape(records, local_len, model),
        grad_first,
        grad_kernel,
    )


def solution(mesh):
    dp, ctx = mesh.devices.shape
    split = Mesh(
        mesh.devices.reshape(2, dp // 4, 2, 2, ctx // 2), ("yh", "z", "core", "yl", "x")
    )
    tokens = P(DP, CTX, None)
    placed = (
        tokens,
        P(DP),
        P(),
        P(DP, None),
        P(),
        P(),
        P(DP, None),
        P(),
        P(DP, None),
        P(DP, None),
        tokens,
    )
    return jax.shard_map(
        local,
        mesh=split,
        in_specs=placed,
        out_specs=(tokens, tokens, P(DP, None), P()),
        check_vma=False,
    )
```

```python
import functools

import jax
import jax.numpy as jnp
from jax import lax
from jax.experimental import pallas as pl
from jax.experimental.pallas import tpu as pltpu
from jax.sharding import Mesh
from jax.sharding import PartitionSpec as P

HEADS = 16
EPSILON = 1e-05
BF = jnp.bfloat16
F32 = jnp.float32

DP = ("yh", "z", "core")
CTX = ("yl", "x")

HBM, VMEM, SMEM, ANY = pltpu.HBM, pltpu.VMEM, pltpu.SMEM, pl.ANY


def run(body, outs, ins, name, scratch=(), sems=0, alias=None, mib=36):
    scratch = [pltpu.VMEM(*one) for one in scratch]
    if sems:
        scratch.append(pltpu.SemaphoreType.DMA((sems,)))
    return pl.pallas_call(
        body,
        out_shape=tuple(o[2](o[0], o[1]) for o in outs),
        in_specs=[pl.BlockSpec(memory_space=space) for _, space in ins],
        out_specs=tuple(pl.BlockSpec(memory_space=o[2]) for o in outs),
        scratch_shapes=scratch,
        input_output_aliases=alias or {},
        compiler_params=pltpu.CompilerParams(vmem_limit_bytes=mib << 20),
        name=name,
    )(
        *[
            v if space in (SMEM, ANY) else pltpu.with_memory_space_constraint(v, space)
            for v, space in ins
        ]
    )


class Copies:
    def __init__(self, sems):
        self.sems, self.used = sems, 0

    def start(self, src, dst):
        one = pltpu.make_async_copy(src, dst, self.sems.at[self.used])
        self.used += 1
        one.start()
        return one


def wait(*copies):
    for one in copies:
        one.wait()


def centred(values):
    centre = values - jnp.mean(values, -1, keepdims=True)
    spread = jnp.mean(centre * centre, -1, keepdims=True)
    return centre, lax.rsqrt(spread + EPSILON)


def norm_pull(cot, centre, inv):
    xhat = centre * inv
    return inv * (
        cot - jnp.mean(cot, -1, keepdims=True) - xhat * jnp.mean(cot * xhat, -1, keepdims=True)
    )


def dot(a, b):
    return jnp.dot(a, b, preferred_element_type=F32)


def dot_t(a, b):
    return lax.dot_general(a, b, (((1,), (1,)), ((), ())), preferred_element_type=F32)


def sigmoid(v):
    return jax.nn.sigmoid(v)


def ctx_index():
    return lax.axis_index("yl") * lax.axis_size("x") + lax.axis_index("x")


def lanes(block, width):
    return pl.ds(pl.multiple_of(block * width, width), width)


def cut_body(blocks, w2, wq, w1, own, w1_own, beside, own_s, w1_s, beside_s, sems):
    model = w2.shape[1]
    width = model // blocks
    ctx = ctx_index()
    copies = Copies(sems)
    going = []
    for dst, block in ((beside_s, lax.rem(ctx + blocks // 2, blocks)), (own_s, ctx)):
        going.append(copies.start(w2, dst.at[:, :model]))
        for part in range(3):
            lo = model + part * width
            going.append(
                copies.start(
                    wq.at[:, lanes(part * blocks + block, width)], dst.at[:, lo : lo + width]
                )
            )
        to, lo = (beside_s, model + 3 * width) if dst is beside_s else (w1_s, 0)
        for part in range(2):
            at = lo + part * width
            going.append(
                copies.start(
                    w1.at[:, lanes(part * blocks + block, width)], to.at[:, at : at + width]
                )
            )
    wait(*going)
    wait(
        copies.start(beside_s, beside), copies.start(own_s, own), copies.start(w1_s, w1_own)
    )


def pack_body(wp, w1, out, out_s, sems):
    model = wp.shape[1]
    copies = Copies(sems)
    wait(copies.start(wp, out_s.at[:, :model]), copies.start(w1, out_s.at[:, model:]))
    wait(copies.start(out_s, out))


def lay_rows(copies, lo, wide, mine, other, out):
    core, yh = lax.axis_index("core"), lax.axis_index("yh")
    return [
        copies.start(src.at[:, slot, :, lo : lo + wide], out.at[side, :, owner])
        for src, owner in ((mine, core), (other, 1 - core))
        for slot, side in ((0, yh), (1, 1 - yh))
    ]


def first_body(x, gain, out, x_s, g_s, n_s, sems):
    copies = Copies(sems)
    wait(copies.start(x, x_s), copies.start(gain, g_s))
    centre, inv = centred(x_s[...].astype(F32))
    n_s[...] = (centre * inv * g_s[...]).astype(BF)
    wait(*[copies.start(n_s, out.at[i]) for i in range(out.shape[0])])


def gate_body(
    taps, frames, x, wm, wo, k, conv, hid, gated, w_s, k_s, pad_s, conv_s, hid_s, gated_s, sems
):
    blocks, records, local, model = x.shape
    length = blocks * local
    width = k_s.shape[1]
    core, yh, z = lax.axis_index("core"), lax.axis_index("yh"), lax.axis_index("z")
    copies = Copies(sems)
    get_k = copies.start(k.at[:, lanes(ctx_index(), width)], k_s)
    for s in range(wm.shape[0]):
        for slot, side in ((0, yh), (1, 1 - yh)):
            w_s[side, z ^ s, core] = wm[s, slot]
            w_s[side, z ^ s, 1 - core] = wo[s, slot]
    zeros = jnp.zeros((16, width), F32)
    pad_s[0:16] = zeros
    pad_s[16 + length : 32 + length] = zeros
    going = []
    for rec in range(records):
        hidden = dot(x[:, rec].reshape(length, model), w_s[...].reshape(model, 2 * width))
        hid_s[rec] = hidden
        going.append(copies.start(hid_s.at[rec], hid.at[rec]))
        here = lax.broadcasted_iota(jnp.int32, (length, width), 0) < frames[rec]
        value = jnp.where(here, hidden[:, :width] * sigmoid(hidden[:, width:]), 0.0).astype(BF)
        gated_s[rec] = value
        going.append(copies.start(gated_s.at[rec], gated.at[rec]))
        pad_s[16 : 16 + length] = value.astype(F32)
        if rec == 0:
            wait(get_k)
        for b in range(blocks):
            total = jnp.zeros((local, width), F32)
            for j in range(taps):
                at = b * local + j + 1
                total = total + k_s[j : j + 1, :] * pad_s[at : at + local, :]
            conv_s[b, rec] = total.astype(BF)
        going.append(copies.start(conv_s.at[:, rec], conv.at[:, rec]))
    wait(*going)


def token_body(
    c, mine, other, x, go, g2, ga, sent, res, gc, c_s, w2_s, x_s, go_s, g2_s, ga_s, n_s, res_s, gc_s, sems
):
    rows, model = x_s.shape
    blocks = c.shape[0]
    width = model // blocks
    copies = Copies(sems)
    get_c = copies.start(c, c_s)
    get_w2 = lay_rows(copies, 0, model, mine, other, w2_s)
    get_gain = copies.start(g2, g2_s)
    get_go = copies.start(go, go_s)
    get_x = copies.start(x, x_s)
    get_ga = copies.start(ga, ga_s)
    wait(get_c)
    conv = jnp.concatenate([c_s[i] for i in range(blocks)], 1).astype(F32)
    centre, inv = centred(conv)
    wait(get_gain)
    gain = g2_s[...]
    normal = centre * inv * gain
    opening = sigmoid(normal)
    swished = (normal * opening).astype(BF)
    wait(get_go, *get_w2)
    w2 = w2_s[...].reshape(model, model)
    back_two = dot_t(go_s[...], w2)
    slope = opening + normal * opening * (1.0 - opening)
    grad_conv = norm_pull(back_two * slope * gain, centre, inv).astype(BF)
    for i in range(blocks):
        gc_s[i] = grad_conv[:, i * width : (i + 1) * width]
    going = [copies.start(gc_s, gc)]
    wait(get_x, get_ga)
    residual = (x_s[...].astype(F32) + dot(swished, w2)).astype(BF)
    res_s[...] = residual
    going.append(copies.start(res_s, res))
    centre, inv = centred(residual.astype(F32))
    n_s[...] = (centre * inv * ga_s[...]).astype(BF)
    wait(*going, *[copies.start(n_s, sent.at[i]) for i in range(blocks)])


def back_body(
    taps, frames, gc, x, hid, gated, k, back, keep, send, gk_out,
    gc_s, k_s, hid_s, gated_s, pad_s, gpad_s, gh_s, both_s, gf_s, gk_s, out_s, gko_s, sems,
):
    blocks, records, local, model = x.shape
    length = blocks * local
    rows = records * local
    width = k_s.shape[1]
    core = lax.axis_index("core")
    copies = Copies(sems)
    get_gc = copies.start(gc, gc_s)
    get_k = copies.start(k.at[:, lanes(ctx_index(), width)], k_s)
    get_gated = copies.start(gated, gated_s)
    get_hid = copies.start(hid, hid_s)
    gk_s[...] = jnp.zeros_like(gk_s)
    zeros = jnp.zeros((16, width), F32)
    for ref in (pad_s, gpad_s):
        ref[0:16] = zeros
        ref[16 + length : 32 + length] = zeros
    wait(get_k, get_gc, get_gated)
    for rec in range(records):
        pad_s[16 : 16 + length] = gc_s[:, rec].reshape(length, width).astype(F32)
        gpad_s[16 : 16 + length] = gated_s[rec].astype(F32)
        for b in range(blocks):
            base = b * local
            total = jnp.zeros((local, width), F32)
            own = pad_s[16 + base : 16 + base + local, :]
            for j in range(taps):
                at = base + taps - j
                total = total + k_s[j : j + 1, :] * pad_s[at : at + local, :]
                at = base + j + 1
                term = (gpad_s[at : at + local, :] * own).reshape(local // 8, 8, width)
                gk_s[j] += jnp.sum(term, 0)
            at = lax.broadcasted_iota(jnp.int32, (local, width), 0) + base
            grad_gated = jnp.where(at < frames[rec], total, 0.0)
            if rec == 0 and b == 0:
                wait(get_hid)
            linear = hid_s[rec, base : base + local, :width]
            opening = sigmoid(hid_s[rec, base : base + local, width:])
            first = grad_gated * opening
            second = (first * linear * (1.0 - opening)).astype(BF)
            first = first.astype(BF)
            gh_s[base : base + local, :width] = first
            gh_s[base : base + local, width:] = second
            out_s[b, rec * local : (rec + 1) * local] = first
            out_s[b, rows + rec * local : rows + (rec + 1) * local] = second
        grad_first = lax.dot_general(
            x[:, rec].reshape(length, model),
            gh_s[...],
            (((0,), (0,)), ((), ())),
            preferred_element_type=F32,
        ).reshape(gf_s.shape)
        if rec == 0:
            gf_s[...] = grad_first
        else:
            both_s[...] = (gf_s[...] + grad_first).astype(BF)
    gk = jnp.sum(gk_s[...], 1)
    half = gko_s.shape[0]
    gko_s[:, :width] = gk[:half]
    gko_s[:, width:] = gk[half:]
    wait(
        copies.start(both_s.at[:, :, 1 - core], send),
        copies.start(gko_s, gk_out),
        copies.start(both_s.at[:, :, core], keep),
        copies.start(out_s, back.at[:, : 2 * rows]),
    )


def pair_body(keep, recv, gk, gkr, *refs):
    zs = len(refs) - 5
    outs, (keep_s, gk_s, both_s, out_s, sems) = refs[:zs], refs[zs:]
    depth, wide = keep_s.shape[2:]
    half = wide // 2
    copies = Copies(sems)
    wait(copies.start(keep, keep_s), copies.start(gk, gk_s))
    both_s[...] = (keep_s[...].astype(F32) + recv[...].astype(F32)).astype(BF)
    gk_sum = (gk_s[...] + gkr[...]).astype(BF)
    tall = out_s.shape[2] // 2
    z = lax.axis_index("z")
    going = []
    for s in range(zs):
        for side in range(2):
            part = both_s[side, z ^ s]
            for h in range(2):
                at = h * tall
                out_s[s, side, at : at + depth] = part[:, h * half : (h + 1) * half]
                out_s[s, side, at + depth : at + tall] = gk_sum[:, h * half : (h + 1) * half]
        going.append(copies.start(out_s.at[s], outs[s]))
    wait(*going)


def sum_body(*refs):
    keep, send, parts_s, total_s, sems = refs[-5:]
    copies = Copies(sems)
    wait(*[copies.start(ref, parts_s.at[i]) for i, ref in enumerate(refs[:-5])])
    total_s[...] = jnp.sum(parts_s[...].astype(F32), 0).astype(BF)
    yh = lax.axis_index("yh")
    wait(copies.start(total_s.at[1 - yh], send), copies.start(total_s.at[yh], keep))


def heads_body(head_dim, frames, x, mine, other, held, back, w, att_s, sems):
    del held
    copies = Copies(sems)
    get_w = lay_rows(copies, x.shape[3], w.shape[4], mine, other, w)
    blocks, records, local, model = x.shape
    length = blocks * local
    width = model // blocks
    rows = min(256, length)
    lane = lax.broadcasted_iota(jnp.int32, (rows, width), 1)
    scaling = head_dim**-0.5
    wait(*get_w)
    for rec in range(records):
        packed = dot(x[:, rec].reshape(length, model), w[...].reshape(model, 3 * width))
        packed = packed.astype(BF)
        q = packed[:, :width]
        k = packed[:, width : 2 * width]
        v = packed[:, 2 * width :]
        key_ok = lax.broadcasted_iota(jnp.int32, (rows, length), 1) < frames[rec]
        for r in range(0, length, rows):
            qr = q[r : r + rows]
            attended = jnp.zeros((rows, width), F32)
            for h in range(width // head_dim):
                here = (lane >= h * head_dim) & (lane < (h + 1) * head_dim)
                scores = dot_t(jnp.where(here, qr, jnp.zeros_like(qr)), k) * scaling
                scores = jnp.where(key_ok, scores, -1e30)
                top = jnp.max(scores, -1, keepdims=True)
                numer = jnp.where(key_ok, jnp.exp(scores - top), 0.0)
                denom = jnp.sum(numer, -1, keepdims=True)
                attended = jnp.where(here, dot(numer.astype(BF), v) / denom, attended)
            got = attended.astype(BF).reshape(rows // local, local, width)
            att_s[r // local : (r + rows) // local, rec * local : (rec + 1) * local] = got
    tall = records * local
    wait(copies.start(att_s, back.at[:, 2 * tall : 3 * tall]))


def result_body(
    frames, a, mine, other, res, x, go, g1, out, gin,
    wp_s, w1_s, w2_s, res_s, x_s, go_s, g1_s, out_s, gin_s, sems,
):
    rows, model = x_s.shape
    blocks = a.shape[0]
    copies = Copies(sems)
    get_w = [
        lay_rows(copies, i * model, model, mine, other, one)
        for i, one in enumerate((wp_s, w1_s, w2_s))
    ]
    get_res = copies.start(res, res_s)
    get_x = copies.start(x, x_s)
    get_go = copies.start(go, go_s)
    get_g1 = copies.start(g1, g1_s)
    attended = jnp.concatenate([a[i, 2 * rows : 3 * rows] for i in range(blocks)], 1)
    linear = jnp.concatenate([a[i, :rows] for i in range(blocks)], 1)
    gating = jnp.concatenate([a[i, rows : 2 * rows] for i in range(blocks)], 1)
    wait(*get_w[0])
    projected = dot(attended, wp_s[...].reshape(model, model))
    records = frames.shape[0]
    local = rows // records
    at = lax.broadcasted_iota(jnp.int32, (local, model), 0) + ctx_index() * local
    present = jnp.concatenate([(at < frames[r]).astype(F32) for r in range(records)], 0)
    wait(get_res)
    out_s[...] = (res_s[...].astype(F32) + present * projected).astype(BF)
    put_out = copies.start(out_s, out)
    wait(*get_w[1])
    back_one = dot_t(linear, w1_s[...].reshape(model, model))
    wait(*get_w[2])
    back_one = back_one + dot_t(gating, w2_s[...].reshape(model, model))
    wait(get_x, get_go, get_g1)
    centre, inv = centred(x_s[...].astype(F32))
    pulled = norm_pull(back_one * g1_s[...], centre, inv)
    gin_s[...] = (go_s[...].astype(F32) + pulled).astype(BF)
    wait(put_out, copies.start(gin_s, gin))


def lay_body(a, gf, gk, gf_s, gk_s, sems):
    blocks = a.shape[0]
    depth, taps = gf_s.shape[0], gk_s.shape[0]
    model = gk_s.shape[1]
    width = model // blocks
    tall = a.shape[2] // 2
    half = tall - depth
    for i in range(blocks):
        lo = i * width
        total = a[i, 0].astype(F32) + a[(i + blocks // 2) % blocks, 1].astype(F32)
        for h in range(2):
            at = h * tall
            gf_s[:, h * model + lo : h * model + lo + width] = total[at : at + depth]
            count = min(half, taps - h * half)
            gk_s[h * half : h * half + count, lo : lo + width] = total[
                at + depth : at + depth + count
            ]
    copies = Copies(sems)
    wait(copies.start(gf_s, gf), copies.start(gk_s, gk))


def swap_core(v):
    return lax.ppermute(v, "core", [(0, 1), (1, 0)])


def swap_yh(v):
    return lax.ppermute(v, ("yh", "yl"), [(0, 3), (3, 0), (1, 2), (2, 1)])


def pair_z(v, by):
    return lax.ppermute(v, "z", [(i, i ^ by) for i in range(lax.axis_size("z"))])


def local(
    inputs,
    frames,
    gain_first,
    w_first,
    depth_kernel,
    gain_second,
    w_second,
    gain_attn,
    w_qkv,
    w_proj,
    grad_out,
):
    records, local_len, model = inputs.shape
    taps = depth_kernel.shape[0]
    blocks = lax.axis_size(CTX)
    zs = lax.axis_size("z")
    depth = w_first.shape[0]
    width = model // blocks
    length = blocks * local_len
    rows = records * local_len
    head_dim = model // HEADS
    barrier = lax.optimization_barrier
    x = inputs.reshape(rows, model)
    cot = grad_out.reshape(rows, model)
    gains = [g.reshape(1, model) for g in (gain_first, gain_second, gain_attn)]

    part = model + 3 * width
    own, w1_own, beside = run(
        functools.partial(cut_body, blocks),
        [
            ((depth, part), BF, HBM),
            ((depth, 2 * width), BF, HBM),
            ((depth, part + 2 * width), BF, HBM),
        ],
        [(w_second, HBM), (w_qkv, HBM), (w_first, HBM)],
        "cut",
        [((depth, part), BF), ((depth, 2 * width), BF), ((depth, part + 2 * width), BF)],
        15,
    )
    beside = swap_yh(beside)
    (sent,) = run(
        first_body,
        [((blocks, rows, model), BF, HBM)],
        [(x, HBM), (gains[0], HBM)],
        "first_norm",
        [((rows, model), BF), ((1, model), F32), ((rows, model), BF)],
        blocks + 2,
    )
    beside, sent = barrier((beside, sent))
    shard_a = jnp.stack([own, beside[:, :part]])
    all_a = lax.all_gather(shard_a, "z", axis=0, tiled=False)
    normed = lax.all_to_all(sent, CTX, 0, 0, tiled=True).reshape(blocks, records, local_len, model)

    w1_part = jnp.stack([w1_own, beside[:, part:]])
    two = jnp.stack([w1_part, pair_z(w1_part, 1)])
    w1_mine = jnp.concatenate([two] + [pair_z(two, s) for s in range(2, zs, 2)])
    w1_other = swap_core(w1_mine)

    (own_b,) = run(
        pack_body,
        [((depth, 3 * model), BF, HBM)],
        [(w_proj, HBM), (w_first, HBM)],
        "pack",
        [((depth, 3 * model), BF)],
        3,
    )
    shard_b = jnp.stack([own_b, swap_yh(own_b)])
    shard_b, normed = barrier((shard_b, normed))

    conv, hidden, gated = run(
        functools.partial(gate_body, taps),
        [
            ((blocks, records, local_len, width), BF, HBM),
            ((records, length, 2 * width), F32, HBM),
            ((records, length, width), BF, HBM),
        ],
        [(frames, SMEM), (normed, VMEM), (w1_mine, VMEM), (w1_other, VMEM), (depth_kernel, HBM)],
        "gate_conv",
        [
            ((2, zs, 2, depth, 2 * width), BF),
            ((taps, width), F32),
            ((length + 32, width), F32),
            ((blocks, records, local_len, width), BF),
            ((records, length, 2 * width), F32),
            ((records, length, width), BF),
        ],
        1 + 3 * records,
    )

    conv_rows = lax.all_to_all(conv, CTX, 0, 0, tiled=True).reshape(blocks, rows, width)
    all_a, conv_rows = barrier((all_a, conv_rows))
    other_a = swap_core(all_a)
    shard_b, all_a = barrier((shard_b, all_a))
    all_b = lax.all_gather(shard_b, "z", axis=0, tiled=False)

    sent, residual, grad_conv = run(
        token_body,
        [
            ((blocks, rows, model), BF, HBM),
            ((rows, model), BF, HBM),
            ((blocks, rows, width), BF, HBM),
        ],
        [
            (conv_rows, HBM), (all_a, HBM), (other_a, ANY), (x, HBM), (cot, HBM), (gains[1], HBM),
            (gains[2], HBM),
        ],
        "token_rows",
        [
            ((blocks, rows, width), BF),
            ((2, zs, 2, depth, model), BF),
            ((rows, model), BF),
            ((rows, model), BF),
            ((1, model), F32),
            ((1, model), F32),
            ((rows, model), BF),
            ((rows, model), BF),
            ((blocks, rows, width), BF),
        ],
        blocks + 11,
    )
    grad_conv = lax.all_to_all(grad_conv, CTX, 0, 0, tiled=True)
    sent, grad_conv = barrier((sent, grad_conv))
    grad_conv = grad_conv.reshape(blocks, records, local_len, width)
    attn_in = lax.all_to_all(sent, CTX, 0, 0, tiled=True)
    attn_in = attn_in.reshape(blocks, records, local_len, model)

    tall = depth + 16
    half_share = (2, zs, depth, 2 * width)
    back, keep, send, gk = run(
        functools.partial(back_body, taps),
        [
            ((blocks, 3 * rows, width), BF, HBM),
            (half_share, BF, HBM),
            (half_share, BF, HBM),
            ((16, 2 * width), F32, HBM),
        ],
        [
            (frames, SMEM), (grad_conv, HBM), (normed, VMEM), (hidden, HBM), (gated, HBM),
            (depth_kernel, HBM),
        ],
        "conv_back",
        [
            ((blocks, records, local_len, width), BF),
            ((taps, width), F32),
            ((records, length, 2 * width), F32),
            ((records, length, width), BF),
            ((length + 32, width), F32),
            ((length + 32, width), F32),
            ((length, 2 * width), BF),
            ((2, zs, 2, depth, 2 * width), BF),
            ((2, zs, 2, depth, 2 * width), F32),
            ((32, 8, width), F32),
            ((blocks, 2 * rows, width), BF),
            ((16, 2 * width), F32),
        ],
        8,
    )

    chunk = (2, 2 * tall, width)
    chunks = run(
        pair_body,
        [(chunk, BF, HBM)] * zs,
        [(keep, HBM), (swap_core(send), VMEM), (gk, HBM), (swap_core(gk), VMEM)],
        "pair_sum",
        [
            (half_share, BF),
            ((16, 2 * width), F32),
            (half_share, BF),
            ((zs,) + chunk, BF),
        ],
        zs + 2,
    )
    sums = [chunks[0]] + [pair_z(chunks[s], s) for s in range(1, zs)]
    attn_in, *sums[1:3] = barrier((attn_in, *sums[1:3]))
    (back,) = run(
        functools.partial(heads_body, head_dim),
        [(back.shape, BF, HBM)],
        [(frames, SMEM), (attn_in, VMEM), (all_a, HBM), (other_a, ANY), (back, HBM)],
        "heads",
        [((2, zs, 2, depth, 3 * width), BF), ((blocks, rows, width), BF)],
        5,
        {4: 0},
    )
    keep, send = run(
        sum_body,
        [(chunk[1:], BF, HBM)] * 2,
        [(one, ANY) for one in sums[:3]] + [(one, VMEM) for one in sums[3:]],
        "share_sum",
        [((zs,) + chunk, BF), (chunk, BF)],
        zs + 2,
    )
    all_b, back, keep, send = barrier((all_b, back, keep, send))
    pair = jnp.stack([keep, swap_yh(send)])
    pair = jnp.broadcast_to(pair, (blocks,) + pair.shape)

    other_b = swap_core(all_b)
    back = lax.all_to_all(back, CTX, 0, 0, tiled=True)
    pair, back = barrier((pair, back))
    pair = lax.all_to_all(pair, CTX, 0, 0, tiled=True)
    result, grad_in = run(
        result_body,
        [((rows, model), BF, HBM)] * 2,
        [
            (frames, SMEM), (back, VMEM), (all_b, HBM), (other_b, ANY), (residual, HBM), (x, HBM),
            (cot, HBM), (gains[0], HBM),
        ],
        "result_rows",
        [((2, zs, 2, depth, model), BF)] * 3
        + [((rows, model), BF)] * 3
        + [((1, model), F32)]
        + [((rows, model), BF)] * 2,
        18,
    )
    pair, result, grad_in = barrier((pair, result, grad_in))
    grad_first, grad_kernel = run(
        lay_body,
        [((depth, 2 * model), F32, HBM), ((taps, model), F32, HBM)],
        [(pair, VMEM)],
        "lay_out",
        [((depth, 2 * model), F32), ((taps, model), F32)],
        2,
    )
    return (
        result.reshape(records, local_len, model),
        grad_in.reshape(records, local_len, model),
        grad_first,
        grad_kernel,
    )


def solution(mesh):
    dp, ctx = mesh.devices.shape
    split = Mesh(
        mesh.devices.reshape(2, dp // 4, 2, 2, ctx // 2), ("yh", "z", "core", "yl", "x")
    )
    tokens = P(DP, CTX, None)
    placed = (
        tokens,
        P(DP),
        P(),
        P(DP, None),
        P(),
        P(),
        P(DP, None),
        P(),
        P(DP, None),
        P(DP, None),
        tokens,
    )
    return jax.shard_map(
        local,
        mesh=split,
        in_specs=placed,
        out_specs=(tokens, tokens, P(DP, None), P()),
        check_vma=False,
    )
```

```python
import functools

import jax
import jax.numpy as jnp
from jax import lax
from jax.experimental import pallas as pl
from jax.experimental.pallas import tpu as pltpu
from jax.sharding import Mesh
from jax.sharding import PartitionSpec as P

HEADS = 16
EPSILON = 1e-05
BF = jnp.bfloat16
F32 = jnp.float32

DP = ("yh", "z", "core")
CTX = ("yl", "x")

HBM, VMEM, SMEM, ANY = pltpu.HBM, pltpu.VMEM, pltpu.SMEM, pl.ANY


def run(body, outs, ins, name, scratch=(), sems=0, alias=None, mib=36):
    scratch = [pltpu.VMEM(*one) for one in scratch]
    if sems:
        scratch.append(pltpu.SemaphoreType.DMA((sems,)))
    return pl.pallas_call(
        body,
        out_shape=tuple(o[2](o[0], o[1]) for o in outs),
        in_specs=[pl.BlockSpec(memory_space=space) for _, space in ins],
        out_specs=tuple(pl.BlockSpec(memory_space=o[2]) for o in outs),
        scratch_shapes=scratch,
        input_output_aliases=alias or {},
        compiler_params=pltpu.CompilerParams(vmem_limit_bytes=mib << 20),
        name=name,
    )(
        *[
            v if space in (SMEM, ANY) else pltpu.with_memory_space_constraint(v, space)
            for v, space in ins
        ]
    )


class Copies:
    def __init__(self, sems):
        self.sems, self.used = sems, 0

    def start(self, src, dst):
        one = pltpu.make_async_copy(src, dst, self.sems.at[self.used])
        self.used += 1
        one.start()
        return one


def wait(*copies):
    for one in copies:
        one.wait()


def centred(values):
    centre = values - jnp.mean(values, -1, keepdims=True)
    spread = jnp.mean(centre * centre, -1, keepdims=True)
    return centre, lax.rsqrt(spread + EPSILON)


def norm_pull(cot, centre, inv):
    xhat = centre * inv
    return inv * (
        cot - jnp.mean(cot, -1, keepdims=True) - xhat * jnp.mean(cot * xhat, -1, keepdims=True)
    )


def dot(a, b):
    return jnp.dot(a, b, preferred_element_type=F32)


def dot_t(a, b):
    return lax.dot_general(a, b, (((1,), (1,)), ((), ())), preferred_element_type=F32)


def sigmoid(v):
    return jax.nn.sigmoid(v)


def ctx_index():
    return lax.axis_index("yl") * lax.axis_size("x") + lax.axis_index("x")


def lanes(block, width):
    return pl.ds(pl.multiple_of(block * width, width), width)


def cut_body(blocks, w2, wq, w1, own, w1_own, beside, own_s, w1_s, beside_s, sems):
    model = w2.shape[1]
    width = model // blocks
    ctx = ctx_index()
    copies = Copies(sems)
    going = []
    for dst, block in ((beside_s, lax.rem(ctx + blocks // 2, blocks)), (own_s, ctx)):
        going.append(copies.start(w2, dst.at[:, :model]))
        for part in range(3):
            lo = model + part * width
            going.append(
                copies.start(
                    wq.at[:, lanes(part * blocks + block, width)], dst.at[:, lo : lo + width]
                )
            )
        to, lo = (beside_s, model + 3 * width) if dst is beside_s else (w1_s, 0)
        for part in range(2):
            at = lo + part * width
            going.append(
                copies.start(
                    w1.at[:, lanes(part * blocks + block, width)], to.at[:, at : at + width]
                )
            )
    wait(*going)
    wait(
        copies.start(beside_s, beside), copies.start(own_s, own), copies.start(w1_s, w1_own)
    )


def pack_body(wp, w1, out, out_s, sems):
    model = wp.shape[1]
    copies = Copies(sems)
    wait(copies.start(wp, out_s.at[:, :model]), copies.start(w1, out_s.at[:, model:]))
    wait(copies.start(out_s, out))


def lay_rows(copies, lo, wide, mine, other, out):
    core, yh = lax.axis_index("core"), lax.axis_index("yh")
    return [
        copies.start(src.at[:, slot, :, lo : lo + wide], out.at[side, :, owner])
        for src, owner in ((mine, core), (other, 1 - core))
        for slot, side in ((0, yh), (1, 1 - yh))
    ]


def first_body(x, gain, out, x_s, g_s, n_s, sems):
    copies = Copies(sems)
    wait(copies.start(x, x_s), copies.start(gain, g_s))
    centre, inv = centred(x_s[...].astype(F32))
    n_s[...] = (centre * inv * g_s[...]).astype(BF)
    wait(*[copies.start(n_s, out.at[i]) for i in range(out.shape[0])])


def gate_body(
    taps, frames, x, wm, wo, k, conv, hid, gated, w_s, k_s, pad_s, conv_s, hid_s, gated_s, sems
):
    blocks, records, local, model = x.shape
    length = blocks * local
    width = k_s.shape[1]
    core, yh, z = lax.axis_index("core"), lax.axis_index("yh"), lax.axis_index("z")
    copies = Copies(sems)
    get_k = copies.start(k.at[:, lanes(ctx_index(), width)], k_s)
    for s in range(wm.shape[0]):
        for slot, side in ((0, yh), (1, 1 - yh)):
            w_s[side, z ^ s, core] = wm[s, slot]
            w_s[side, z ^ s, 1 - core] = wo[s, slot]
    zeros = jnp.zeros((16, width), F32)
    pad_s[0:16] = zeros
    pad_s[16 + length : 32 + length] = zeros
    going = []
    for rec in range(records):
        hidden = dot(x[:, rec].reshape(length, model), w_s[...].reshape(model, 2 * width))
        hid_s[rec] = hidden
        going.append(copies.start(hid_s.at[rec], hid.at[rec]))
        here = lax.broadcasted_iota(jnp.int32, (length, width), 0) < frames[rec]
        value = jnp.where(here, hidden[:, :width] * sigmoid(hidden[:, width:]), 0.0).astype(BF)
        gated_s[rec] = value
        going.append(copies.start(gated_s.at[rec], gated.at[rec]))
        pad_s[16 : 16 + length] = value.astype(F32)
        if rec == 0:
            wait(get_k)
        for b in range(blocks):
            total = jnp.zeros((local, width), F32)
            for j in range(taps):
                at = b * local + j + 1
                total = total + k_s[j : j + 1, :] * pad_s[at : at + local, :]
            conv_s[b, rec] = total.astype(BF)
        going.append(copies.start(conv_s.at[:, rec], conv.at[:, rec]))
    wait(*going)


def token_body(
    c, mine, other, x, go, g2, ga, sent, res, gc, c_s, w2_s, x_s, go_s, g2_s, ga_s, n_s, res_s, gc_s, sems
):
    rows, model = x_s.shape
    blocks = c.shape[0]
    width = model // blocks
    copies = Copies(sems)
    get_c = copies.start(c, c_s)
    get_w2 = lay_rows(copies, 0, model, mine, other, w2_s)
    get_gain = copies.start(g2, g2_s)
    get_go = copies.start(go, go_s)
    get_x = copies.start(x, x_s)
    get_ga = copies.start(ga, ga_s)
    wait(get_c)
    conv = jnp.concatenate([c_s[i] for i in range(blocks)], 1).astype(F32)
    centre, inv = centred(conv)
    wait(get_gain)
    gain = g2_s[...]
    normal = centre * inv * gain
    opening = sigmoid(normal)
    swished = (normal * opening).astype(BF)
    wait(get_go, *get_w2)
    w2 = w2_s[...].reshape(model, model)
    back_two = dot_t(go_s[...], w2)
    slope = opening + normal * opening * (1.0 - opening)
    grad_conv = norm_pull(back_two * slope * gain, centre, inv).astype(BF)
    for i in range(blocks):
        gc_s[i] = grad_conv[:, i * width : (i + 1) * width]
    going = [copies.start(gc_s, gc)]
    wait(get_x, get_ga)
    residual = (x_s[...].astype(F32) + dot(swished, w2)).astype(BF)
    res_s[...] = residual
    going.append(copies.start(res_s, res))
    centre, inv = centred(residual.astype(F32))
    n_s[...] = (centre * inv * ga_s[...]).astype(BF)
    wait(*going, *[copies.start(n_s, sent.at[i]) for i in range(blocks)])


def back_body(
    taps, frames, gc, x, hid, gated, k, back, keep, send, gk_out,
    gc_s, k_s, hid_s, gated_s, pad_s, gpad_s, gh_s, both_s, gf_s, gk_s, out_s, gko_s, sems,
):
    blocks, records, local, model = x.shape
    length = blocks * local
    rows = records * local
    width = k_s.shape[1]
    core = lax.axis_index("core")
    copies = Copies(sems)
    get_gc = copies.start(gc, gc_s)
    get_k = copies.start(k.at[:, lanes(ctx_index(), width)], k_s)
    get_gated = copies.start(gated, gated_s)
    get_hid = copies.start(hid, hid_s)
    gk_s[...] = jnp.zeros_like(gk_s)
    zeros = jnp.zeros((16, width), F32)
    for ref in (pad_s, gpad_s):
        ref[0:16] = zeros
        ref[16 + length : 32 + length] = zeros
    going = []
    wait(get_k, get_gc, get_gated)
    for rec in range(records):
        pad_s[16 : 16 + length] = gc_s[:, rec].reshape(length, width).astype(F32)
        gpad_s[16 : 16 + length] = gated_s[rec].astype(F32)
        for b in range(blocks):
            base = b * local
            total = jnp.zeros((local, width), F32)
            own = pad_s[16 + base : 16 + base + local, :]
            for j in range(taps):
                at = base + taps - j
                total = total + k_s[j : j + 1, :] * pad_s[at : at + local, :]
                at = base + j + 1
                term = (gpad_s[at : at + local, :] * own).reshape(local // 8, 8, width)
                gk_s[j] += jnp.sum(term, 0)
            at = lax.broadcasted_iota(jnp.int32, (local, width), 0) + base
            grad_gated = jnp.where(at < frames[rec], total, 0.0)
            if rec == 0 and b == 0:
                wait(get_hid)
            linear = hid_s[rec, base : base + local, :width]
            opening = sigmoid(hid_s[rec, base : base + local, width:])
            first = grad_gated * opening
            second = (first * linear * (1.0 - opening)).astype(BF)
            first = first.astype(BF)
            gh_s[base : base + local, :width] = first
            gh_s[base : base + local, width:] = second
            out_s[b, rec * local : (rec + 1) * local] = first
            out_s[b, rows + rec * local : rows + (rec + 1) * local] = second
        for part in range(2):
            at = part * rows + rec * local
            going.append(
                copies.start(out_s.at[:, at : at + local], back.at[:, at : at + local])
            )
        grad_first = lax.dot_general(
            x[:, rec].reshape(length, model),
            gh_s[...],
            (((0,), (0,)), ((), ())),
            preferred_element_type=F32,
        ).reshape(gf_s.shape)
        if rec == 0:
            gf_s[...] = grad_first
        else:
            both_s[...] = (gf_s[...] + grad_first).astype(BF)
    gk = jnp.sum(gk_s[...], 1)
    half = gko_s.shape[0]
    gko_s[:, :width] = gk[:half]
    gko_s[:, width:] = gk[half:]
    wait(
        copies.start(both_s.at[:, :, 1 - core], send),
        copies.start(gko_s, gk_out),
        copies.start(both_s.at[:, :, core], keep),
        *going,
    )


def pair_body(keep, recv, gk, gkr, *refs):
    zs = len(refs) - 5
    outs, (keep_s, gk_s, both_s, out_s, sems) = refs[:zs], refs[zs:]
    depth, wide = keep_s.shape[2:]
    half = wide // 2
    copies = Copies(sems)
    wait(copies.start(keep, keep_s), copies.start(gk, gk_s))
    both_s[...] = (keep_s[...].astype(F32) + recv[...].astype(F32)).astype(BF)
    gk_sum = (gk_s[...] + gkr[...]).astype(BF)
    tall = out_s.shape[2] // 2
    z = lax.axis_index("z")
    going = []
    for s in range(zs):
        for side in range(2):
            part = both_s[side, z ^ s]
            for h in range(2):
                at = h * tall
                out_s[s, side, at : at + depth] = part[:, h * half : (h + 1) * half]
                out_s[s, side, at + depth : at + tall] = gk_sum[:, h * half : (h + 1) * half]
        going.append(copies.start(out_s.at[s], outs[s]))
    wait(*going)


def sum_body(*refs):
    keep, send, parts_s, total_s, sems = refs[-5:]
    copies = Copies(sems)
    wait(*[copies.start(ref, parts_s.at[i]) for i, ref in enumerate(refs[:-5])])
    total_s[...] = jnp.sum(parts_s[...].astype(F32), 0).astype(BF)
    yh = lax.axis_index("yh")
    wait(copies.start(total_s.at[1 - yh], send), copies.start(total_s.at[yh], keep))


def spread_body(keep, recv, out, pair_s, sems):
    copies = Copies(sems)
    wait(copies.start(keep, pair_s.at[0]), copies.start(recv, pair_s.at[1]))
    wait(*[copies.start(pair_s, out.at[i]) for i in range(out.shape[0])])


def heads_body(head_dim, frames, x, mine, other, held, back, w, att_s, sems):
    del held
    copies = Copies(sems)
    get_w = lay_rows(copies, x.shape[3], w.shape[4], mine, other, w)
    blocks, records, local, model = x.shape
    length = blocks * local
    width = model // blocks
    rows = min(256, length)
    lane = lax.broadcasted_iota(jnp.int32, (rows, width), 1)
    scaling = head_dim**-0.5
    wait(*get_w)
    for rec in range(records):
        packed = dot(x[:, rec].reshape(length, model), w[...].reshape(model, 3 * width))
        packed = packed.astype(BF)
        q = packed[:, :width] * jnp.asarray(scaling, BF)
        k = packed[:, width : 2 * width]
        v = packed[:, 2 * width :]
        bias = jnp.where(
            lax.broadcasted_iota(jnp.int32, (1, length), 1) < frames[rec], 0.0, -1e30
        )
        for r in range(0, length, rows):
            qr = q[r : r + rows]
            attended = jnp.zeros((rows, width), F32)
            for h in range(width // head_dim):
                here = (lane >= h * head_dim) & (lane < (h + 1) * head_dim)
                scores = dot_t(jnp.where(here, qr, jnp.zeros_like(qr)), k) + bias
                top = jnp.max(scores, -1, keepdims=True)
                numer = jnp.exp(scores - top)
                denom = jnp.sum(numer, -1, keepdims=True)
                attended = jnp.where(here, dot(numer.astype(BF), v) / denom, attended)
            got = attended.astype(BF).reshape(rows // local, local, width)
            att_s[r // local : (r + rows) // local, rec * local : (rec + 1) * local] = got
    tall = records * local
    wait(copies.start(att_s, back.at[:, 2 * tall : 3 * tall]))


def result_body(
    frames, a, mine, other, res, x, go, g1, out, gin,
    wp_s, w1_s, w2_s, res_s, x_s, go_s, g1_s, out_s, gin_s, sems,
):
    rows, model = x_s.shape
    blocks = a.shape[0]
    copies = Copies(sems)
    get_w = [
        lay_rows(copies, i * model, model, mine, other, one)
        for i, one in enumerate((wp_s, w1_s, w2_s))
    ]
    get_res = copies.start(res, res_s)
    get_x = copies.start(x, x_s)
    get_go = copies.start(go, go_s)
    get_g1 = copies.start(g1, g1_s)
    attended = jnp.concatenate([a[i, 2 * rows : 3 * rows] for i in range(blocks)], 1)
    linear = jnp.concatenate([a[i, :rows] for i in range(blocks)], 1)
    gating = jnp.concatenate([a[i, rows : 2 * rows] for i in range(blocks)], 1)
    wait(*get_w[0])
    projected = dot(attended, wp_s[...].reshape(model, model))
    records = frames.shape[0]
    local = rows // records
    at = lax.broadcasted_iota(jnp.int32, (local, model), 0) + ctx_index() * local
    present = jnp.concatenate([(at < frames[r]).astype(F32) for r in range(records)], 0)
    wait(get_res)
    out_s[...] = (res_s[...].astype(F32) + present * projected).astype(BF)
    put_out = copies.start(out_s, out)
    wait(*get_w[1])
    back_one = dot_t(linear, w1_s[...].reshape(model, model))
    wait(*get_w[2])
    back_one = back_one + dot_t(gating, w2_s[...].reshape(model, model))
    wait(get_x, get_go, get_g1)
    centre, inv = centred(x_s[...].astype(F32))
    pulled = norm_pull(back_one * g1_s[...], centre, inv)
    gin_s[...] = (go_s[...].astype(F32) + pulled).astype(BF)
    wait(put_out, copies.start(gin_s, gin))


def lay_body(a, gf, gk, gf_s, gk_s, sems):
    blocks = a.shape[0]
    depth, taps = gf_s.shape[0], gk_s.shape[0]
    model = gk_s.shape[1]
    width = model // blocks
    tall = a.shape[2] // 2
    half = tall - depth
    for i in range(blocks):
        lo = i * width
        total = a[i, 0].astype(F32) + a[(i + blocks // 2) % blocks, 1].astype(F32)
        for h in range(2):
            at = h * tall
            gf_s[:, h * model + lo : h * model + lo + width] = total[at : at + depth]
            count = min(half, taps - h * half)
            gk_s[h * half : h * half + count, lo : lo + width] = total[
                at + depth : at + depth + count
            ]
    copies = Copies(sems)
    wait(copies.start(gf_s, gf), copies.start(gk_s, gk))


def swap_core(v):
    return lax.ppermute(v, "core", [(0, 1), (1, 0)])


def swap_yh(v):
    return lax.ppermute(v, ("yh", "yl"), [(0, 3), (3, 0), (1, 2), (2, 1)])


def pair_z(v, by):
    return lax.ppermute(v, "z", [(i, i ^ by) for i in range(lax.axis_size("z"))])


def local(
    inputs,
    frames,
    gain_first,
    w_first,
    depth_kernel,
    gain_second,
    w_second,
    gain_attn,
    w_qkv,
    w_proj,
    grad_out,
):
    records, local_len, model = inputs.shape
    taps = depth_kernel.shape[0]
    blocks = lax.axis_size(CTX)
    zs = lax.axis_size("z")
    depth = w_first.shape[0]
    width = model // blocks
    length = blocks * local_len
    rows = records * local_len
    head_dim = model // HEADS
    barrier = lax.optimization_barrier
    x = inputs.reshape(rows, model)
    cot = grad_out.reshape(rows, model)
    gains = [g.reshape(1, model) for g in (gain_first, gain_second, gain_attn)]

    part = model + 3 * width
    own, w1_own, beside = run(
        functools.partial(cut_body, blocks),
        [
            ((depth, part), BF, HBM),
            ((depth, 2 * width), BF, HBM),
            ((depth, part + 2 * width), BF, HBM),
        ],
        [(w_second, HBM), (w_qkv, HBM), (w_first, HBM)],
        "cut",
        [((depth, part), BF), ((depth, 2 * width), BF), ((depth, part + 2 * width), BF)],
        15,
    )
    beside = swap_yh(beside)
    (sent,) = run(
        first_body,
        [((blocks, rows, model), BF, HBM)],
        [(x, HBM), (gains[0], HBM)],
        "first_norm",
        [((rows, model), BF), ((1, model), F32), ((rows, model), BF)],
        blocks + 2,
    )
    beside, sent = barrier((beside, sent))
    shard_a = jnp.stack([own, beside[:, :part]])
    all_a = lax.all_gather(shard_a, "z", axis=0, tiled=False)
    normed = lax.all_to_all(sent, CTX, 0, 0, tiled=True).reshape(blocks, records, local_len, model)

    w1_part = jnp.stack([w1_own, beside[:, part:]])
    two = jnp.stack([w1_part, pair_z(w1_part, 1)])
    w1_mine = jnp.concatenate([two] + [pair_z(two, s) for s in range(2, zs, 2)])
    w1_other = swap_core(w1_mine)

    (own_b,) = run(
        pack_body,
        [((depth, 3 * model), BF, HBM)],
        [(w_proj, HBM), (w_first, HBM)],
        "pack",
        [((depth, 3 * model), BF)],
        3,
    )
    shard_b = jnp.stack([own_b, swap_yh(own_b)])
    conv, hidden, gated = run(
        functools.partial(gate_body, taps),
        [
            ((blocks, records, local_len, width), BF, HBM),
            ((records, length, 2 * width), F32, HBM),
            ((records, length, width), BF, HBM),
        ],
        [(frames, SMEM), (normed, VMEM), (w1_mine, VMEM), (w1_other, VMEM), (depth_kernel, HBM)],
        "gate_conv",
        [
            ((2, zs, 2, depth, 2 * width), BF),
            ((taps, width), F32),
            ((length + 32, width), F32),
            ((blocks, records, local_len, width), BF),
            ((records, length, 2 * width), F32),
            ((records, length, width), BF),
        ],
        1 + 3 * records,
    )

    conv_rows = lax.all_to_all(conv, CTX, 0, 0, tiled=True).reshape(blocks, rows, width)
    all_a, conv_rows = barrier((all_a, conv_rows))
    other_a = swap_core(all_a)
    shard_b, all_a = barrier((shard_b, all_a))
    all_b = lax.all_gather(shard_b, "z", axis=0, tiled=False)

    sent, residual, grad_conv = run(
        token_body,
        [
            ((blocks, rows, model), BF, HBM),
            ((rows, model), BF, HBM),
            ((blocks, rows, width), BF, HBM),
        ],
        [
            (conv_rows, HBM), (all_a, HBM), (other_a, ANY), (x, HBM), (cot, HBM), (gains[1], HBM),
            (gains[2], HBM),
        ],
        "token_rows",
        [
            ((blocks, rows, width), BF),
            ((2, zs, 2, depth, model), BF),
            ((rows, model), BF),
            ((rows, model), BF),
            ((1, model), F32),
            ((1, model), F32),
            ((rows, model), BF),
            ((rows, model), BF),
            ((blocks, rows, width), BF),
        ],
        blocks + 11,
    )
    grad_conv = lax.all_to_all(grad_conv, CTX, 0, 0, tiled=True)
    sent, grad_conv = barrier((sent, grad_conv))
    grad_conv = grad_conv.reshape(blocks, records, local_len, width)
    attn_in = lax.all_to_all(sent, CTX, 0, 0, tiled=True)
    attn_in = attn_in.reshape(blocks, records, local_len, model)

    tall = depth + 16
    half_share = (2, zs, depth, 2 * width)
    back, keep, send, gk = run(
        functools.partial(back_body, taps),
        [
            ((blocks, 3 * rows, width), BF, HBM),
            (half_share, BF, HBM),
            (half_share, BF, HBM),
            ((16, 2 * width), F32, HBM),
        ],
        [
            (frames, SMEM), (grad_conv, HBM), (normed, VMEM), (hidden, HBM), (gated, HBM),
            (depth_kernel, HBM),
        ],
        "conv_back",
        [
            ((blocks, records, local_len, width), BF),
            ((taps, width), F32),
            ((records, length, 2 * width), F32),
            ((records, length, width), BF),
            ((length + 32, width), F32),
            ((length + 32, width), F32),
            ((length, 2 * width), BF),
            ((2, zs, 2, depth, 2 * width), BF),
            ((2, zs, 2, depth, 2 * width), F32),
            ((32, 8, width), F32),
            ((blocks, 2 * rows, width), BF),
            ((16, 2 * width), F32),
        ],
        7 + 2 * records,
    )

    chunk = (2, 2 * tall, width)
    chunks = run(
        pair_body,
        [(chunk, BF, HBM)] * zs,
        [(keep, HBM), (swap_core(send), VMEM), (gk, HBM), (swap_core(gk), VMEM)],
        "pair_sum",
        [
            (half_share, BF),
            ((16, 2 * width), F32),
            (half_share, BF),
            ((zs,) + chunk, BF),
        ],
        zs + 2,
    )
    sums = [chunks[0]] + [pair_z(chunks[s], s) for s in range(1, zs)]
    attn_in, *sums[1:3] = barrier((attn_in, *sums[1:3]))
    (back,) = run(
        functools.partial(heads_body, head_dim),
        [(back.shape, BF, HBM)],
        [(frames, SMEM), (attn_in, VMEM), (all_a, HBM), (other_a, ANY), (back, HBM)],
        "heads",
        [((2, zs, 2, depth, 3 * width), BF), ((blocks, rows, width), BF)],
        5,
        {4: 0},
    )
    keep, send = run(
        sum_body,
        [(chunk[1:], BF, HBM)] * 2,
        [(one, ANY) for one in sums[:3]] + [(one, VMEM) for one in sums[3:]],
        "share_sum",
        [((zs,) + chunk, BF), (chunk, BF)],
        zs + 2,
    )
    all_b, back, keep, send = barrier((all_b, back, keep, send))
    (pair,) = run(
        spread_body,
        [((blocks,) + chunk, BF, HBM)],
        [(keep, HBM), (swap_yh(send), ANY)],
        "spread",
        [(chunk, BF)],
        blocks + 2,
    )

    other_b = swap_core(all_b)
    back = lax.all_to_all(back, CTX, 0, 0, tiled=True)
    pair, back = barrier((pair, back))
    pair = lax.all_to_all(pair, CTX, 0, 0, tiled=True)
    result, grad_in = run(
        result_body,
        [((rows, model), BF, HBM)] * 2,
        [
            (frames, SMEM), (back, VMEM), (all_b, HBM), (other_b, ANY), (residual, HBM), (x, HBM),
            (cot, HBM), (gains[0], HBM),
        ],
        "result_rows",
        [((2, zs, 2, depth, model), BF)] * 3
        + [((rows, model), BF)] * 3
        + [((1, model), F32)]
        + [((rows, model), BF)] * 2,
        18,
    )
    pair, result, grad_in = barrier((pair, result, grad_in))
    grad_first, grad_kernel = run(
        lay_body,
        [((depth, 2 * model), F32, HBM), ((taps, model), F32, HBM)],
        [(pair, VMEM)],
        "lay_out",
        [((depth, 2 * model), F32), ((taps, model), F32)],
        2,
    )
    return (
        result.reshape(records, local_len, model),
        grad_in.reshape(records, local_len, model),
        grad_first,
        grad_kernel,
    )


def solution(mesh):
    dp, ctx = mesh.devices.shape
    split = Mesh(
        mesh.devices.reshape(2, dp // 4, 2, 2, ctx // 2), ("yh", "z", "core", "yl", "x")
    )
    tokens = P(DP, CTX, None)
    placed = (
        tokens,
        P(DP),
        P(),
        P(DP, None),
        P(),
        P(),
        P(DP, None),
        P(),
        P(DP, None),
        P(DP, None),
        tokens,
    )
    return jax.shard_map(
        local,
        mesh=split,
        in_specs=placed,
        out_specs=(tokens, tokens, P(DP, None), P()),
        check_vma=False,
    )
```

```python
import functools

import jax
import jax.numpy as jnp
from jax import lax
from jax.experimental import pallas as pl
from jax.experimental.pallas import tpu as pltpu
from jax.sharding import Mesh
from jax.sharding import PartitionSpec as P

HEADS = 16
EPSILON = 1e-05
BF = jnp.bfloat16
F32 = jnp.float32

DP = ("yh", "z", "core")
CTX = ("yl", "x")

HBM, VMEM, SMEM, ANY = pltpu.HBM, pltpu.VMEM, pltpu.SMEM, pl.ANY


def run(body, outs, ins, name, scratch=(), sems=0, alias=None, mib=36):
    scratch = [pltpu.VMEM(*one) for one in scratch]
    if sems:
        scratch.append(pltpu.SemaphoreType.DMA((sems,)))
    return pl.pallas_call(
        body,
        out_shape=tuple(o[2](o[0], o[1]) for o in outs),
        in_specs=[pl.BlockSpec(memory_space=space) for _, space in ins],
        out_specs=tuple(pl.BlockSpec(memory_space=o[2]) for o in outs),
        scratch_shapes=scratch,
        input_output_aliases=alias or {},
        compiler_params=pltpu.CompilerParams(vmem_limit_bytes=mib << 20),
        name=name,
    )(
        *[
            v if space in (SMEM, ANY) else pltpu.with_memory_space_constraint(v, space)
            for v, space in ins
        ]
    )


class Copies:
    def __init__(self, sems):
        self.sems, self.used = sems, 0

    def start(self, src, dst):
        one = pltpu.make_async_copy(src, dst, self.sems.at[self.used])
        self.used += 1
        one.start()
        return one


def wait(*copies):
    for one in copies:
        one.wait()


def centred(values):
    centre = values - jnp.mean(values, -1, keepdims=True)
    spread = jnp.mean(centre * centre, -1, keepdims=True)
    return centre, lax.rsqrt(spread + EPSILON)


def norm_pull(cot, centre, inv):
    xhat = centre * inv
    return inv * (
        cot - jnp.mean(cot, -1, keepdims=True) - xhat * jnp.mean(cot * xhat, -1, keepdims=True)
    )


def dot(a, b):
    return jnp.dot(a, b, preferred_element_type=F32)


def dot_t(a, b):
    return lax.dot_general(a, b, (((1,), (1,)), ((), ())), preferred_element_type=F32)


def sigmoid(v):
    return jax.nn.sigmoid(v)


def ctx_index():
    return lax.axis_index("yl") * lax.axis_size("x") + lax.axis_index("x")


def lanes(block, width):
    return pl.ds(pl.multiple_of(block * width, width), width)


def cut_body(blocks, w2, wq, w1, own, w1_own, beside, own_s, w1_s, beside_s, sems):
    model = w2.shape[1]
    width = model // blocks
    ctx = ctx_index()
    copies = Copies(sems)
    going = []
    for dst, block in ((beside_s, lax.rem(ctx + blocks // 2, blocks)), (own_s, ctx)):
        going.append(copies.start(w2, dst.at[:, :model]))
        for part in range(3):
            lo = model + part * width
            going.append(
                copies.start(
                    wq.at[:, lanes(part * blocks + block, width)], dst.at[:, lo : lo + width]
                )
            )
        to, lo = (beside_s, model + 3 * width) if dst is beside_s else (w1_s, 0)
        for part in range(2):
            at = lo + part * width
            going.append(
                copies.start(
                    w1.at[:, lanes(part * blocks + block, width)], to.at[:, at : at + width]
                )
            )
    wait(*going)
    wait(
        copies.start(beside_s, beside), copies.start(own_s, own), copies.start(w1_s, w1_own)
    )


def pack_body(wp, w1, out, out_s, sems):
    model = wp.shape[1]
    copies = Copies(sems)
    wait(copies.start(wp, out_s.at[:, :model]), copies.start(w1, out_s.at[:, model:]))
    wait(copies.start(out_s, out))


def lay_rows(copies, lo, wide, mine, other, out):
    core, yh = lax.axis_index("core"), lax.axis_index("yh")
    return [
        copies.start(src.at[:, slot, :, lo : lo + wide], out.at[side, :, owner])
        for src, owner in ((mine, core), (other, 1 - core))
        for slot, side in ((0, yh), (1, 1 - yh))
    ]


def first_body(x, gain, out, x_s, g_s, n_s, sems):
    copies = Copies(sems)
    wait(copies.start(x, x_s), copies.start(gain, g_s))
    centre, inv = centred(x_s[...].astype(F32))
    n_s[...] = (centre * inv * g_s[...]).astype(BF)
    wait(*[copies.start(n_s, out.at[i]) for i in range(out.shape[0])])


def gate_body(
    taps, frames, x, wm, wo, k, conv, hid, gated, w_s, k_s, pad_s, conv_s, hid_s, gated_s, sems
):
    blocks, records, local, model = x.shape
    length = blocks * local
    width = k_s.shape[1]
    core, yh, z = lax.axis_index("core"), lax.axis_index("yh"), lax.axis_index("z")
    copies = Copies(sems)
    get_k = copies.start(k.at[:, lanes(ctx_index(), width)], k_s)
    for s in range(wm.shape[0]):
        for slot, side in ((0, yh), (1, 1 - yh)):
            w_s[side, z ^ s, core] = wm[s, slot]
            w_s[side, z ^ s, 1 - core] = wo[s, slot]
    zeros = jnp.zeros((16, width), F32)
    pad_s[0:16] = zeros
    pad_s[16 + length : 32 + length] = zeros
    going = []
    for rec in range(records):
        hidden = dot(x[:, rec].reshape(length, model), w_s[...].reshape(model, 2 * width))
        hid_s[rec] = hidden
        going.append(copies.start(hid_s.at[rec], hid.at[rec]))
        here = lax.broadcasted_iota(jnp.int32, (length, width), 0) < frames[rec]
        value = jnp.where(here, hidden[:, :width] * sigmoid(hidden[:, width:]), 0.0).astype(BF)
        gated_s[rec] = value
        going.append(copies.start(gated_s.at[rec], gated.at[rec]))
        pad_s[16 : 16 + length] = value.astype(F32)
        if rec == 0:
            wait(get_k)
        for b in range(blocks):
            total = jnp.zeros((local, width), F32)
            for j in range(taps):
                at = b * local + j + 1
                total = total + k_s[j : j + 1, :] * pad_s[at : at + local, :]
            conv_s[b, rec] = total.astype(BF)
        going.append(copies.start(conv_s.at[:, rec], conv.at[:, rec]))
    wait(*going)


def token_body(
    c, mine, other, x, go, g2, ga, sent, res, gc, c_s, w2_s, x_s, go_s, g2_s, ga_s, n_s, res_s, gc_s, sems
):
    rows, model = x_s.shape
    blocks = c.shape[0]
    width = model // blocks
    copies = Copies(sems)
    get_c = copies.start(c, c_s)
    get_w2 = lay_rows(copies, 0, model, mine, other, w2_s)
    get_gain = copies.start(g2, g2_s)
    get_go = copies.start(go, go_s)
    get_x = copies.start(x, x_s)
    get_ga = copies.start(ga, ga_s)
    wait(get_c)
    conv = jnp.concatenate([c_s[i] for i in range(blocks)], 1).astype(F32)
    centre, inv = centred(conv)
    wait(get_gain)
    gain = g2_s[...]
    normal = centre * inv * gain
    opening = sigmoid(normal)
    swished = (normal * opening).astype(BF)
    wait(get_x, get_ga, *get_w2)
    w2 = w2_s[...].reshape(model, model)
    residual = (x_s[...].astype(F32) + dot(swished, w2)).astype(BF)
    res_s[...] = residual
    going = [copies.start(res_s, res)]
    centre_r, inv_r = centred(residual.astype(F32))
    n_s[...] = (centre_r * inv_r * ga_s[...]).astype(BF)
    going += [copies.start(n_s, sent.at[i]) for i in range(blocks)]
    wait(get_go)
    back_two = dot_t(go_s[...], w2)
    slope = opening + normal * opening * (1.0 - opening)
    grad_conv = norm_pull(back_two * slope * gain, centre, inv).astype(BF)
    for i in range(blocks):
        gc_s[i] = grad_conv[:, i * width : (i + 1) * width]
    wait(*going, copies.start(gc_s, gc))


def back_body(
    taps, frames, gc, x, hid, gated, k, back, keep, send, gk_out,
    gc_s, k_s, hid_s, gated_s, pad_s, gpad_s, gh_s, both_s, gf_s, gk_s, out_s, gko_s, sems,
):
    blocks, records, local, model = x.shape
    length = blocks * local
    rows = records * local
    width = k_s.shape[1]
    core = lax.axis_index("core")
    copies = Copies(sems)
    get_gc = copies.start(gc, gc_s)
    get_k = copies.start(k.at[:, lanes(ctx_index(), width)], k_s)
    get_gated = copies.start(gated, gated_s)
    get_hid = copies.start(hid, hid_s)
    gk_s[...] = jnp.zeros_like(gk_s)
    zeros = jnp.zeros((16, width), F32)
    for ref in (pad_s, gpad_s):
        ref[0:16] = zeros
        ref[16 + length : 32 + length] = zeros
    going = []
    wait(get_k, get_gc, get_gated)
    for rec in range(records):
        pad_s[16 : 16 + length] = gc_s[:, rec].reshape(length, width).astype(F32)
        gpad_s[16 : 16 + length] = gated_s[rec].astype(F32)
        for b in range(blocks):
            base = b * local
            total = jnp.zeros((local, width), F32)
            own = pad_s[16 + base : 16 + base + local, :]
            for j in range(taps):
                at = base + taps - j
                total = total + k_s[j : j + 1, :] * pad_s[at : at + local, :]
                at = base + j + 1
                term = (gpad_s[at : at + local, :] * own).reshape(local // 8, 8, width)
                gk_s[j] += jnp.sum(term, 0)
            at = lax.broadcasted_iota(jnp.int32, (local, width), 0) + base
            grad_gated = jnp.where(at < frames[rec], total, 0.0)
            if rec == 0 and b == 0:
                wait(get_hid)
            linear = hid_s[rec, base : base + local, :width]
            opening = sigmoid(hid_s[rec, base : base + local, width:])
            first = grad_gated * opening
            second = (first * linear * (1.0 - opening)).astype(BF)
            first = first.astype(BF)
            gh_s[base : base + local, :width] = first
            gh_s[base : base + local, width:] = second
            out_s[b, rec * local : (rec + 1) * local] = first
            out_s[b, rows + rec * local : rows + (rec + 1) * local] = second
        for part in range(2):
            at = part * rows + rec * local
            going.append(
                copies.start(out_s.at[:, at : at + local], back.at[:, at : at + local])
            )
        grad_first = lax.dot_general(
            x[:, rec].reshape(length, model),
            gh_s[...],
            (((0,), (0,)), ((), ())),
            preferred_element_type=F32,
        ).reshape(gf_s.shape)
        if rec == 0:
            gf_s[...] = grad_first
        else:
            both_s[...] = (gf_s[...] + grad_first).astype(BF)
    gk = jnp.sum(gk_s[...], 1)
    half = gko_s.shape[0]
    gko_s[:, :width] = gk[:half]
    gko_s[:, width:] = gk[half:]
    wait(
        copies.start(both_s.at[:, :, 1 - core], send),
        copies.start(gko_s, gk_out),
        copies.start(both_s.at[:, :, core], keep),
        *going,
    )


def pair_body(keep, recv, gk, gkr, *refs):
    zs = len(refs) - 5
    outs, (keep_s, gk_s, both_s, out_s, sems) = refs[:zs], refs[zs:]
    depth, wide = keep_s.shape[2:]
    half = wide // 2
    copies = Copies(sems)
    wait(copies.start(keep, keep_s), copies.start(gk, gk_s))
    both_s[...] = (keep_s[...].astype(F32) + recv[...].astype(F32)).astype(BF)
    gk_sum = (gk_s[...] + gkr[...]).astype(BF)
    tall = out_s.shape[2] // 2
    z = lax.axis_index("z")
    going = []
    for s in range(zs):
        for side in range(2):
            part = both_s[side, z ^ s]
            for h in range(2):
                at = h * tall
                out_s[s, side, at : at + depth] = part[:, h * half : (h + 1) * half]
                out_s[s, side, at + depth : at + tall] = gk_sum[:, h * half : (h + 1) * half]
        going.append(copies.start(out_s.at[s], outs[s]))
    wait(*going)


def sum_body(*refs):
    keep, send, parts_s, total_s, sems = refs[-5:]
    copies = Copies(sems)
    wait(*[copies.start(ref, parts_s.at[i]) for i, ref in enumerate(refs[:-5])])
    total_s[...] = jnp.sum(parts_s[...].astype(F32), 0).astype(BF)
    yh = lax.axis_index("yh")
    wait(copies.start(total_s.at[1 - yh], send), copies.start(total_s.at[yh], keep))


def spread_body(keep, recv, out, pair_s, sems):
    copies = Copies(sems)
    wait(copies.start(keep, pair_s.at[0]), copies.start(recv, pair_s.at[1]))
    wait(*[copies.start(pair_s, out.at[i]) for i in range(out.shape[0])])


def heads_body(head_dim, frames, x, mine, other, held, back, w, att_s, sems):
    del held
    copies = Copies(sems)
    get_w = lay_rows(copies, x.shape[3], w.shape[4], mine, other, w)
    blocks, records, local, model = x.shape
    length = blocks * local
    width = model // blocks
    rows = min(256, length)
    lane = lax.broadcasted_iota(jnp.int32, (rows, width), 1)
    scaling = head_dim**-0.5
    wait(*get_w)
    for rec in range(records):
        packed = dot(x[:, rec].reshape(length, model), w[...].reshape(model, 3 * width))
        packed = packed.astype(BF)
        q = packed[:, :width] * jnp.asarray(scaling, BF)
        k = packed[:, width : 2 * width]
        v = jnp.concatenate([packed[:, 2 * width :], jnp.ones((length, width), BF)], 1)
        bias = jnp.where(
            lax.broadcasted_iota(jnp.int32, (1, length), 1) < frames[rec], 0.0, -1e30
        )
        for r in range(0, length, rows):
            qr = q[r : r + rows]
            attended = jnp.zeros((rows, width), F32)
            for h in range(width // head_dim):
                here = (lane >= h * head_dim) & (lane < (h + 1) * head_dim)
                scores = dot_t(jnp.where(here, qr, jnp.zeros_like(qr)), k) + bias
                top = jnp.max(scores, -1, keepdims=True)
                both = dot(jnp.exp(scores - top).astype(BF), v)
                attended = jnp.where(here, both[:, :width] / both[:, width:], attended)
            got = attended.astype(BF).reshape(rows // local, local, width)
            att_s[r // local : (r + rows) // local, rec * local : (rec + 1) * local] = got
    tall = records * local
    wait(copies.start(att_s, back.at[:, 2 * tall : 3 * tall]))


def result_body(
    frames, a, mine, other, res, x, go, g1, out, gin,
    wp_s, w1_s, w2_s, res_s, x_s, go_s, g1_s, out_s, gin_s, sems,
):
    rows, model = x_s.shape
    blocks = a.shape[0]
    copies = Copies(sems)
    get_w = [
        lay_rows(copies, i * model, model, mine, other, one)
        for i, one in enumerate((wp_s, w1_s, w2_s))
    ]
    get_res = copies.start(res, res_s)
    get_x = copies.start(x, x_s)
    get_go = copies.start(go, go_s)
    get_g1 = copies.start(g1, g1_s)
    attended = jnp.concatenate([a[i, 2 * rows : 3 * rows] for i in range(blocks)], 1)
    linear = jnp.concatenate([a[i, :rows] for i in range(blocks)], 1)
    gating = jnp.concatenate([a[i, rows : 2 * rows] for i in range(blocks)], 1)
    wait(*get_w[0])
    projected = dot(attended, wp_s[...].reshape(model, model))
    records = frames.shape[0]
    local = rows // records
    at = lax.broadcasted_iota(jnp.int32, (local, model), 0) + ctx_index() * local
    present = jnp.concatenate([(at < frames[r]).astype(F32) for r in range(records)], 0)
    wait(get_res)
    out_s[...] = (res_s[...].astype(F32) + present * projected).astype(BF)
    put_out = copies.start(out_s, out)
    wait(*get_w[1])
    back_one = dot_t(linear, w1_s[...].reshape(model, model))
    wait(*get_w[2])
    back_one = back_one + dot_t(gating, w2_s[...].reshape(model, model))
    wait(get_x, get_go, get_g1)
    centre, inv = centred(x_s[...].astype(F32))
    pulled = norm_pull(back_one * g1_s[...], centre, inv)
    gin_s[...] = (go_s[...].astype(F32) + pulled).astype(BF)
    wait(put_out, copies.start(gin_s, gin))


def lay_body(a, gf, gk, gf_s, gk_s, sems):
    blocks = a.shape[0]
    depth, taps = gf_s.shape[0], gk_s.shape[0]
    model = gk_s.shape[1]
    width = model // blocks
    tall = a.shape[2] // 2
    half = tall - depth
    for i in range(blocks):
        lo = i * width
        total = a[i, 0].astype(F32) + a[(i + blocks // 2) % blocks, 1].astype(F32)
        for h in range(2):
            at = h * tall
            gf_s[:, h * model + lo : h * model + lo + width] = total[at : at + depth]
            count = min(half, taps - h * half)
            gk_s[h * half : h * half + count, lo : lo + width] = total[
                at + depth : at + depth + count
            ]
    copies = Copies(sems)
    wait(copies.start(gf_s, gf), copies.start(gk_s, gk))


def swap_core(v):
    return lax.ppermute(v, "core", [(0, 1), (1, 0)])


def swap_yh(v):
    return lax.ppermute(v, ("yh", "yl"), [(0, 3), (3, 0), (1, 2), (2, 1)])


def pair_z(v, by):
    return lax.ppermute(v, "z", [(i, i ^ by) for i in range(lax.axis_size("z"))])


def local(
    inputs,
    frames,
    gain_first,
    w_first,
    depth_kernel,
    gain_second,
    w_second,
    gain_attn,
    w_qkv,
    w_proj,
    grad_out,
):
    records, local_len, model = inputs.shape
    taps = depth_kernel.shape[0]
    blocks = lax.axis_size(CTX)
    zs = lax.axis_size("z")
    depth = w_first.shape[0]
    width = model // blocks
    length = blocks * local_len
    rows = records * local_len
    head_dim = model // HEADS
    barrier = lax.optimization_barrier
    x = inputs.reshape(rows, model)
    cot = grad_out.reshape(rows, model)
    gains = [g.reshape(1, model) for g in (gain_first, gain_second, gain_attn)]

    part = model + 3 * width
    own, w1_own, beside = run(
        functools.partial(cut_body, blocks),
        [
            ((depth, part), BF, HBM),
            ((depth, 2 * width), BF, HBM),
            ((depth, part + 2 * width), BF, HBM),
        ],
        [(w_second, HBM), (w_qkv, HBM), (w_first, HBM)],
        "cut",
        [((depth, part), BF), ((depth, 2 * width), BF), ((depth, part + 2 * width), BF)],
        15,
    )
    beside = swap_yh(beside)
    (sent,) = run(
        first_body,
        [((blocks, rows, model), BF, HBM)],
        [(x, HBM), (gains[0], HBM)],
        "first_norm",
        [((rows, model), BF), ((1, model), F32), ((rows, model), BF)],
        blocks + 2,
    )
    beside, sent = barrier((beside, sent))
    shard_a = jnp.stack([own, beside[:, :part]])
    all_a = lax.all_gather(shard_a, "z", axis=0, tiled=False)
    normed = lax.all_to_all(sent, CTX, 0, 0, tiled=True).reshape(blocks, records, local_len, model)

    w1_part = jnp.stack([w1_own, beside[:, part:]])
    two = jnp.stack([w1_part, pair_z(w1_part, 1)])
    w1_mine = jnp.concatenate([two] + [pair_z(two, s) for s in range(2, zs, 2)])
    w1_other = swap_core(w1_mine)

    (own_b,) = run(
        pack_body,
        [((depth, 3 * model), BF, HBM)],
        [(w_proj, HBM), (w_first, HBM)],
        "pack",
        [((depth, 3 * model), BF)],
        3,
    )
    shard_b = jnp.stack([own_b, swap_yh(own_b)])
    conv, hidden, gated = run(
        functools.partial(gate_body, taps),
        [
            ((blocks, records, local_len, width), BF, HBM),
            ((records, length, 2 * width), F32, HBM),
            ((records, length, width), BF, HBM),
        ],
        [(frames, SMEM), (normed, VMEM), (w1_mine, VMEM), (w1_other, VMEM), (depth_kernel, HBM)],
        "gate_conv",
        [
            ((2, zs, 2, depth, 2 * width), BF),
            ((taps, width), F32),
            ((length + 32, width), F32),
            ((blocks, records, local_len, width), BF),
            ((records, length, 2 * width), F32),
            ((records, length, width), BF),
        ],
        1 + 3 * records,
    )

    conv_rows = lax.all_to_all(conv, CTX, 0, 0, tiled=True).reshape(blocks, rows, width)
    all_a, conv_rows = barrier((all_a, conv_rows))
    other_a = swap_core(all_a)
    shard_b, all_a = barrier((shard_b, all_a))
    all_b = lax.all_gather(shard_b, "z", axis=0, tiled=False)

    sent, residual, grad_conv = run(
        token_body,
        [
            ((blocks, rows, model), BF, HBM),
            ((rows, model), BF, HBM),
            ((blocks, rows, width), BF, HBM),
        ],
        [
            (conv_rows, HBM), (all_a, HBM), (other_a, ANY), (x, HBM), (cot, HBM), (gains[1], HBM),
            (gains[2], HBM),
        ],
        "token_rows",
        [
            ((blocks, rows, width), BF),
            ((2, zs, 2, depth, model), BF),
            ((rows, model), BF),
            ((rows, model), BF),
            ((1, model), F32),
            ((1, model), F32),
            ((rows, model), BF),
            ((rows, model), BF),
            ((blocks, rows, width), BF),
        ],
        blocks + 11,
    )
    grad_conv = lax.all_to_all(grad_conv, CTX, 0, 0, tiled=True)
    sent, grad_conv = barrier((sent, grad_conv))
    grad_conv = grad_conv.reshape(blocks, records, local_len, width)
    attn_in = lax.all_to_all(sent, CTX, 0, 0, tiled=True)
    attn_in = attn_in.reshape(blocks, records, local_len, model)

    tall = depth + 16
    half_share = (2, zs, depth, 2 * width)
    back, keep, send, gk = run(
        functools.partial(back_body, taps),
        [
            ((blocks, 3 * rows, width), BF, HBM),
            (half_share, BF, HBM),
            (half_share, BF, HBM),
            ((16, 2 * width), F32, HBM),
        ],
        [
            (frames, SMEM), (grad_conv, HBM), (normed, VMEM), (hidden, HBM), (gated, HBM),
            (depth_kernel, HBM),
        ],
        "conv_back",
        [
            ((blocks, records, local_len, width), BF),
            ((taps, width), F32),
            ((records, length, 2 * width), F32),
            ((records, length, width), BF),
            ((length + 32, width), F32),
            ((length + 32, width), F32),
            ((length, 2 * width), BF),
            ((2, zs, 2, depth, 2 * width), BF),
            ((2, zs, 2, depth, 2 * width), F32),
            ((32, 8, width), F32),
            ((blocks, 2 * rows, width), BF),
            ((16, 2 * width), F32),
        ],
        7 + 2 * records,
    )

    chunk = (2, 2 * tall, width)
    chunks = run(
        pair_body,
        [(chunk, BF, HBM)] * zs,
        [(keep, HBM), (swap_core(send), VMEM), (gk, HBM), (swap_core(gk), VMEM)],
        "pair_sum",
        [
            (half_share, BF),
            ((16, 2 * width), F32),
            (half_share, BF),
            ((zs,) + chunk, BF),
        ],
        zs + 2,
    )
    sums = [chunks[0]] + [pair_z(chunks[s], s) for s in range(1, zs)]
    attn_in, *sums[1:3] = barrier((attn_in, *sums[1:3]))
    (back,) = run(
        functools.partial(heads_body, head_dim),
        [(back.shape, BF, HBM)],
        [(frames, SMEM), (attn_in, VMEM), (all_a, HBM), (other_a, ANY), (back, HBM)],
        "heads",
        [((2, zs, 2, depth, 3 * width), BF), ((blocks, rows, width), BF)],
        5,
        {4: 0},
    )
    keep, send = run(
        sum_body,
        [(chunk[1:], BF, HBM)] * 2,
        [(one, ANY) for one in sums[:3]] + [(one, VMEM) for one in sums[3:]],
        "share_sum",
        [((zs,) + chunk, BF), (chunk, BF)],
        zs + 2,
    )
    all_b, back, keep, send = barrier((all_b, back, keep, send))
    (pair,) = run(
        spread_body,
        [((blocks,) + chunk, BF, HBM)],
        [(keep, HBM), (swap_yh(send), ANY)],
        "spread",
        [(chunk, BF)],
        blocks + 2,
    )

    other_b = swap_core(all_b)
    back = lax.all_to_all(back, CTX, 0, 0, tiled=True)
    pair, back = barrier((pair, back))
    pair = lax.all_to_all(pair, CTX, 0, 0, tiled=True)
    result, grad_in = run(
        result_body,
        [((rows, model), BF, HBM)] * 2,
        [
            (frames, SMEM), (back, VMEM), (all_b, HBM), (other_b, ANY), (residual, HBM), (x, HBM),
            (cot, HBM), (gains[0], HBM),
        ],
        "result_rows",
        [((2, zs, 2, depth, model), BF)] * 3
        + [((rows, model), BF)] * 3
        + [((1, model), F32)]
        + [((rows, model), BF)] * 2,
        18,
    )
    pair, result, grad_in = barrier((pair, result, grad_in))
    grad_first, grad_kernel = run(
        lay_body,
        [((depth, 2 * model), F32, HBM), ((taps, model), F32, HBM)],
        [(pair, VMEM)],
        "lay_out",
        [((depth, 2 * model), F32), ((taps, model), F32)],
        2,
    )
    return (
        result.reshape(records, local_len, model),
        grad_in.reshape(records, local_len, model),
        grad_first,
        grad_kernel,
    )


def solution(mesh):
    dp, ctx = mesh.devices.shape
    split = Mesh(
        mesh.devices.reshape(2, dp // 4, 2, 2, ctx // 2), ("yh", "z", "core", "yl", "x")
    )
    tokens = P(DP, CTX, None)
    placed = (
        tokens,
        P(DP),
        P(),
        P(DP, None),
        P(),
        P(),
        P(DP, None),
        P(),
        P(DP, None),
        P(DP, None),
        tokens,
    )
    return jax.shard_map(
        local,
        mesh=split,
        in_specs=placed,
        out_specs=(tokens, tokens, P(DP, None), P()),
        check_vma=False,
    )
```

```python
import functools

import jax
import jax.numpy as jnp
from jax import lax
from jax.experimental import pallas as pl
from jax.experimental.pallas import tpu as pltpu
from jax.sharding import Mesh
from jax.sharding import PartitionSpec as P

HEADS = 16
EPSILON = 1e-05
BF = jnp.bfloat16
F32 = jnp.float32

DP = ("yh", "z", "core")
CTX = ("yl", "x")

HBM, VMEM, SMEM, ANY = pltpu.HBM, pltpu.VMEM, pltpu.SMEM, pl.ANY


def run(body, outs, ins, name, scratch=(), sems=0, alias=None, mib=36):
    scratch = [pltpu.VMEM(*one) for one in scratch]
    if sems:
        scratch.append(pltpu.SemaphoreType.DMA((sems,)))
    return pl.pallas_call(
        body,
        out_shape=tuple(o[2](o[0], o[1]) for o in outs),
        in_specs=[pl.BlockSpec(memory_space=space) for _, space in ins],
        out_specs=tuple(pl.BlockSpec(memory_space=o[2]) for o in outs),
        scratch_shapes=scratch,
        input_output_aliases=alias or {},
        compiler_params=pltpu.CompilerParams(vmem_limit_bytes=mib << 20),
        name=name,
    )(
        *[
            v if space in (SMEM, ANY) else pltpu.with_memory_space_constraint(v, space)
            for v, space in ins
        ]
    )


class Copies:
    def __init__(self, sems):
        self.sems, self.used = sems, 0

    def start(self, src, dst):
        one = pltpu.make_async_copy(src, dst, self.sems.at[self.used])
        self.used += 1
        one.start()
        return one


def wait(*copies):
    for one in copies:
        one.wait()


def centred(values):
    centre = values - jnp.mean(values, -1, keepdims=True)
    spread = jnp.mean(centre * centre, -1, keepdims=True)
    return centre, lax.rsqrt(spread + EPSILON)


def norm_pull(cot, centre, inv):
    xhat = centre * inv
    return inv * (
        cot - jnp.mean(cot, -1, keepdims=True) - xhat * jnp.mean(cot * xhat, -1, keepdims=True)
    )


def dot(a, b):
    return jnp.dot(a, b, preferred_element_type=F32)


def dot_t(a, b):
    return lax.dot_general(a, b, (((1,), (1,)), ((), ())), preferred_element_type=F32)


def sigmoid(v):
    return jax.nn.sigmoid(v)


def ctx_index():
    return lax.axis_index("yl") * lax.axis_size("x") + lax.axis_index("x")


def lanes(block, width):
    return pl.ds(pl.multiple_of(block * width, width), width)


def cut_body(blocks, w2, wq, w1, own, w1_own, beside, own_s, w1_s, beside_s, sems):
    model = w2.shape[1]
    width = model // blocks
    ctx = ctx_index()
    copies = Copies(sems)
    going = []
    for dst, block in ((beside_s, lax.rem(ctx + blocks // 2, blocks)), (own_s, ctx)):
        going.append(copies.start(w2, dst.at[:, :model]))
        for part in range(3):
            lo = model + part * width
            going.append(
                copies.start(
                    wq.at[:, lanes(part * blocks + block, width)], dst.at[:, lo : lo + width]
                )
            )
        to, lo = (beside_s, model + 3 * width) if dst is beside_s else (w1_s, 0)
        for part in range(2):
            at = lo + part * width
            going.append(
                copies.start(
                    w1.at[:, lanes(part * blocks + block, width)], to.at[:, at : at + width]
                )
            )
    wait(*going)
    wait(
        copies.start(beside_s, beside), copies.start(own_s, own), copies.start(w1_s, w1_own)
    )


def pack_body(wp, w1, out, out_s, sems):
    model = wp.shape[1]
    copies = Copies(sems)
    wait(copies.start(wp, out_s.at[:, :model]), copies.start(w1, out_s.at[:, model:]))
    wait(copies.start(out_s, out))


def lay_rows(copies, lo, wide, mine, other, out):
    core, yh = lax.axis_index("core"), lax.axis_index("yh")
    return [
        copies.start(src.at[:, slot, :, lo : lo + wide], out.at[side, :, owner])
        for src, owner in ((mine, core), (other, 1 - core))
        for slot, side in ((0, yh), (1, 1 - yh))
    ]


def first_body(x, gain, out, x_s, g_s, n_s, sems):
    copies = Copies(sems)
    wait(copies.start(x, x_s), copies.start(gain, g_s))
    centre, inv = centred(x_s[...].astype(F32))
    n_s[...] = (centre * inv * g_s[...]).astype(BF)
    wait(*[copies.start(n_s, out.at[i]) for i in range(out.shape[0])])


def gate_body(
    taps, frames, x, wm, wo, k, conv, hid, gated, w_s, k_s, pad_s, conv_s, hid_s, gated_s, sems
):
    blocks, records, local, model = x.shape
    length = blocks * local
    width = k_s.shape[1]
    core, yh, z = lax.axis_index("core"), lax.axis_index("yh"), lax.axis_index("z")
    copies = Copies(sems)
    get_k = copies.start(k.at[:, lanes(ctx_index(), width)], k_s)
    for s in range(wm.shape[0]):
        for slot, side in ((0, yh), (1, 1 - yh)):
            w_s[side, z ^ s, core] = wm[s, slot]
            w_s[side, z ^ s, 1 - core] = wo[s, slot]
    zeros = jnp.zeros((16, width), F32)
    pad_s[0:16] = zeros
    pad_s[16 + length : 32 + length] = zeros
    going = []
    for rec in range(records):
        hidden = dot(x[:, rec].reshape(length, model), w_s[...].reshape(model, 2 * width))
        hid_s[rec] = hidden
        going.append(copies.start(hid_s.at[rec], hid.at[rec]))
        here = lax.broadcasted_iota(jnp.int32, (length, width), 0) < frames[rec]
        value = jnp.where(here, hidden[:, :width] * sigmoid(hidden[:, width:]), 0.0).astype(BF)
        gated_s[rec] = value
        going.append(copies.start(gated_s.at[rec], gated.at[rec]))
        pad_s[16 : 16 + length] = value.astype(F32)
        if rec == 0:
            wait(get_k)
        for b in range(blocks):
            total = jnp.zeros((local, width), F32)
            for j in range(taps):
                at = b * local + j + 1
                total = total + k_s[j : j + 1, :] * pad_s[at : at + local, :]
            conv_s[b, rec] = total.astype(BF)
        going.append(copies.start(conv_s.at[:, rec], conv.at[:, rec]))
    wait(*going)


def pull_body(c, mine, other, go, g2, gc, swished, c_s, w2_s, go_s, g2_s, gc_s, sw_s, sems):
    rows, model = go_s.shape
    blocks = c.shape[0]
    width = model // blocks
    copies = Copies(sems)
    get_c = copies.start(c, c_s)
    get_gain = copies.start(g2, g2_s)
    get_go = copies.start(go, go_s)
    get_w2 = lay_rows(copies, 0, model, mine, other, w2_s)
    wait(get_c, get_gain)
    conv = jnp.concatenate([c_s[i] for i in range(blocks)], 1).astype(F32)
    centre, inv = centred(conv)
    gain = g2_s[...]
    normal = centre * inv * gain
    opening = sigmoid(normal)
    sw_s[...] = (normal * opening).astype(BF)
    going = [copies.start(sw_s, swished)]
    slope = opening + normal * opening * (1.0 - opening)
    wait(get_go, *get_w2)
    back_two = dot_t(go_s[...], w2_s[...].reshape(model, model))
    grad_conv = norm_pull(back_two * slope * gain, centre, inv).astype(BF)
    for i in range(blocks):
        gc_s[i] = grad_conv[:, i * width : (i + 1) * width]
    wait(*going, copies.start(gc_s, gc))


def residual_body(swished, mine, other, x, ga, sent, res, sw_s, w2_s, x_s, ga_s, n_s, res_s, sems):
    model = x_s.shape[1]
    copies = Copies(sems)
    get_sw = copies.start(swished, sw_s)
    get_x = copies.start(x, x_s)
    get_ga = copies.start(ga, ga_s)
    get_w2 = lay_rows(copies, 0, model, mine, other, w2_s)
    wait(get_sw, get_x, get_ga, *get_w2)
    summed = x_s[...].astype(F32) + dot(sw_s[...], w2_s[...].reshape(model, model))
    residual = summed.astype(BF)
    res_s[...] = residual
    going = [copies.start(res_s, res)]
    centre, inv = centred(residual.astype(F32))
    n_s[...] = (centre * inv * ga_s[...]).astype(BF)
    wait(*going, *[copies.start(n_s, sent.at[i]) for i in range(sent.shape[0])])


def back_body(
    taps, frames, gc, x, hid, gated, k, mine, other, back, keep, send, gk_out, wq,
    gc_s, k_s, hid_s, gated_s, pad_s, gpad_s, gh_s, both_s, gf_s, gk_s, out_s, gko_s, wq_s, sems,
):
    blocks, records, local, model = x.shape
    length = blocks * local
    rows = records * local
    width = k_s.shape[1]
    core = lax.axis_index("core")
    copies = Copies(sems)
    get_gc = copies.start(gc, gc_s)
    get_k = copies.start(k.at[:, lanes(ctx_index(), width)], k_s)
    get_gated = copies.start(gated, gated_s)
    get_hid = copies.start(hid, hid_s)
    get_wq = lay_rows(copies, model, wq_s.shape[4], mine, other, wq_s)
    gk_s[...] = jnp.zeros_like(gk_s)
    zeros = jnp.zeros((16, width), F32)
    for ref in (pad_s, gpad_s):
        ref[0:16] = zeros
        ref[16 + length : 32 + length] = zeros
    going = []
    wait(get_k, get_gc, get_gated)
    for rec in range(records):
        pad_s[16 : 16 + length] = gc_s[:, rec].reshape(length, width).astype(F32)
        gpad_s[16 : 16 + length] = gated_s[rec].astype(F32)
        for b in range(blocks):
            base = b * local
            total = jnp.zeros((local, width), F32)
            own = pad_s[16 + base : 16 + base + local, :]
            for j in range(taps):
                at = base + taps - j
                total = total + k_s[j : j + 1, :] * pad_s[at : at + local, :]
                at = base + j + 1
                term = (gpad_s[at : at + local, :] * own).reshape(local // 8, 8, width)
                gk_s[j] += jnp.sum(term, 0)
            at = lax.broadcasted_iota(jnp.int32, (local, width), 0) + base
            grad_gated = jnp.where(at < frames[rec], total, 0.0)
            if rec == 0 and b == 0:
                wait(get_hid)
            linear = hid_s[rec, base : base + local, :width]
            opening = sigmoid(hid_s[rec, base : base + local, width:])
            first = grad_gated * opening
            second = (first * linear * (1.0 - opening)).astype(BF)
            first = first.astype(BF)
            gh_s[base : base + local, :width] = first
            gh_s[base : base + local, width:] = second
            out_s[b, rec * local : (rec + 1) * local] = first
            out_s[b, rows + rec * local : rows + (rec + 1) * local] = second
        for part in range(2):
            at = part * rows + rec * local
            going.append(
                copies.start(out_s.at[:, at : at + local], back.at[:, at : at + local])
            )
        grad_first = lax.dot_general(
            x[:, rec].reshape(length, model),
            gh_s[...],
            (((0,), (0,)), ((), ())),
            preferred_element_type=F32,
        ).reshape(gf_s.shape)
        if rec == 0:
            gf_s[...] = grad_first
        else:
            both_s[...] = (gf_s[...] + grad_first).astype(BF)
    wait(*get_wq)
    going.append(copies.start(wq_s, wq))
    gk = jnp.sum(gk_s[...], 1)
    half = gko_s.shape[0]
    gko_s[:, :width] = gk[:half]
    gko_s[:, width:] = gk[half:]
    wait(
        copies.start(both_s.at[:, :, 1 - core], send),
        copies.start(gko_s, gk_out),
        copies.start(both_s.at[:, :, core], keep),
        *going,
    )


def pair_body(keep, recv, gk, gkr, *refs):
    zs = len(refs) - 5
    outs, (keep_s, gk_s, both_s, out_s, sems) = refs[:zs], refs[zs:]
    depth, wide = keep_s.shape[2:]
    half = wide // 2
    copies = Copies(sems)
    wait(copies.start(keep, keep_s), copies.start(gk, gk_s))
    both_s[...] = (keep_s[...].astype(F32) + recv[...].astype(F32)).astype(BF)
    gk_sum = (gk_s[...] + gkr[...]).astype(BF)
    tall = out_s.shape[2] // 2
    z = lax.axis_index("z")
    going = []
    for s in range(zs):
        for side in range(2):
            part = both_s[side, z ^ s]
            for h in range(2):
                at = h * tall
                out_s[s, side, at : at + depth] = part[:, h * half : (h + 1) * half]
                out_s[s, side, at + depth : at + tall] = gk_sum[:, h * half : (h + 1) * half]
        going.append(copies.start(out_s.at[s], outs[s]))
    wait(*going)


def sum_body(*refs):
    keep, send, parts_s, total_s, sems = refs[-5:]
    copies = Copies(sems)
    wait(*[copies.start(ref, parts_s.at[i]) for i, ref in enumerate(refs[:-5])])
    total_s[...] = jnp.sum(parts_s[...].astype(F32), 0).astype(BF)
    yh = lax.axis_index("yh")
    wait(copies.start(total_s.at[1 - yh], send), copies.start(total_s.at[yh], keep))


def spread_body(keep, recv, out, pair_s, sems):
    copies = Copies(sems)
    wait(copies.start(keep, pair_s.at[0]), copies.start(recv, pair_s.at[1]))
    wait(*[copies.start(pair_s, out.at[i]) for i in range(out.shape[0])])


def heads_body(head_dim, frames, x, wq, held, back, w, att_s, sems):
    del held
    copies = Copies(sems)
    get_w = [copies.start(wq, w)]
    blocks, records, local, model = x.shape
    length = blocks * local
    width = model // blocks
    rows = min(256, length)
    lane = lax.broadcasted_iota(jnp.int32, (rows, width), 1)
    scaling = head_dim**-0.5
    wait(*get_w)
    for rec in range(records):
        packed = dot(x[:, rec].reshape(length, model), w[...].reshape(model, 3 * width))
        packed = packed.astype(BF)
        q = packed[:, :width] * jnp.asarray(scaling, BF)
        k = packed[:, width : 2 * width]
        v = jnp.concatenate([packed[:, 2 * width :], jnp.ones((length, width), BF)], 1)
        bias = jnp.where(
            lax.broadcasted_iota(jnp.int32, (1, length), 1) < frames[rec], 0.0, -1e30
        )
        for r in range(0, length, rows):
            qr = q[r : r + rows]
            attended = jnp.zeros((rows, width), F32)
            for h in range(width // head_dim):
                here = (lane >= h * head_dim) & (lane < (h + 1) * head_dim)
                scores = dot_t(jnp.where(here, qr, jnp.zeros_like(qr)), k) + bias
                top = jnp.max(scores, -1, keepdims=True)
                both = dot(jnp.exp(scores - top).astype(BF), v)
                attended = jnp.where(here, both[:, :width] / both[:, width:], attended)
            got = attended.astype(BF).reshape(rows // local, local, width)
            att_s[r // local : (r + rows) // local, rec * local : (rec + 1) * local] = got
    tall = records * local
    wait(copies.start(att_s, back.at[:, 2 * tall : 3 * tall]))


def result_body(
    frames, a, mine, other, res, x, go, g1, out, gin,
    wp_s, w1_s, w2_s, res_s, x_s, go_s, g1_s, out_s, gin_s, sems,
):
    rows, model = x_s.shape
    blocks = a.shape[0]
    copies = Copies(sems)
    get_w = [
        lay_rows(copies, i * model, model, mine, other, one)
        for i, one in enumerate((wp_s, w1_s, w2_s))
    ]
    get_res = copies.start(res, res_s)
    get_x = copies.start(x, x_s)
    get_go = copies.start(go, go_s)
    get_g1 = copies.start(g1, g1_s)
    attended = jnp.concatenate([a[i, 2 * rows : 3 * rows] for i in range(blocks)], 1)
    linear = jnp.concatenate([a[i, :rows] for i in range(blocks)], 1)
    gating = jnp.concatenate([a[i, rows : 2 * rows] for i in range(blocks)], 1)
    wait(*get_w[0])
    projected = dot(attended, wp_s[...].reshape(model, model))
    records = frames.shape[0]
    local = rows // records
    at = lax.broadcasted_iota(jnp.int32, (local, model), 0) + ctx_index() * local
    present = jnp.concatenate([(at < frames[r]).astype(F32) for r in range(records)], 0)
    wait(get_res)
    out_s[...] = (res_s[...].astype(F32) + present * projected).astype(BF)
    put_out = copies.start(out_s, out)
    wait(*get_w[1])
    back_one = dot_t(linear, w1_s[...].reshape(model, model))
    wait(*get_w[2])
    back_one = back_one + dot_t(gating, w2_s[...].reshape(model, model))
    wait(get_x, get_go, get_g1)
    centre, inv = centred(x_s[...].astype(F32))
    pulled = norm_pull(back_one * g1_s[...], centre, inv)
    gin_s[...] = (go_s[...].astype(F32) + pulled).astype(BF)
    wait(put_out, copies.start(gin_s, gin))


def lay_body(a, gf, gk, gf_s, gk_s, sems):
    blocks = a.shape[0]
    depth, taps = gf_s.shape[0], gk_s.shape[0]
    model = gk_s.shape[1]
    width = model // blocks
    tall = a.shape[2] // 2
    half = tall - depth
    for i in range(blocks):
        lo = i * width
        total = a[i, 0].astype(F32) + a[(i + blocks // 2) % blocks, 1].astype(F32)
        for h in range(2):
            at = h * tall
            gf_s[:, h * model + lo : h * model + lo + width] = total[at : at + depth]
            count = min(half, taps - h * half)
            gk_s[h * half : h * half + count, lo : lo + width] = total[
                at + depth : at + depth + count
            ]
    copies = Copies(sems)
    wait(copies.start(gf_s, gf), copies.start(gk_s, gk))


def swap_core(v):
    return lax.ppermute(v, "core", [(0, 1), (1, 0)])


def swap_yh(v):
    return lax.ppermute(v, ("yh", "yl"), [(0, 3), (3, 0), (1, 2), (2, 1)])


def pair_z(v, by):
    return lax.ppermute(v, "z", [(i, i ^ by) for i in range(lax.axis_size("z"))])


def local(
    inputs,
    frames,
    gain_first,
    w_first,
    depth_kernel,
    gain_second,
    w_second,
    gain_attn,
    w_qkv,
    w_proj,
    grad_out,
):
    records, local_len, model = inputs.shape
    taps = depth_kernel.shape[0]
    blocks = lax.axis_size(CTX)
    zs = lax.axis_size("z")
    depth = w_first.shape[0]
    width = model // blocks
    length = blocks * local_len
    rows = records * local_len
    head_dim = model // HEADS
    barrier = lax.optimization_barrier
    x = inputs.reshape(rows, model)
    cot = grad_out.reshape(rows, model)
    gains = [g.reshape(1, model) for g in (gain_first, gain_second, gain_attn)]

    part = model + 3 * width
    own, w1_own, beside = run(
        functools.partial(cut_body, blocks),
        [
            ((depth, part), BF, HBM),
            ((depth, 2 * width), BF, HBM),
            ((depth, part + 2 * width), BF, HBM),
        ],
        [(w_second, HBM), (w_qkv, HBM), (w_first, HBM)],
        "cut",
        [((depth, part), BF), ((depth, 2 * width), BF), ((depth, part + 2 * width), BF)],
        15,
    )
    beside = swap_yh(beside)
    (sent,) = run(
        first_body,
        [((blocks, rows, model), BF, HBM)],
        [(x, HBM), (gains[0], HBM)],
        "first_norm",
        [((rows, model), BF), ((1, model), F32), ((rows, model), BF)],
        blocks + 2,
    )
    beside, _ = barrier((beside, sent))
    shard_a = jnp.stack([own, beside[:, :part]])
    all_a = lax.all_gather(shard_a, "z", axis=0, tiled=False)
    normed = lax.all_to_all(sent, CTX, 0, 0, tiled=True).reshape(blocks, records, local_len, model)

    w1_part = jnp.stack([w1_own, beside[:, part:]])
    two = jnp.stack([w1_part, pair_z(w1_part, 1)])
    w1_mine = jnp.concatenate([two] + [pair_z(two, s) for s in range(2, zs, 2)])
    w1_other = swap_core(w1_mine)

    (own_b,) = run(
        pack_body,
        [((depth, 3 * model), BF, HBM)],
        [(w_proj, HBM), (w_first, HBM)],
        "pack",
        [((depth, 3 * model), BF)],
        3,
    )
    shard_b = jnp.stack([own_b, swap_yh(own_b)])
    conv, hidden, gated = run(
        functools.partial(gate_body, taps),
        [
            ((blocks, records, local_len, width), BF, HBM),
            ((records, length, 2 * width), F32, HBM),
            ((records, length, width), BF, HBM),
        ],
        [(frames, SMEM), (normed, VMEM), (w1_mine, VMEM), (w1_other, VMEM), (depth_kernel, HBM)],
        "gate_conv",
        [
            ((2, zs, 2, depth, 2 * width), BF),
            ((taps, width), F32),
            ((length + 32, width), F32),
            ((blocks, records, local_len, width), BF),
            ((records, length, 2 * width), F32),
            ((records, length, width), BF),
        ],
        1 + 3 * records,
    )

    conv_rows = lax.all_to_all(conv, CTX, 0, 0, tiled=True).reshape(blocks, rows, width)
    all_a, conv_rows = barrier((all_a, conv_rows))
    other_a = swap_core(all_a)
    shard_b, all_a = barrier((shard_b, all_a))
    all_b = lax.all_gather(shard_b, "z", axis=0, tiled=False)

    w2_shape = (2, zs, 2, depth, model)
    grad_conv, swished = run(
        pull_body,
        [((blocks, rows, width), BF, HBM), ((rows, model), BF, HBM)],
        [(conv_rows, HBM), (all_a, HBM), (other_a, ANY), (cot, HBM), (gains[1], HBM)],
        "token_pull",
        [
            ((blocks, rows, width), BF),
            (w2_shape, BF),
            ((rows, model), BF),
            ((1, model), F32),
            ((blocks, rows, width), BF),
            ((rows, model), BF),
        ],
        9,
    )
    sent, residual = run(
        residual_body,
        [((blocks, rows, model), BF, HBM), ((rows, model), BF, HBM)],
        [(swished, HBM), (all_a, HBM), (other_a, ANY), (x, HBM), (gains[2], HBM)],
        "token_residual",
        [
            ((rows, model), BF),
            (w2_shape, BF),
            ((rows, model), BF),
            ((1, model), F32),
            ((rows, model), BF),
            ((rows, model), BF),
        ],
        blocks + 8,
    )
    grad_conv = lax.all_to_all(grad_conv, CTX, 0, 0, tiled=True)
    sent, grad_conv = barrier((sent, grad_conv))
    grad_conv = grad_conv.reshape(blocks, records, local_len, width)
    attn_in = lax.all_to_all(sent, CTX, 0, 0, tiled=True)
    attn_in = attn_in.reshape(blocks, records, local_len, model)

    tall = depth + 16
    half_share = (2, zs, depth, 2 * width)
    back, keep, send, gk, wq_rows = run(
        functools.partial(back_body, taps),
        [
            ((blocks, 3 * rows, width), BF, HBM),
            (half_share, BF, HBM),
            (half_share, BF, HBM),
            ((16, 2 * width), F32, HBM),
            ((2, zs, 2, depth, 3 * width), BF, HBM),
        ],
        [
            (frames, SMEM), (grad_conv, HBM), (normed, VMEM), (hidden, HBM), (gated, HBM),
            (depth_kernel, HBM), (all_a, HBM), (other_a, ANY),
        ],
        "conv_back",
        [
            ((blocks, records, local_len, width), BF),
            ((taps, width), F32),
            ((records, length, 2 * width), F32),
            ((records, length, width), BF),
            ((length + 32, width), F32),
            ((length + 32, width), F32),
            ((length, 2 * width), BF),
            ((2, zs, 2, depth, 2 * width), BF),
            ((2, zs, 2, depth, 2 * width), F32),
            ((32, 8, width), F32),
            ((blocks, 2 * rows, width), BF),
            ((16, 2 * width), F32),
            ((2, zs, 2, depth, 3 * width), BF),
        ],
        12 + 2 * records,
    )

    chunk = (2, 2 * tall, width)
    chunks = run(
        pair_body,
        [(chunk, BF, HBM)] * zs,
        [(keep, HBM), (swap_core(send), VMEM), (gk, HBM), (swap_core(gk), VMEM)],
        "pair_sum",
        [
            (half_share, BF),
            ((16, 2 * width), F32),
            (half_share, BF),
            ((zs,) + chunk, BF),
        ],
        zs + 2,
    )
    sums = [chunks[0]] + [pair_z(chunks[s], s) for s in range(1, zs)]
    attn_in, *sums[1:3] = barrier((attn_in, *sums[1:3]))
    (back,) = run(
        functools.partial(heads_body, head_dim),
        [(back.shape, BF, HBM)],
        [(frames, SMEM), (attn_in, VMEM), (wq_rows, HBM), (back, HBM)],
        "heads",
        [((2, zs, 2, depth, 3 * width), BF), ((blocks, rows, width), BF)],
        2,
        {3: 0},
    )
    keep, send = run(
        sum_body,
        [(chunk[1:], BF, HBM)] * 2,
        [(one, ANY) for one in sums[:3]] + [(one, VMEM) for one in sums[3:]],
        "share_sum",
        [((zs,) + chunk, BF), (chunk, BF)],
        zs + 2,
    )
    all_b, back, keep, send = barrier((all_b, back, keep, send))
    (pair,) = run(
        spread_body,
        [((blocks,) + chunk, BF, HBM)],
        [(keep, HBM), (swap_yh(send), ANY)],
        "spread",
        [(chunk, BF)],
        blocks + 2,
    )

    other_b = swap_core(all_b)
    back = lax.all_to_all(back, CTX, 0, 0, tiled=True)
    pair, back = barrier((pair, back))
    pair = lax.all_to_all(pair, CTX, 0, 0, tiled=True)
    result, grad_in = run(
        result_body,
        [((rows, model), BF, HBM)] * 2,
        [
            (frames, SMEM), (back, VMEM), (all_b, HBM), (other_b, ANY), (residual, HBM), (x, HBM),
            (cot, HBM), (gains[0], HBM),
        ],
        "result_rows",
        [((2, zs, 2, depth, model), BF)] * 3
        + [((rows, model), BF)] * 3
        + [((1, model), F32)]
        + [((rows, model), BF)] * 2,
        18,
    )
    pair, result, grad_in = barrier((pair, result, grad_in))
    grad_first, grad_kernel = run(
        lay_body,
        [((depth, 2 * model), F32, HBM), ((taps, model), F32, HBM)],
        [(pair, VMEM)],
        "lay_out",
        [((depth, 2 * model), F32), ((taps, model), F32)],
        2,
    )
    return (
        result.reshape(records, local_len, model),
        grad_in.reshape(records, local_len, model),
        grad_first,
        grad_kernel,
    )


def solution(mesh):
    dp, ctx = mesh.devices.shape
    split = Mesh(
        mesh.devices.reshape(2, dp // 4, 2, 2, ctx // 2), ("yh", "z", "core", "yl", "x")
    )
    tokens = P(DP, CTX, None)
    placed = (
        tokens,
        P(DP),
        P(),
        P(DP, None),
        P(),
        P(),
        P(DP, None),
        P(),
        P(DP, None),
        P(DP, None),
        tokens,
    )
    return jax.shard_map(
        local,
        mesh=split,
        in_specs=placed,
        out_specs=(tokens, tokens, P(DP, None), P()),
        check_vma=False,
    )
```

```python
import functools

import jax
import jax.numpy as jnp
from jax import lax
from jax.experimental import pallas as pl
from jax.experimental.pallas import tpu as pltpu
from jax.sharding import Mesh
from jax.sharding import PartitionSpec as P

HEADS = 16
EPSILON = 1e-05
BF = jnp.bfloat16
F32 = jnp.float32

DP = ("yh", "z", "core")
CTX = ("yl", "x")

HBM, VMEM, SMEM, ANY = pltpu.HBM, pltpu.VMEM, pltpu.SMEM, pl.ANY


def run(body, outs, ins, name, scratch=(), sems=0, alias=None, mib=36):
    scratch = [pltpu.VMEM(*one) for one in scratch]
    if sems:
        scratch.append(pltpu.SemaphoreType.DMA((sems,)))
    return pl.pallas_call(
        body,
        out_shape=tuple(o[2](o[0], o[1]) for o in outs),
        in_specs=[pl.BlockSpec(memory_space=space) for _, space in ins],
        out_specs=tuple(pl.BlockSpec(memory_space=o[2]) for o in outs),
        scratch_shapes=scratch,
        input_output_aliases=alias or {},
        compiler_params=pltpu.CompilerParams(vmem_limit_bytes=mib << 20),
        name=name,
    )(
        *[
            v if space in (SMEM, ANY) else pltpu.with_memory_space_constraint(v, space)
            for v, space in ins
        ]
    )


class Copies:
    def __init__(self, sems):
        self.sems, self.used = sems, 0

    def start(self, src, dst):
        one = pltpu.make_async_copy(src, dst, self.sems.at[self.used])
        self.used += 1
        one.start()
        return one


def wait(*copies):
    for one in copies:
        one.wait()


def centred(values):
    centre = values - jnp.mean(values, -1, keepdims=True)
    spread = jnp.mean(centre * centre, -1, keepdims=True)
    return centre, lax.rsqrt(spread + EPSILON)


def norm_pull(cot, centre, inv):
    xhat = centre * inv
    return inv * (
        cot - jnp.mean(cot, -1, keepdims=True) - xhat * jnp.mean(cot * xhat, -1, keepdims=True)
    )


def dot(a, b):
    return jnp.dot(a, b, preferred_element_type=F32)


def dot_t(a, b):
    return lax.dot_general(a, b, (((1,), (1,)), ((), ())), preferred_element_type=F32)


def sigmoid(v):
    return jax.nn.sigmoid(v)


def ctx_index():
    return lax.axis_index("yl") * lax.axis_size("x") + lax.axis_index("x")


def lanes(block, width):
    return pl.ds(pl.multiple_of(block * width, width), width)


def cut_body(blocks, w2, wq, w1, own, w1_own, beside, own_s, w1_s, beside_s, sems):
    model = w2.shape[1]
    width = model // blocks
    ctx = ctx_index()
    copies = Copies(sems)
    going = []
    for dst, block in ((beside_s, lax.rem(ctx + blocks // 2, blocks)), (own_s, ctx)):
        going.append(copies.start(w2, dst.at[:, :model]))
        for part in range(3):
            lo = model + part * width
            going.append(
                copies.start(
                    wq.at[:, lanes(part * blocks + block, width)], dst.at[:, lo : lo + width]
                )
            )
        to, lo = (beside_s, model + 3 * width) if dst is beside_s else (w1_s, 0)
        for part in range(2):
            at = lo + part * width
            going.append(
                copies.start(
                    w1.at[:, lanes(part * blocks + block, width)], to.at[:, at : at + width]
                )
            )
    wait(*going)
    wait(
        copies.start(beside_s, beside), copies.start(own_s, own), copies.start(w1_s, w1_own)
    )


def pack_body(wp, w1, out, out_s, sems):
    model = wp.shape[1]
    copies = Copies(sems)
    wait(copies.start(wp, out_s.at[:, :model]), copies.start(w1, out_s.at[:, model:]))
    wait(copies.start(out_s, out))


def lay_rows(copies, lo, wide, mine, other, out):
    core, yh = lax.axis_index("core"), lax.axis_index("yh")
    return [
        copies.start(src.at[:, slot, :, lo : lo + wide], out.at[side, :, owner])
        for src, owner in ((mine, core), (other, 1 - core))
        for slot, side in ((0, yh), (1, 1 - yh))
    ]


def first_body(x, gain, out, x_s, g_s, n_s, sems):
    copies = Copies(sems)
    wait(copies.start(x, x_s), copies.start(gain, g_s))
    centre, inv = centred(x_s[...].astype(F32))
    n_s[...] = (centre * inv * g_s[...]).astype(BF)
    wait(*[copies.start(n_s, out.at[i]) for i in range(out.shape[0])])


def gate_body(
    taps, frames, x, wm, wo, k, conv, hid, gated, w_s, k_s, pad_s, conv_s, hid_s, gated_s, sems
):
    blocks, records, local, model = x.shape
    length = blocks * local
    width = k_s.shape[1]
    core, yh, z = lax.axis_index("core"), lax.axis_index("yh"), lax.axis_index("z")
    copies = Copies(sems)
    get_k = copies.start(k.at[:, lanes(ctx_index(), width)], k_s)
    for s in range(wm.shape[0]):
        for slot, side in ((0, yh), (1, 1 - yh)):
            w_s[side, z ^ s, core] = wm[s, slot]
            w_s[side, z ^ s, 1 - core] = wo[s, slot]
    zeros = jnp.zeros((16, width), F32)
    pad_s[0:16] = zeros
    pad_s[16 + length : 32 + length] = zeros
    going = []
    for rec in range(records):
        hidden = dot(x[:, rec].reshape(length, model), w_s[...].reshape(model, 2 * width))
        hid_s[rec] = hidden
        going.append(copies.start(hid_s.at[rec], hid.at[rec]))
        here = lax.broadcasted_iota(jnp.int32, (length, width), 0) < frames[rec]
        value = jnp.where(here, hidden[:, :width] * sigmoid(hidden[:, width:]), 0.0).astype(BF)
        gated_s[rec] = value
        going.append(copies.start(gated_s.at[rec], gated.at[rec]))
        pad_s[16 : 16 + length] = value.astype(F32)
        if rec == 0:
            wait(get_k)
        for b in range(blocks):
            total = jnp.zeros((local, width), F32)
            for j in range(taps):
                at = b * local + j + 1
                total = total + k_s[j : j + 1, :] * pad_s[at : at + local, :]
            conv_s[b, rec] = total.astype(BF)
        going.append(copies.start(conv_s.at[:, rec], conv.at[:, rec]))
    wait(*going)


def pull_body(c, mine, other, go, g2, gc, swished, c_s, w2_s, go_s, g2_s, gc_s, sw_s, sems):
    rows, model = go_s.shape
    blocks = c.shape[0]
    width = model // blocks
    copies = Copies(sems)
    get_c = copies.start(c, c_s)
    get_gain = copies.start(g2, g2_s)
    get_go = copies.start(go, go_s)
    get_w2 = lay_rows(copies, 0, model, mine, other, w2_s)
    wait(get_c, get_gain)
    conv = jnp.concatenate([c_s[i] for i in range(blocks)], 1).astype(F32)
    centre, inv = centred(conv)
    gain = g2_s[...]
    normal = centre * inv * gain
    opening = sigmoid(normal)
    sw_s[...] = (normal * opening).astype(BF)
    going = [copies.start(sw_s, swished)]
    slope = opening + normal * opening * (1.0 - opening)
    wait(get_go, *get_w2)
    back_two = dot_t(go_s[...], w2_s[...].reshape(model, model))
    grad_conv = norm_pull(back_two * slope * gain, centre, inv).astype(BF)
    for i in range(blocks):
        gc_s[i] = grad_conv[:, i * width : (i + 1) * width]
    wait(*going, copies.start(gc_s, gc))


def residual_body(swished, mine, other, x, ga, sent, res, sw_s, w2_s, x_s, ga_s, n_s, res_s, sems):
    model = x_s.shape[1]
    copies = Copies(sems)
    get_sw = copies.start(swished, sw_s)
    get_x = copies.start(x, x_s)
    get_ga = copies.start(ga, ga_s)
    get_w2 = lay_rows(copies, 0, model, mine, other, w2_s)
    wait(get_sw, get_x, get_ga, *get_w2)
    summed = x_s[...].astype(F32) + dot(sw_s[...], w2_s[...].reshape(model, model))
    residual = summed.astype(BF)
    res_s[...] = residual
    going = [copies.start(res_s, res)]
    centre, inv = centred(residual.astype(F32))
    n_s[...] = (centre * inv * ga_s[...]).astype(BF)
    wait(*going, *[copies.start(n_s, sent.at[i]) for i in range(sent.shape[0])])


def back_body(
    taps, frames, gc, x, hid, gated, k, mine, other, back, keep, send, gk_out, wq,
    gc_s, k_s, hid_s, gated_s, pad_s, gpad_s, gh_s, both_s, gf_s, gk_s, out_s, gko_s, wq_s, sems,
):
    blocks, records, local, model = x.shape
    length = blocks * local
    rows = records * local
    width = k_s.shape[1]
    core = lax.axis_index("core")
    copies = Copies(sems)
    get_gc = copies.start(gc, gc_s)
    get_k = copies.start(k.at[:, lanes(ctx_index(), width)], k_s)
    get_gated = copies.start(gated, gated_s)
    get_hid = copies.start(hid, hid_s)
    get_wq = lay_rows(copies, model, wq_s.shape[4], mine, other, wq_s)
    gk_s[...] = jnp.zeros_like(gk_s)
    zeros = jnp.zeros((16, width), F32)
    for ref in (pad_s, gpad_s):
        ref[0:16] = zeros
        ref[16 + length : 32 + length] = zeros
    going = []
    wait(get_k, get_gc, get_gated)
    for rec in range(records):
        pad_s[16 : 16 + length] = gc_s[:, rec].reshape(length, width).astype(F32)
        gpad_s[16 : 16 + length] = gated_s[rec].astype(F32)
        for b in range(blocks):
            base = b * local
            total = jnp.zeros((local, width), F32)
            own = pad_s[16 + base : 16 + base + local, :]
            for j in range(taps):
                at = base + taps - j
                total = total + k_s[j : j + 1, :] * pad_s[at : at + local, :]
                at = base + j + 1
                term = (gpad_s[at : at + local, :] * own).reshape(local // 8, 8, width)
                gk_s[j] += jnp.sum(term, 0)
            at = lax.broadcasted_iota(jnp.int32, (local, width), 0) + base
            grad_gated = jnp.where(at < frames[rec], total, 0.0)
            if rec == 0 and b == 0:
                wait(get_hid)
            linear = hid_s[rec, base : base + local, :width]
            opening = sigmoid(hid_s[rec, base : base + local, width:])
            first = grad_gated * opening
            second = (first * linear * (1.0 - opening)).astype(BF)
            first = first.astype(BF)
            gh_s[base : base + local, :width] = first
            gh_s[base : base + local, width:] = second
            out_s[b, rec * local : (rec + 1) * local] = first
            out_s[b, rows + rec * local : rows + (rec + 1) * local] = second
        for part in range(2):
            at = part * rows + rec * local
            going.append(
                copies.start(out_s.at[:, at : at + local], back.at[:, at : at + local])
            )
        grad_first = lax.dot_general(
            x[:, rec].reshape(length, model),
            gh_s[...],
            (((0,), (0,)), ((), ())),
            preferred_element_type=F32,
        ).reshape(gf_s.shape)
        if rec == 0:
            gf_s[...] = grad_first
        else:
            both_s[...] = (gf_s[...] + grad_first).astype(BF)
    wait(*get_wq)
    going.append(copies.start(wq_s, wq))
    gk = jnp.sum(gk_s[...], 1)
    half = gko_s.shape[0]
    gko_s[:, :width] = gk[:half]
    gko_s[:, width:] = gk[half:]
    wait(
        copies.start(both_s.at[:, :, 1 - core], send),
        copies.start(gko_s, gk_out),
        copies.start(both_s.at[:, :, core], keep),
        *going,
    )


def pair_body(keep, recv, gk, gkr, *refs):
    zs = len(refs) - 5
    outs, (keep_s, gk_s, both_s, out_s, sems) = refs[:zs], refs[zs:]
    depth, wide = keep_s.shape[2:]
    half = wide // 2
    copies = Copies(sems)
    wait(copies.start(keep, keep_s), copies.start(gk, gk_s))
    both_s[...] = (keep_s[...].astype(F32) + recv[...].astype(F32)).astype(BF)
    gk_sum = (gk_s[...] + gkr[...]).astype(BF)
    tall = out_s.shape[2] // 2
    z = lax.axis_index("z")
    going = []
    for s in range(zs):
        for side in range(2):
            part = both_s[side, z ^ s]
            for h in range(2):
                at = h * tall
                out_s[s, side, at : at + depth] = part[:, h * half : (h + 1) * half]
                out_s[s, side, at + depth : at + tall] = gk_sum[:, h * half : (h + 1) * half]
        going.append(copies.start(out_s.at[s], outs[s]))
    wait(*going)


def sum_body(*refs):
    keep, send, parts_s, total_s, sems = refs[-5:]
    copies = Copies(sems)
    wait(*[copies.start(ref, parts_s.at[i]) for i, ref in enumerate(refs[:-5])])
    total_s[...] = jnp.sum(parts_s[...].astype(F32), 0).astype(BF)
    yh = lax.axis_index("yh")
    wait(copies.start(total_s.at[1 - yh], send), copies.start(total_s.at[yh], keep))


def spread_body(keep, recv, out, pair_s, sems):
    copies = Copies(sems)
    wait(copies.start(keep, pair_s.at[0]), copies.start(recv, pair_s.at[1]))
    wait(*[copies.start(pair_s, out.at[i]) for i in range(out.shape[0])])


def heads_body(head_dim, frames, x, wq, held, back, w, att_s, sems):
    del held
    copies = Copies(sems)
    get_w = [copies.start(wq, w)]
    blocks, records, local, model = x.shape
    length = blocks * local
    width = model // blocks
    rows = min(256, length)
    lane = lax.broadcasted_iota(jnp.int32, (rows, width), 1)
    scaling = head_dim**-0.5
    wait(*get_w)
    for rec in range(records):
        packed = dot(x[:, rec].reshape(length, model), w[...].reshape(model, 3 * width))
        packed = packed.astype(BF)
        q = packed[:, :width] * jnp.asarray(scaling, BF)
        k = packed[:, width : 2 * width]
        v = jnp.concatenate([packed[:, 2 * width :], jnp.ones((length, width), BF)], 1)
        bias = jnp.where(
            lax.broadcasted_iota(jnp.int32, (1, length), 1) < frames[rec], 0.0, -1e30
        )
        for r in range(0, length, rows):
            qr = q[r : r + rows]
            attended = jnp.zeros((rows, width), F32)
            for h in range(width // head_dim):
                here = (lane >= h * head_dim) & (lane < (h + 1) * head_dim)
                scores = dot_t(jnp.where(here, qr, jnp.zeros_like(qr)), k) + bias
                top = jnp.max(scores, -1, keepdims=True)
                both = dot(jnp.exp(scores - top).astype(BF), v)
                attended = jnp.where(here, both[:, :width] / both[:, width:], attended)
            got = attended.astype(BF).reshape(rows // local, local, width)
            att_s[r // local : (r + rows) // local, rec * local : (rec + 1) * local] = got
    tall = records * local
    wait(copies.start(att_s, back.at[:, 2 * tall : 3 * tall]))


def result_body(
    frames, a, mine, other, res, x, go, g1, out, gin,
    wp_s, w1_s, w2_s, res_s, x_s, go_s, g1_s, out_s, gin_s, sems,
):
    rows, model = x_s.shape
    blocks = a.shape[0]
    copies = Copies(sems)
    get_w = [
        lay_rows(copies, i * model, model, mine, other, one)
        for i, one in enumerate((wp_s, w1_s, w2_s))
    ]
    get_res = copies.start(res, res_s)
    get_x = copies.start(x, x_s)
    get_go = copies.start(go, go_s)
    get_g1 = copies.start(g1, g1_s)
    attended = jnp.concatenate([a[i, 2 * rows : 3 * rows] for i in range(blocks)], 1)
    linear = jnp.concatenate([a[i, :rows] for i in range(blocks)], 1)
    gating = jnp.concatenate([a[i, rows : 2 * rows] for i in range(blocks)], 1)
    wait(*get_w[0])
    projected = dot(attended, wp_s[...].reshape(model, model))
    records = frames.shape[0]
    local = rows // records
    at = lax.broadcasted_iota(jnp.int32, (local, model), 0) + ctx_index() * local
    present = jnp.concatenate([(at < frames[r]).astype(F32) for r in range(records)], 0)
    wait(get_res)
    out_s[...] = (res_s[...].astype(F32) + present * projected).astype(BF)
    put_out = copies.start(out_s, out)
    wait(*get_w[1])
    back_one = dot_t(linear, w1_s[...].reshape(model, model))
    wait(*get_w[2])
    back_one = back_one + dot_t(gating, w2_s[...].reshape(model, model))
    wait(get_x, get_go, get_g1)
    centre, inv = centred(x_s[...].astype(F32))
    pulled = norm_pull(back_one * g1_s[...], centre, inv)
    gin_s[...] = (go_s[...].astype(F32) + pulled).astype(BF)
    wait(put_out, copies.start(gin_s, gin))


def lay_body(a, gf, gk, gf_s, gk_s, sems):
    blocks = a.shape[0]
    depth, taps = gf_s.shape[0], gk_s.shape[0]
    model = gk_s.shape[1]
    width = model // blocks
    tall = a.shape[2] // 2
    half = tall - depth
    for i in range(blocks):
        lo = i * width
        total = a[i, 0].astype(F32) + a[(i + blocks // 2) % blocks, 1].astype(F32)
        for h in range(2):
            at = h * tall
            gf_s[:, h * model + lo : h * model + lo + width] = total[at : at + depth]
            count = min(half, taps - h * half)
            gk_s[h * half : h * half + count, lo : lo + width] = total[
                at + depth : at + depth + count
            ]
    copies = Copies(sems)
    wait(copies.start(gf_s, gf), copies.start(gk_s, gk))


def swap_core(v):
    return lax.ppermute(v, "core", [(0, 1), (1, 0)])


def swap_yh(v):
    return lax.ppermute(v, ("yh", "yl"), [(0, 3), (3, 0), (1, 2), (2, 1)])


def pair_z(v, by):
    return lax.ppermute(v, "z", [(i, i ^ by) for i in range(lax.axis_size("z"))])


def local(
    inputs,
    frames,
    gain_first,
    w_first,
    depth_kernel,
    gain_second,
    w_second,
    gain_attn,
    w_qkv,
    w_proj,
    grad_out,
):
    records, local_len, model = inputs.shape
    taps = depth_kernel.shape[0]
    blocks = lax.axis_size(CTX)
    zs = lax.axis_size("z")
    depth = w_first.shape[0]
    width = model // blocks
    length = blocks * local_len
    rows = records * local_len
    head_dim = model // HEADS
    barrier = lax.optimization_barrier
    x = inputs.reshape(rows, model)
    cot = grad_out.reshape(rows, model)
    gains = [g.reshape(1, model) for g in (gain_first, gain_second, gain_attn)]

    part = model + 3 * width
    own, w1_own, beside = run(
        functools.partial(cut_body, blocks),
        [
            ((depth, part), BF, HBM),
            ((depth, 2 * width), BF, HBM),
            ((depth, part + 2 * width), BF, HBM),
        ],
        [(w_second, HBM), (w_qkv, HBM), (w_first, HBM)],
        "cut",
        [((depth, part), BF), ((depth, 2 * width), BF), ((depth, part + 2 * width), BF)],
        15,
    )
    beside = swap_yh(beside)
    (sent,) = run(
        first_body,
        [((blocks, rows, model), BF, HBM)],
        [(x, HBM), (gains[0], HBM)],
        "first_norm",
        [((rows, model), BF), ((1, model), F32), ((rows, model), BF)],
        blocks + 2,
    )
    beside, _ = barrier((beside, sent))
    shard_a = jnp.stack([own, beside[:, :part]])
    all_a = lax.all_gather(shard_a, "z", axis=0, tiled=False)
    normed = lax.all_to_all(sent, CTX, 0, 0, tiled=True).reshape(blocks, records, local_len, model)

    w1_part = jnp.stack([w1_own, beside[:, part:]])
    two = jnp.stack([w1_part, pair_z(w1_part, 1)])
    w1_mine = jnp.concatenate([two] + [pair_z(two, s) for s in range(2, zs, 2)])
    w1_other = swap_core(w1_mine)

    (own_b,) = run(
        pack_body,
        [((depth, 3 * model), BF, HBM)],
        [(w_proj, HBM), (w_first, HBM)],
        "pack",
        [((depth, 3 * model), BF)],
        3,
    )
    shard_b = jnp.stack([own_b, swap_yh(own_b)])
    conv, hidden, gated = run(
        functools.partial(gate_body, taps),
        [
            ((blocks, records, local_len, width), BF, HBM),
            ((records, length, 2 * width), F32, HBM),
            ((records, length, width), BF, HBM),
        ],
        [(frames, SMEM), (normed, VMEM), (w1_mine, VMEM), (w1_other, VMEM), (depth_kernel, HBM)],
        "gate_conv",
        [
            ((2, zs, 2, depth, 2 * width), BF),
            ((taps, width), F32),
            ((length + 32, width), F32),
            ((blocks, records, local_len, width), BF),
            ((records, length, 2 * width), F32),
            ((records, length, width), BF),
        ],
        1 + 3 * records,
    )

    conv_rows = lax.all_to_all(conv, CTX, 0, 0, tiled=True).reshape(blocks, rows, width)
    all_a, conv_rows = barrier((all_a, conv_rows))
    other_a = swap_core(all_a)
    shard_b, all_a = barrier((shard_b, all_a))
    all_b = lax.all_gather(shard_b, "z", axis=0, tiled=False)

    w2_shape = (2, zs, 2, depth, model)
    grad_conv, swished = run(
        pull_body,
        [((blocks, rows, width), BF, HBM), ((rows, model), BF, HBM)],
        [(conv_rows, HBM), (all_a, HBM), (other_a, ANY), (cot, HBM), (gains[1], HBM)],
        "token_pull",
        [
            ((blocks, rows, width), BF),
            (w2_shape, BF),
            ((rows, model), BF),
            ((1, model), F32),
            ((blocks, rows, width), BF),
            ((rows, model), BF),
        ],
        9,
    )
    sent, residual = run(
        residual_body,
        [((blocks, rows, model), BF, HBM), ((rows, model), BF, HBM)],
        [(swished, HBM), (all_a, HBM), (other_a, ANY), (x, HBM), (gains[2], HBM)],
        "token_residual",
        [
            ((rows, model), BF),
            (w2_shape, BF),
            ((rows, model), BF),
            ((1, model), F32),
            ((rows, model), BF),
            ((rows, model), BF),
        ],
        blocks + 8,
    )
    grad_conv = lax.all_to_all(grad_conv, CTX, 0, 0, tiled=True)
    sent, grad_conv = barrier((sent, grad_conv))
    grad_conv = grad_conv.reshape(blocks, records, local_len, width)
    attn_in = lax.all_to_all(sent, CTX, 0, 0, tiled=True)
    attn_in = attn_in.reshape(blocks, records, local_len, model)

    tall = depth + 16
    half_share = (2, zs, depth, 2 * width)
    back, keep, send, gk, wq_rows = run(
        functools.partial(back_body, taps),
        [
            ((blocks, 3 * rows, width), BF, HBM),
            (half_share, BF, HBM),
            (half_share, BF, HBM),
            ((16, 2 * width), F32, HBM),
            ((2, zs, 2, depth, 3 * width), BF, HBM),
        ],
        [
            (frames, SMEM), (grad_conv, HBM), (normed, VMEM), (hidden, HBM), (gated, HBM),
            (depth_kernel, HBM), (all_a, HBM), (other_a, ANY),
        ],
        "conv_back",
        [
            ((blocks, records, local_len, width), BF),
            ((taps, width), F32),
            ((records, length, 2 * width), F32),
            ((records, length, width), BF),
            ((length + 32, width), F32),
            ((length + 32, width), F32),
            ((length, 2 * width), BF),
            ((2, zs, 2, depth, 2 * width), BF),
            ((2, zs, 2, depth, 2 * width), F32),
            ((32, 8, width), F32),
            ((blocks, 2 * rows, width), BF),
            ((16, 2 * width), F32),
            ((2, zs, 2, depth, 3 * width), BF),
        ],
        12 + 2 * records,
    )

    chunk = (2, 2 * tall, width)
    chunks = run(
        pair_body,
        [(chunk, BF, HBM)] * zs,
        [(keep, HBM), (swap_core(send), VMEM), (gk, HBM), (swap_core(gk), VMEM)],
        "pair_sum",
        [
            (half_share, BF),
            ((16, 2 * width), F32),
            (half_share, BF),
            ((zs,) + chunk, BF),
        ],
        zs + 2,
    )
    sums = [chunks[0]] + [pair_z(chunks[s], s) for s in range(1, zs)]
    attn_in, *sums[1:3] = barrier((attn_in, *sums[1:3]))
    (back,) = run(
        functools.partial(heads_body, head_dim),
        [(back.shape, BF, HBM)],
        [(frames, SMEM), (attn_in, VMEM), (wq_rows, HBM), (back, HBM)],
        "heads",
        [((2, zs, 2, depth, 3 * width), BF), ((blocks, rows, width), BF)],
        2,
        {3: 0},
    )
    keep, send = run(
        sum_body,
        [(chunk[1:], BF, HBM)] * 2,
        [(one, ANY) for one in sums[:3]] + [(one, VMEM) for one in sums[3:]],
        "share_sum",
        [((zs,) + chunk, BF), (chunk, BF)],
        zs + 2,
    )
    all_b, back, keep, send = barrier((all_b, back, keep, send))
    (pair,) = run(
        spread_body,
        [((blocks,) + chunk, BF, HBM)],
        [(keep, HBM), (swap_yh(send), ANY)],
        "spread",
        [(chunk, BF)],
        blocks + 2,
    )

    back = lax.all_to_all(back, CTX, 0, 0, tiled=True)
    pair, back, all_b = barrier((pair, back, all_b))
    other_b = swap_core(all_b)
    pair = lax.all_to_all(pair, CTX, 0, 0, tiled=True)
    result, grad_in = run(
        result_body,
        [((rows, model), BF, HBM)] * 2,
        [
            (frames, SMEM), (back, VMEM), (all_b, HBM), (other_b, ANY), (residual, HBM), (x, HBM),
            (cot, HBM), (gains[0], HBM),
        ],
        "result_rows",
        [((2, zs, 2, depth, model), BF)] * 3
        + [((rows, model), BF)] * 3
        + [((1, model), F32)]
        + [((rows, model), BF)] * 2,
        18,
    )
    pair, result, grad_in = barrier((pair, result, grad_in))
    grad_first, grad_kernel = run(
        lay_body,
        [((depth, 2 * model), F32, HBM), ((taps, model), F32, HBM)],
        [(pair, VMEM)],
        "lay_out",
        [((depth, 2 * model), F32), ((taps, model), F32)],
        2,
    )
    return (
        result.reshape(records, local_len, model),
        grad_in.reshape(records, local_len, model),
        grad_first,
        grad_kernel,
    )


def solution(mesh):
    dp, ctx = mesh.devices.shape
    split = Mesh(
        mesh.devices.reshape(2, dp // 4, 2, 2, ctx // 2), ("yh", "z", "core", "yl", "x")
    )
    tokens = P(DP, CTX, None)
    placed = (
        tokens,
        P(DP),
        P(),
        P(DP, None),
        P(),
        P(),
        P(DP, None),
        P(),
        P(DP, None),
        P(DP, None),
        tokens,
    )
    return jax.shard_map(
        local,
        mesh=split,
        in_specs=placed,
        out_specs=(tokens, tokens, P(DP, None), P()),
        check_vma=False,
    )
```
